32 devices in a mesh: bin: 16 (over z, y, x), wave: 2 (over core).
Axes of the slice: x: 2, y: 2, z: 4, core: 2. Of those that a mesh axis runs over, the one named last changes fastest.
Arguments:
- sources: bfloat16 [16384, 256], P(('bin', 'wave')), may hold values from -6 to 6
- density: bfloat16 [16384], P(('bin', 'wave')), may hold values from 0.5 to 1.5
- temp_bins: int32 [16384, 1], P(('bin', 'wave')), may hold values from 0 to 15; in each aligned block of 512 rows (0 to 511, 512 to 1023, ...) at most 64 rows name the same one
- ray_index: int32 [16384], P(('bin', 'wave')), may hold values from 0 to 255
- rate_tables: bfloat16 [16, 256, 256], P('bin'), as said below
- line_table: bfloat16 [256, 8192], P(None, 'wave'), may hold values from -0.046875 to 0.046875
Outputs:
- intensity: float32 [256, 8192], P('bin', 'wave')
The draws below stay inside these ranges and needn't reach their ends.
Inputs may be any that keep to these rules, and one draw needn't show every extreme that they name: `temp_bins`: among the 512 cells of one device (aligned blocks of 512 rows) no bin is named more than 64 times; some bin is named exactly 64 times. `rate_tables`: each bin's matrix has a diagonal between 0.25 and 0.55 and independent off-diagonal entries.
All inputs are finite; a program needn't handle non-finite values.
Results may differ from the reference program's by a relative error of at most 0.005.
Values may be sent and summed in bfloat16 or wider, within the bound.
No kernel may reach another device: no remote copies, remote signals or barrier semaphores. Data moves between devices by JAX's collectives and lax.ppermute only.
A program may use at most 64 MiB of HBM per device.

```python
import math
import jax
import jax.numpy as jnp
import numpy as np
from jax import lax

L = 256
W = 8192
C = 512
BINS = 16
CAP = 64
CELLS = 16384
RAYS = 256
N_BIN = 16
N_WAVE = 2


def draw_rate_tables(key, part):
    key_diag = jax.random.fold_in(key, 11)
    key_off = jax.random.fold_in(key, 23)
    diag_values = jax.random.uniform(key_diag, (BINS, L), jnp.float32, 0.3, 0.5)
    off_values = jax.random.normal(key_off, (BINS, L, L), jnp.float32) * (0.3 / jnp.sqrt(1.0 * L))
    eye_mask = (jnp.arange(L)[:, None] == jnp.arange(L)[None, :]).astype(jnp.float32)
    tables = off_values * (1.0 - eye_mask)[None, :, :] + eye_mask[None, :, :] * diag_values[:, None, :]
    return tables.astype(jnp.bfloat16)


def set_ends(result, stream_key, smallest, largest):
    longest = result.shape.index(max(result.shape))
    spots = []
    for shift in (0, 1):
        where = [jax.random.randint(jax.random.fold_in(stream_key, axis), (), 0, length) for axis, length in enumerate(result.shape)]
        where[longest] = (where[longest] + shift) % result.shape[longest]
        spots.append(tuple(where))
    return result.at[spots[0]].set(smallest).at[spots[1]].set(largest)


def levels(stream_key, extent, cuts, smallest, top_value):
    def one(axis_at, parts):
        heights = jax.random.uniform(jax.random.fold_in(jax.random.fold_in(stream_key, 6), axis_at), (parts,), jnp.float32, smallest / len(cuts), top_value / len(cuts))
        return jnp.repeat(jnp.exp(heights), extent[axis_at] // parts).reshape((-1,) + (1,) * (len(extent) - axis_at - 1))

    level = one(*cuts[0])
    for cut in cuts[1:]:
        level = level * one(*cut)
    return level


def routed_block(stream_key, own, number, rows, number_of, top, bound, lean):
    sequence = jax.random.permutation(stream_key, number_of)
    packed, ordinary = shares(number_of, rows * top, bound, lean, True), shares(number_of, rows * top, bound, lean, False)
    places = jnp.arange(number_of)

    def named(lengths, offset_by):
        used = int((lengths > 0).sum())
        fixed = max(1, used // 4)
        shifted = fixed + (places - fixed + offset_by * (used - fixed)) % max(1, number_of - fixed)
        return jnp.zeros((number_of,), jnp.int32).at[sequence[jnp.where(places < fixed, places, shifted)]].set(jnp.asarray(lengths, jnp.int32))

    lengths = jnp.where(number % 4 == 0, named(packed, number // 4), named(ordinary, number - number // 4 - 1))
    mixed = jax.random.permutation(jax.random.fold_in(own, 3), number_of)
    giver, taker = mixed[0:number_of // 2 * 2:2], mixed[1:number_of // 2 * 2:2]
    room = jnp.minimum(lengths[giver] - 1, bound - lengths[taker]) // 2
    room = jnp.where((giver == sequence[0]) | (taker == sequence[0]) | (lengths[taker] == 0), 0, jnp.maximum(room, 0))
    shifted = jax.random.randint(jax.random.fold_in(own, 4), (number_of // 2,), 0, 1 << 20) % (room + 1)
    lengths = lengths.at[giver].add(-shifted).at[taker].add(shifted)
    labels = jnp.searchsorted(jnp.cumsum(lengths), jnp.arange(rows * top), side="right").astype(jnp.int32)
    table = labels.reshape(top, rows).T
    table = table[jax.random.permutation(jax.random.fold_in(own, 1), rows)]
    offset_by = jax.random.randint(jax.random.fold_in(own, 2), (rows, 1), 0, top)
    return jnp.take_along_axis(table, (jnp.arange(top)[None, :] + offset_by) % top, axis=1)


def shares(amount, total, most, slope, full):
    portions = [(1 << 20) // math.isqrt(standing ** slope) + 1 for standing in range(1, amount + 1)]
    largest = most if full else min(most, max(-(-total // amount), total * portions[0] // sum(portions)))
    least = 1 if total - largest >= amount - 1 else 0
    holding, rest = [largest] + [least] * (amount - 1), total - largest - least * (amount - 1)
    while rest > 0:
        free = [i for i in range(1, amount) if holding[i] < largest] or [i for i in range(1, amount) if holding[i] < most]
        mass, left = sum([portions[i] for i in free]), rest
        for i in free:
            addition = min(most - holding[i], max(1, left * portions[i] // mass), rest)
            holding[i] = holding[i] + addition
            rest = rest - addition
    return np.array(holding)


def noise(own_key, dims, scale, bound, cuts=(), held_as=jnp.bfloat16):
    values = jax.random.normal(own_key, dims, jnp.float32) * scale
    if len(cuts) > 0:
        values = levels(own_key, dims, cuts, -0.22, 0.18) * values
    return jnp.clip(values, min=-bound, max=bound).astype(held_as)


def setup_inputs(seed: int = 0) -> dict:
    key_of = jax.random.split(jax.random.key(seed), 7)
    sources = noise(key_of[0], (CELLS, L), 1.0, 6.0, ((0, 32),))
    density = jnp.clip(jnp.exp(math.log(1.5) - 1.0986123 * jax.random.uniform(key_of[1], (CELLS,), jnp.float32) ** levels(key_of[1], (CELLS,), ((0, 32),), -0.2, 0.2)), 0.5, 1.5).astype(jnp.bfloat16)
    temp_bins_keys = jax.random.split(jax.random.fold_in(key_of[2], 1), CELLS // C)
    temp_bins_turns = jax.random.permutation(jax.random.fold_in(key_of[2], 3), CELLS // C)
    temp_bins = jax.vmap(lambda own, number: routed_block(jax.random.fold_in(key_of[2], 2), own, number, C, BINS, 1, CAP, 2))(temp_bins_keys, temp_bins_turns).reshape((CELLS, 1))
    ray_index = set_ends(jax.random.randint(key_of[3], (CELLS,), 0, RAYS), jax.random.fold_in(key_of[3], 1), 0, RAYS - 1).astype(jnp.int32)
    rate_tables = draw_rate_tables(jax.random.fold_in(key_of[6], 71), 0)
    line_table = noise(key_of[5], (L, W), (L * CELLS // RAYS) ** -0.5, 0.046875, ((1, 2),))
    return {"sources": sources, "density": density, "temp_bins": temp_bins, "ray_index": ray_index, "rate_tables": rate_tables, "line_table": line_table}


def iterate_levels(src_rows, den_rows, table):
    den_col = den_rows[:, None].astype(jnp.float32)
    src_wide = src_rows.astype(jnp.float32)
    first = (den_col * jnp.dot(src_rows, table, preferred_element_type=jnp.float32) + src_wide).astype(jnp.bfloat16)
    second = (den_col * jnp.dot(first, table, preferred_element_type=jnp.float32) + src_wide).astype(jnp.bfloat16)
    return second


def reference(sources, density, temp_bins, ray_index, rate_tables, line_table):
    cell_count = sources.shape[0]
    level_count = sources.shape[1]
    bin_count = rate_tables.shape[0]
    room = N_BIN * N_WAVE * CAP
    bin_of = temp_bins[:, 0].astype(jnp.int32)
    order_cells = jnp.argsort(bin_of, stable=True).astype(jnp.int32)
    sorted_bins = bin_of[order_cells]
    counts = jax.ops.segment_sum(jnp.ones_like(sorted_bins), sorted_bins, num_segments=bin_count)
    starts = (jnp.cumsum(counts) - counts).astype(jnp.int32)
    position = jnp.arange(cell_count, dtype=jnp.int32) - starts[sorted_bins]
    slot_index = (sorted_bins * room + position).astype(jnp.int32)
    src_buffer = jnp.zeros((bin_count * room, level_count), sources.dtype).at[slot_index].set(sources[order_cells])
    den_buffer = jnp.zeros((bin_count * room,), density.dtype).at[slot_index].set(density[order_cells])

    def per_bin(inputs):
        src_rows, den_rows, table = inputs
        return iterate_levels(src_rows, den_rows, table)

    pops_buffer = lax.map(per_bin, (src_buffer.reshape(bin_count, room, level_count), den_buffer.reshape(bin_count, room), rate_tables))
    pops_buffer = pops_buffer.reshape(bin_count * room, level_count)
    populations = jnp.zeros_like(sources).at[order_cells].set(pops_buffer[slot_index])
    ray_sums = jax.ops.segment_sum(populations.astype(jnp.float32), ray_index, num_segments=RAYS)
    return jnp.dot(ray_sums, line_table.astype(jnp.float32), precision=lax.Precision.HIGHEST, preferred_element_type=jnp.float32)
```

```python
import functools

import jax
import jax.numpy as jnp
from jax import lax
from jax.experimental import pallas as pl
from jax.experimental.pallas import tpu as pltpu
from jax.sharding import PartitionSpec as P

META_ROWS = 16
RAY_BASE = 32
VMEM_LIMIT = 32 * 1024 * 1024
F32 = jnp.float32
BF16 = jnp.bfloat16


def nt_dot(a, b):
    return lax.dot_general(a, b, (((1,), (1,)), ((), ())), preferred_element_type=F32)


def pack_kernel(bin_total, capacity, half_ref, src_ref, den_ref, bin_ref, ray_ref, out_ref):
    cells, levels = src_ref.shape
    half = bin_total // 2
    block = 2 * capacity
    bins = bin_ref[...]
    hot = (lax.broadcasted_iota(jnp.int32, (bin_total, cells), 0) == bins).astype(F32)
    earlier = (
        lax.broadcasted_iota(jnp.int32, (cells, cells), 0)
        < lax.broadcasted_iota(jnp.int32, (cells, cells), 1)
    ).astype(F32).astype(BF16)
    before = jnp.dot(hot.astype(BF16), earlier, preferred_element_type=F32)
    position = jnp.sum(hot * before, axis=0, keepdims=True).astype(jnp.int32)
    upper = (bins >= half).astype(jnp.int32)
    other = jnp.where(upper == half_ref[0], 0, 1)
    slot = (bins - upper * half) * block + other * capacity + position
    rays = ray_ref[...]
    ray_high = rays // RAY_BASE
    ray_low = rays - ray_high * RAY_BASE
    meta = jnp.concatenate(
        [
            den_ref[...].astype(F32),
            ray_high.astype(F32),
            ray_low.astype(F32),
            jnp.zeros((META_ROWS - 3, cells), F32),
        ],
        axis=0,
    ).astype(BF16)
    place = (
        lax.broadcasted_iota(jnp.int32, (half * block, cells), 0) == slot
    ).astype(F32).astype(BF16)
    rows = jnp.dot(place, src_ref[...], preferred_element_type=F32).astype(BF16)
    moved = nt_dot(meta, place).astype(BF16)
    out_ref[:, :block, :] = rows.reshape(half, block, levels)
    out_ref[:, block:, :] = jnp.zeros((half, META_ROWS, levels), BF16)
    for target in range(half):
        out_ref[target, block:, :block] = moved[:, target * block : (target + 1) * block]


def level_kernel(capacity, rays, got_ref, own_ref, other_ref, out_ref):
    sources, _, levels = got_ref.shape
    block = 2 * capacity
    total = jnp.zeros((rays, levels), F32)
    meta = [got_ref[s, block:, :block].astype(F32) for s in range(sources)]
    columns = [jnp.transpose(m[:8]) for m in meta]
    for part, table_ref in ((0, own_ref), (1, other_ref)):
        low, high = part * capacity, (part + 1) * capacity
        src = got_ref[:, low:high, :].reshape(sources * capacity, levels)
        den = jnp.concatenate([c[low:high, 0:1] for c in columns], axis=0)
        ray = jnp.concatenate(
            [m[1:2, low:high] * RAY_BASE + m[2:3, low:high] for m in meta], axis=1
        ).astype(jnp.int32)
        wide = src.astype(F32)
        table = table_ref[...]
        first = (den * jnp.dot(src, table, preferred_element_type=F32) + wide).astype(BF16)
        pops = (den * jnp.dot(first, table, preferred_element_type=F32) + wide).astype(BF16)
        pick = (
            lax.broadcasted_iota(jnp.int32, (rays, sources * capacity), 0) == ray
        ).astype(F32).astype(BF16)
        total = total + jnp.dot(pick, pops, preferred_element_type=F32)
    out_ref[...] = total.astype(BF16)


def line_kernel(mine_ref, theirs_ref, line_ref, out_ref):
    sums = mine_ref[...] + theirs_ref[...]
    rows = sums.shape[0]
    high = sums.astype(BF16)
    low = (sums - high.astype(F32)).astype(BF16)
    both = jnp.concatenate([high, low], axis=0)
    got = jnp.dot(both, line_ref[...], preferred_element_type=F32)
    out_ref[...] = got[:rows] + got[rows:]


def whole(shape):
    return pl.BlockSpec(memory_space=pltpu.VMEM)


def per_device(ray_total, sources, density, temp_bins, ray_index, rate_tables, line_table):
    cells, levels = sources.shape
    bin_total = lax.axis_size("bin")
    wave_total = lax.axis_size("wave")
    half = bin_total // 2
    capacity = max(2, 2 * cells // bin_total)
    block = 2 * capacity
    params = pltpu.CompilerParams(vmem_limit_bytes=VMEM_LIMIT)
    vmem = pl.BlockSpec(memory_space=pltpu.VMEM)
    smem = pl.BlockSpec(memory_space=pltpu.SMEM)

    own = rate_tables[0]
    other = lax.ppermute(own, "bin", [(i, (i + half) % bin_total) for i in range(bin_total)])

    my_half = (lax.axis_index("bin") // half).astype(jnp.int32).reshape(1)
    outgoing = pl.pallas_call(
        functools.partial(pack_kernel, bin_total, capacity),
        out_shape=jax.ShapeDtypeStruct((half, block + META_ROWS, levels), BF16),
        in_specs=[smem, vmem, vmem, vmem, vmem],
        out_specs=vmem,
        compiler_params=params,
    )(
        my_half,
        sources,
        density.reshape(1, cells),
        temp_bins.reshape(1, cells),
        ray_index.reshape(1, cells),
    )
    groups = [list(range(half)), list(range(half, bin_total))]
    got = lax.all_to_all(
        outgoing, "bin", split_axis=0, concat_axis=0, tiled=True, axis_index_groups=groups
    )
    partial_sums = pl.pallas_call(
        functools.partial(level_kernel, capacity, ray_total),
        out_shape=jax.ShapeDtypeStruct((ray_total, levels), BF16),
        in_specs=[vmem, vmem, vmem],
        out_specs=vmem,
        compiler_params=params,
    )(got, own, other)
    ray_rows = ray_total // bin_total
    held = lax.all_to_all(
        partial_sums.reshape(bin_total, ray_rows, levels), "bin", split_axis=0, concat_axis=0, tiled=True
    )
    sums = jnp.sum(held.astype(F32), axis=0)
    step = 1
    theirs = jnp.zeros_like(sums)
    while step < wave_total:
        sums = sums + theirs
        theirs = lax.ppermute(sums, "wave", [(i, i ^ step) for i in range(wave_total)])
        step *= 2
    return pl.pallas_call(
        line_kernel,
        out_shape=jax.ShapeDtypeStruct((ray_rows, line_table.shape[1]), F32),
        in_specs=[vmem, vmem, vmem],
        out_specs=vmem,
        compiler_params=params,
    )(sums, theirs, line_table)


def solution(mesh):
    in_specs = (
        P(("bin", "wave"), None),
        P(("bin", "wave")),
        P(("bin", "wave"), None),
        P(("bin", "wave")),
        P("bin", None, None),
        P(None, "wave"),
    )
    ray_total = RAY_DEV * mesh.shape["bin"]
    return jax.shard_map(
        functools.partial(per_device, ray_total),
        mesh=mesh,
        in_specs=in_specs,
        out_specs=P("bin", "wave"),
        check_vma=False,
    )


RAY_DEV = 16
```

```python
import functools

import jax
import jax.numpy as jnp
from jax import lax
from jax.experimental import pallas as pl
from jax.experimental.pallas import tpu as pltpu
from jax.sharding import PartitionSpec as P

RAY_DEV = 16
META_ROWS = 16
RAY_BASE = 32
LANES = 128
VMEM_LIMIT = 32 * 1024 * 1024
PACK_VMEM = 60 * 1024 * 1024
F32 = jnp.float32
BF16 = jnp.bfloat16
I32 = jnp.int32


def nt_dot(a, b):
    return lax.dot_general(a, b, (((1,), (1,)), ((), ())), preferred_element_type=F32)


def iota(shape, dim):
    return lax.broadcasted_iota(I32, shape, dim)


def pack_kernel(bin_total, capacity, me_ref, src_hbm, den_hbm, bin_hbm, ray_hbm, *rest):
    half = bin_total // 2
    outs = rest[:half]
    src_ref, den_ref, bin_ref, ray_ref, held, in_sems, out_sems = rest[half:]
    copies = [
        pltpu.make_async_copy(a, b, in_sems.at[i])
        for i, (a, b) in enumerate(
            ((bin_hbm, bin_ref), (ray_hbm, ray_ref), (den_hbm, den_ref), (src_hbm, src_ref))
        )
    ]
    for copy in copies:
        copy.start()
    cells, levels = src_ref.shape
    block = 2 * capacity
    earlier = (iota((cells, cells), 0) < iota((cells, cells), 1)).astype(F32).astype(BF16)
    me = me_ref[0]
    held[:, block:, :] = jnp.zeros((half, META_ROWS, levels), BF16)
    for copy in copies[:3]:
        copy.wait()
    bins = bin_ref[...]
    hot = (iota((bin_total, cells), 0) == bins).astype(F32)
    before = jnp.dot(hot.astype(BF16), earlier, preferred_element_type=F32)
    position = jnp.sum(hot * before, axis=0, keepdims=True).astype(I32)
    relative = bins ^ me
    upper = (relative >= half).astype(I32)
    slot = (relative - upper * half) * block + upper * capacity + position
    rays = ray_ref[...]
    ray_high = rays // RAY_BASE
    ray_low = rays - ray_high * RAY_BASE
    den = den_ref[...].astype(F32)
    den_row = jnp.concatenate([den[i : i + 1] for i in range(den.shape[0])], axis=1)
    meta = jnp.concatenate(
        [den_row, ray_high.astype(F32), ray_low.astype(F32), jnp.zeros((META_ROWS - 3, cells), F32)],
        axis=0,
    ).astype(BF16)
    place = (iota((half * block, cells), 0) == slot).astype(F32).astype(BF16)
    moved = nt_dot(meta, place).astype(BF16)
    copies[3].wait()
    src = src_ref[...]
    leaving = [
        pltpu.make_async_copy(held.at[t], outs[t], out_sems.at[t]) for t in range(half)
    ]
    for target in list(range(1, half)) + [0]:
        low, high = target * block, (target + 1) * block
        rows = jnp.dot(place[low:high], src, preferred_element_type=F32)
        held[target, :block, :] = rows.astype(BF16)
        held[target, block:, :block] = moved[:, low:high]
        leaving[target].start()
    for copy in leaving:
        copy.wait()


def level_kernel(capacity, low_total, high_total, ray_rows, me_ref, *refs):
    got = refs[: -(low_total + 2)]
    own_ref, other_ref = refs[len(got) : len(got) + 2]
    outs = refs[len(got) + 2 :]
    block = 2 * capacity
    rays = low_total * high_total * ray_rows
    me = me_ref[0]
    meta = [g[block:, :block].astype(F32) for g in got]
    columns = [jnp.transpose(m[:8]) for m in meta]
    total = jnp.zeros((rays, own_ref.shape[1]), F32)
    for part, table_ref in ((0, own_ref), (1, other_ref)):
        low, high = part * capacity, (part + 1) * capacity
        src = jnp.concatenate([g[low:high, :] for g in got], axis=0)
        den = jnp.concatenate([c[low:high, 0:1] for c in columns], axis=0)
        ray = jnp.concatenate(
            [m[1:2, low:high] * RAY_BASE + m[2:3, low:high] for m in meta], axis=1
        ).astype(I32)
        owner = ray // ray_rows
        relative = owner ^ me
        row = (
            (relative % low_total) * (high_total * ray_rows)
            + (relative // low_total) * ray_rows
            + (ray - owner * ray_rows)
        )
        wide = src.astype(F32)
        table = table_ref[...]
        first = (den * jnp.dot(src, table, preferred_element_type=F32) + wide).astype(BF16)
        pops = (den * jnp.dot(first, table, preferred_element_type=F32) + wide).astype(BF16)
        pick = (iota((rays, src.shape[0]), 0) == row).astype(F32).astype(BF16)
        total = total + jnp.dot(pick, pops, preferred_element_type=F32)
    size = high_total * ray_rows
    for d in range(low_total):
        outs[d][...] = total[d * size : (d + 1) * size].astype(outs[d].dtype)


def line_kernel(mine_ref, theirs_ref, line_ref, out_ref):
    sums = mine_ref[...] + theirs_ref[...]
    rows = sums.shape[0]
    high = sums.astype(BF16)
    low = (sums - high.astype(F32)).astype(BF16)
    both = jnp.concatenate([high, low], axis=0)
    got = jnp.dot(both, line_ref[...], preferred_element_type=F32)
    out_ref[...] = got[:rows] + got[rows:]


def swap(value, axis, mask):
    total = lax.axis_size(axis)
    return lax.ppermute(value, axis, [(i, i ^ mask) for i in range(total)])


def per_device(sources, density, temp_bins, ray_index, rate_tables, line_table):
    cells, levels = sources.shape
    bin_total = lax.axis_size("bin")
    wave_total = lax.axis_size("wave")
    half = bin_total // 2
    capacity = max(2, 2 * cells // bin_total)
    block = 2 * capacity
    low_total = 1 << (bin_total.bit_length() // 2)
    high_total = bin_total // low_total
    params = pltpu.CompilerParams(vmem_limit_bytes=VMEM_LIMIT)
    vmem = pl.BlockSpec(memory_space=pltpu.VMEM)
    smem = pl.BlockSpec(memory_space=pltpu.SMEM)
    hbm = pl.BlockSpec(memory_space=pl.ANY)

    other = swap(rate_tables[0], "bin", half)
    me = lax.axis_index("bin").astype(I32).reshape(1)
    den_rows = cells // min(cells, LANES)
    outgoing = pl.pallas_call(
        functools.partial(pack_kernel, bin_total, capacity),
        out_shape=[jax.ShapeDtypeStruct((block + META_ROWS, levels), BF16)] * half,
        in_specs=[smem] + [hbm] * 4,
        out_specs=[hbm] * half,
        scratch_shapes=[
            pltpu.VMEM((cells, levels), BF16),
            pltpu.VMEM((den_rows, cells // den_rows), BF16),
            pltpu.VMEM((1, cells), I32),
            pltpu.VMEM((1, cells), I32),
            pltpu.VMEM((half, block + META_ROWS, levels), BF16),
            pltpu.SemaphoreType.DMA((4,)),
            pltpu.SemaphoreType.DMA((half,)),
        ],
        compiler_params=pltpu.CompilerParams(vmem_limit_bytes=PACK_VMEM),
    )(
        me,
        sources,
        density.reshape(den_rows, cells // den_rows),
        temp_bins.reshape(1, cells),
        ray_index.reshape(1, cells),
    )
    got = [outgoing[0]] + [swap(outgoing[d], "bin", d) for d in range(1, half)]
    ray_rows = RAY_DEV
    size = high_total * ray_rows
    partial_sums = pl.pallas_call(
        functools.partial(level_kernel, capacity, low_total, high_total, ray_rows),
        out_shape=[
            jax.ShapeDtypeStruct((size, levels), F32 if d == 0 else BF16) for d in range(low_total)
        ],
        in_specs=[smem] + [vmem] * (half + 2),
        out_specs=[vmem] * low_total,
        compiler_params=params,
    )(me, *got, rate_tables[0], other)
    sums = partial_sums[0]
    for d in range(1, low_total):
        sums = sums + swap(partial_sums[d], "bin", d).astype(F32)
    total = sums[:ray_rows]
    for h in range(1, high_total):
        leaving = sums[h * ray_rows : (h + 1) * ray_rows].astype(BF16)
        total = total + swap(leaving, "bin", h * low_total).astype(F32)
    step = 1
    theirs = jnp.zeros_like(total)
    while step < wave_total:
        total = total + theirs if step > 1 else total
        theirs = swap(total, "wave", step)
        step *= 2
    return pl.pallas_call(
        line_kernel,
        out_shape=jax.ShapeDtypeStruct((ray_rows, line_table.shape[1]), F32),
        in_specs=[vmem, vmem, vmem],
        out_specs=vmem,
        compiler_params=params,
    )(total, theirs, line_table)


def solution(mesh):
    in_specs = (
        P(("bin", "wave"), None),
        P(("bin", "wave")),
        P(("bin", "wave"), None),
        P(("bin", "wave")),
        P("bin", None, None),
        P(None, "wave"),
    )
    return jax.shard_map(
        per_device, mesh=mesh, in_specs=in_specs, out_specs=P("bin", "wave"), check_vma=False
    )
```

```python
import functools

import jax
import jax.numpy as jnp
from jax import lax
from jax.experimental import pallas as pl
from jax.experimental.pallas import tpu as pltpu
from jax.sharding import PartitionSpec as P

RAY_DEV = 16
META_ROWS = 16
RAY_BASE = 32
LANES = 128
VMEM_LIMIT = 32 * 1024 * 1024
F32 = jnp.float32
BF16 = jnp.bfloat16
I32 = jnp.int32


def nt_dot(a, b):
    return lax.dot_general(a, b, (((1,), (1,)), ((), ())), preferred_element_type=F32)


def iota(shape, dim):
    return lax.broadcasted_iota(I32, shape, dim)


def pack_kernel(plan, me_ref, src_hbm, den_hbm, bin_hbm, ray_hbm, out_hbm, *scratch):
    src_ref, den_ref, bin_ref, ray_ref, held, in_sems, out_sems = scratch
    copies = [
        pltpu.make_async_copy(a, b, in_sems.at[i])
        for i, (a, b) in enumerate(
            ((bin_hbm, bin_ref), (ray_hbm, ray_ref), (den_hbm, den_ref), (src_hbm, src_ref))
        )
    ]
    for copy in copies:
        copy.start()
    cells, levels = src_ref.shape
    targets, block = plan.targets, plan.block
    earlier = (iota((cells, cells), 0) < iota((cells, cells), 1)).astype(F32).astype(BF16)
    held[:, block:, :] = jnp.zeros((targets, META_ROWS, levels), BF16)
    my_part = me_ref[0] // plan.wave
    for copy in copies[:3]:
        copy.wait()
    bins = bin_ref[...]
    hot = (iota((plan.low * plan.high, cells), 0) == bins).astype(F32)
    before = jnp.dot(hot.astype(BF16), earlier, preferred_element_type=F32)
    position = jnp.sum(hot * before, axis=0, keepdims=True).astype(I32)
    high = bins // plan.low
    target = (bins - high * plan.low) * plan.wave + high % plan.wave
    slot = target * block + ((high // plan.wave) ^ my_part) * plan.capacity + position
    rays = ray_ref[...]
    ray_high = rays // RAY_BASE
    ray_low = rays - ray_high * RAY_BASE
    den = den_ref[...].astype(F32)
    den_row = jnp.concatenate([den[i : i + 1] for i in range(den.shape[0])], axis=1)
    meta = jnp.concatenate(
        [den_row, ray_high.astype(F32), ray_low.astype(F32), jnp.zeros((META_ROWS - 3, cells), F32)],
        axis=0,
    ).astype(BF16)
    place = (iota((targets * block, cells), 0) == slot).astype(F32).astype(BF16)
    moved = nt_dot(meta, place).astype(BF16)
    copies[3].wait()
    src = src_ref[...]
    leaving = [
        pltpu.make_async_copy(held.at[t], out_hbm.at[t], out_sems.at[t]) for t in range(targets)
    ]
    for t in range(targets):
        first, last = t * block, (t + 1) * block
        rows = jnp.dot(place[first:last], src, preferred_element_type=F32)
        held[t, :block, :] = rows.astype(BF16)
        held[t, block:, :block] = moved[:, first:last]
        leaving[t].start()
    for copy in leaving:
        copy.wait()


def level_kernel(plan, rays, got_ref, *refs):
    table_refs, out_ref = refs[:-1], refs[-1]
    targets, block = plan.targets, plan.block
    meta = [got_ref[s, block:, :block].astype(F32) for s in range(targets)]
    columns = [jnp.transpose(m[:8]) for m in meta]
    total = jnp.zeros(out_ref.shape, F32)
    for part, table_ref in enumerate(table_refs):
        low, high = part * plan.capacity, (part + 1) * plan.capacity
        src = got_ref[:, low:high, :].reshape(targets * plan.capacity, got_ref.shape[2])
        den = jnp.concatenate([c[low:high, 0:1] for c in columns], axis=0)
        ray = jnp.concatenate(
            [m[1:2, low:high] * RAY_BASE + m[2:3, low:high] for m in meta], axis=1
        ).astype(I32)
        wide = src.astype(F32)
        table = table_ref[...]
        first = (den * jnp.dot(src, table, preferred_element_type=F32) + wide).astype(BF16)
        pops = (den * jnp.dot(first, table, preferred_element_type=F32) + wide).astype(BF16)
        pick = (iota((rays, src.shape[0]), 0) == ray).astype(F32).astype(BF16)
        total = total + jnp.dot(pick, pops, preferred_element_type=F32)
    out_ref[...] = total.astype(BF16)


def line_kernel(mine_ref, theirs_ref, line_ref, out_ref):
    sums = mine_ref[...] + theirs_ref[...]
    rows = sums.shape[0]
    high = sums.astype(BF16)
    low = (sums - high.astype(F32)).astype(BF16)
    both = jnp.concatenate([high, low], axis=0)
    got = jnp.dot(both, line_ref[...], preferred_element_type=F32)
    out_ref[...] = got[:rows] + got[rows:]


class Plan:
    def __init__(self, bin_total, wave_total, cells):
        self.wave = wave_total
        self.high = max(wave_total, 1 << (bin_total.bit_length() // 2))
        self.low = bin_total // self.high
        self.parts = self.high // wave_total
        self.targets = self.low * wave_total
        self.capacity = max(2, 2 * cells // bin_total)
        self.block = self.parts * self.capacity

    def device(self, high, low, wave):
        return (high * self.low + low) * self.wave + wave

    def table_moves(self, k):
        moves = []
        for high in range(self.high):
            for low in range(self.low):
                for core in range(self.wave):
                    to = self.wave * ((high // self.wave) ^ k) + core
                    moves.append(
                        (self.device(high, low, core), self.device(to, low, high % self.wave))
                    )
        return moves

    def planes(self):
        size = self.low * self.wave
        return [list(range(h * size, (h + 1) * size)) for h in range(self.high)]


def per_device(sources, density, temp_bins, ray_index, rate_tables, line_table):
    cells, levels = sources.shape
    bin_total = lax.axis_size("bin")
    wave_total = lax.axis_size("wave")
    plan = Plan(bin_total, wave_total, cells)
    rows = plan.block + META_ROWS
    params = pltpu.CompilerParams(vmem_limit_bytes=VMEM_LIMIT)
    vmem = pl.BlockSpec(memory_space=pltpu.VMEM)
    smem = pl.BlockSpec(memory_space=pltpu.SMEM)
    hbm = pl.BlockSpec(memory_space=pltpu.HBM)

    def in_hbm(x):
        return pltpu.with_memory_space_constraint(x, pltpu.HBM)

    tables = [
        lax.ppermute(rate_tables[0], ("bin", "wave"), plan.table_moves(k)) for k in range(plan.parts)
    ]
    me = (lax.axis_index("bin") // plan.low).astype(I32).reshape(1)
    den_rows = cells // min(cells, LANES)
    outgoing = pl.pallas_call(
        functools.partial(pack_kernel, plan),
        out_shape=jax.ShapeDtypeStruct((plan.targets, rows, levels), BF16),
        in_specs=[smem] + [hbm] * 4,
        out_specs=hbm,
        scratch_shapes=[
            pltpu.VMEM((cells, levels), BF16),
            pltpu.VMEM((den_rows, cells // den_rows), BF16),
            pltpu.VMEM((1, cells), I32),
            pltpu.VMEM((1, cells), I32),
            pltpu.VMEM((plan.targets, rows, levels), BF16),
            pltpu.SemaphoreType.DMA((4,)),
            pltpu.SemaphoreType.DMA((plan.targets,)),
        ],
        compiler_params=params,
    )(
        me,
        in_hbm(sources),
        in_hbm(density.reshape(den_rows, cells // den_rows)),
        in_hbm(temp_bins.reshape(1, cells)),
        in_hbm(ray_index.reshape(1, cells)),
    )
    got = lax.all_to_all(
        outgoing,
        ("bin", "wave"),
        split_axis=0,
        concat_axis=0,
        tiled=True,
        axis_index_groups=plan.planes(),
    )
    ray_rows = RAY_DEV
    rays = ray_rows * bin_total
    partial_sums = pl.pallas_call(
        functools.partial(level_kernel, plan, rays),
        out_shape=jax.ShapeDtypeStruct((rays, levels), BF16),
        in_specs=[vmem] * (1 + plan.parts),
        out_specs=vmem,
        compiler_params=params,
    )(got, *tables)
    held = lax.all_to_all(
        partial_sums.reshape(bin_total, ray_rows, levels),
        "bin",
        split_axis=0,
        concat_axis=0,
        tiled=True,
    )
    total = jnp.sum(held.astype(F32), axis=0)
    theirs = jnp.zeros_like(total)
    step = 1
    while step < wave_total:
        total = total + theirs if step > 1 else total
        theirs = lax.ppermute(total, "wave", [(i, i ^ step) for i in range(wave_total)])
        step *= 2
    return pl.pallas_call(
        line_kernel,
        out_shape=jax.ShapeDtypeStruct((ray_rows, line_table.shape[1]), F32),
        in_specs=[vmem, vmem, vmem],
        out_specs=vmem,
        compiler_params=params,
    )(total, theirs, line_table)


def solution(mesh):
    in_specs = (
        P(("bin", "wave"), None),
        P(("bin", "wave")),
        P(("bin", "wave"), None),
        P(("bin", "wave")),
        P("bin", None, None),
        P(None, "wave"),
    )
    return jax.shard_map(
        per_device, mesh=mesh, in_specs=in_specs, out_specs=P("bin", "wave"), check_vma=False
    )
```

```python
import functools

import jax
import jax.numpy as jnp
from jax import lax
from jax.experimental import pallas as pl
from jax.experimental.pallas import tpu as pltpu
from jax.sharding import PartitionSpec as P

RAY_DEV = 16
META_ROWS = 16
RAY_BASE = 32
LANES = 128
VMEM_LIMIT = 32 * 1024 * 1024
F32 = jnp.float32
BF16 = jnp.bfloat16
I32 = jnp.int32


def nt_dot(a, b):
    return lax.dot_general(a, b, (((1,), (1,)), ((), ())), preferred_element_type=F32)


def iota(shape, dim):
    return lax.broadcasted_iota(I32, shape, dim)


def pack_kernel(plan, me_ref, src_hbm, den_hbm, bin_hbm, ray_hbm, table_hbm, line_hbm, *rest):
    targets, block = plan.targets, plan.block
    outs, table_out, line_out = rest[:targets], rest[targets], rest[targets + 1]
    src_ref, den_ref, bin_ref, ray_ref, sems = rest[targets + 2 :]
    copies = [
        pltpu.make_async_copy(a, b, sems.at[i])
        for i, (a, b) in enumerate(
            (
                (bin_hbm, bin_ref),
                (ray_hbm, ray_ref),
                (den_hbm, den_ref),
                (src_hbm, src_ref),
                (table_hbm, table_out),
                (line_hbm, line_out),
            )
        )
    ]
    for copy in copies:
        copy.start()
    cells, levels = src_ref.shape
    earlier = (iota((cells, cells), 0) < iota((cells, cells), 1)).astype(F32).astype(BF16)
    my_high = me_ref[0] // targets
    my_place = me_ref[0] - my_high * targets
    for copy in copies[:3]:
        copy.wait()
    bins = bin_ref[...]
    hot = (iota((plan.low * plan.high, cells), 0) == bins).astype(F32)
    before = jnp.dot(hot.astype(BF16), earlier, preferred_element_type=F32)
    position = jnp.sum(hot * before, axis=0, keepdims=True).astype(I32)
    high = bins // plan.low
    turn = high ^ my_high
    core = turn // plan.parts
    target = ((bins - high * plan.low) * plan.wave + core) ^ my_place
    slot = target * block + (turn - core * plan.parts) * plan.capacity + position
    rays = ray_ref[...]
    ray_high = rays // RAY_BASE
    ray_low = rays - ray_high * RAY_BASE
    den = den_ref[...].astype(F32)
    den_row = jnp.concatenate([den[i : i + 1] for i in range(den.shape[0])], axis=1)
    meta = jnp.concatenate(
        [den_row, ray_high.astype(F32), ray_low.astype(F32), jnp.zeros((META_ROWS - 3, cells), F32)],
        axis=0,
    ).astype(BF16)
    place = (iota((targets * block, cells), 0) == slot).astype(F32).astype(BF16)
    moved = nt_dot(meta, place).astype(BF16)
    copies[3].wait()
    rows = jnp.dot(place, src_ref[...], preferred_element_type=F32).astype(BF16)
    for t in range(targets):
        first, last = t * block, (t + 1) * block
        outs[t][:block, :] = rows[first:last]
        outs[t][block:, :] = jnp.zeros((META_ROWS, levels), BF16)
        outs[t][block:, :block] = moved[:, first:last]
    for copy in copies[4:]:
        copy.wait()


def level_kernel(plan, rays, me_ref, own_ref, *refs):
    got, table_refs, out_ref = refs[: plan.targets], refs[plan.targets : -1], refs[-1]
    block = plan.block
    first_core = me_ref[0] % plan.wave == 0
    meta = [g[block:, :block].astype(F32) for g in got]
    columns = [jnp.transpose(m[:8]) for m in meta]
    total = jnp.zeros(out_ref.shape, F32)
    for part, table_ref in enumerate(table_refs):
        low, high = part * plan.capacity, (part + 1) * plan.capacity
        src = jnp.concatenate([g[low:high, :] for g in got], axis=0)
        den = jnp.concatenate([c[low:high, 0:1] for c in columns], axis=0)
        ray = jnp.concatenate(
            [m[1:2, low:high] * RAY_BASE + m[2:3, low:high] for m in meta], axis=1
        ).astype(I32)
        wide = src.astype(F32)
        table = table_ref[...]
        if part == 0:
            table = jnp.where(first_core, own_ref[...], table)
        first = (den * jnp.dot(src, table, preferred_element_type=F32) + wide).astype(BF16)
        pops = (den * jnp.dot(first, table, preferred_element_type=F32) + wide).astype(BF16)
        pick = (iota((rays, src.shape[0]), 0) == ray).astype(F32).astype(BF16)
        total = total + jnp.dot(pick, pops, preferred_element_type=F32)
    out_ref[...] = total.astype(BF16)


def line_kernel(mine_ref, theirs_ref, line_ref, out_ref):
    sums = mine_ref[...] + theirs_ref[...]
    rows = sums.shape[0]
    high = sums.astype(BF16)
    low = (sums - high.astype(F32)).astype(BF16)
    both = jnp.concatenate([high, low], axis=0)
    got = jnp.dot(both, line_ref[...], preferred_element_type=F32)
    out_ref[...] = got[:rows] + got[rows:]


class Plan:
    def __init__(self, bin_total, wave_total, cells):
        self.wave = wave_total
        self.high = max(wave_total, 1 << (bin_total.bit_length() // 2))
        self.low = bin_total // self.high
        self.parts = self.high // wave_total
        self.targets = self.low * wave_total
        self.capacity = max(2, 2 * cells // bin_total)
        self.block = self.parts * self.capacity

    def device(self, high, low, wave):
        return (high * self.low + low) * self.wave + wave

    def table_moves(self, k):
        moves = []
        for high in range(self.high):
            for low in range(self.low):
                for core in range(self.wave):
                    turn = core * self.parts + k
                    if turn:
                        moves.append(
                            (self.device(high, low, core), self.device(high ^ turn, low, core))
                        )
        return moves

    def plane_moves(self, k):
        return [(i, i ^ k) for i in range(self.high * self.targets)]


def per_device(sources, density, temp_bins, ray_index, rate_tables, line_table):
    cells, levels = sources.shape
    bin_total = lax.axis_size("bin")
    wave_total = lax.axis_size("wave")
    plan = Plan(bin_total, wave_total, cells)
    rows = plan.block + META_ROWS
    params = pltpu.CompilerParams(vmem_limit_bytes=VMEM_LIMIT)
    vmem = pl.BlockSpec(memory_space=pltpu.VMEM)
    smem = pl.BlockSpec(memory_space=pltpu.SMEM)
    hbm = pl.BlockSpec(memory_space=pltpu.HBM)
    both = ("bin", "wave")

    def in_hbm(x):
        return pltpu.with_memory_space_constraint(x, pltpu.HBM)

    tables = [
        lax.ppermute(rate_tables[0], both, plan.table_moves(k)) for k in reversed(range(plan.parts))
    ][::-1]
    me = lax.axis_index(both).astype(I32).reshape(1)
    den_rows = cells // min(cells, LANES)
    *outgoing, own, held_line = pl.pallas_call(
        functools.partial(pack_kernel, plan),
        out_shape=[jax.ShapeDtypeStruct((rows, levels), BF16)] * plan.targets
        + [jax.ShapeDtypeStruct(a, BF16) for a in (rate_tables.shape[1:], line_table.shape)],
        in_specs=[smem] + [hbm] * 6,
        out_specs=[vmem] * (plan.targets + 2),
        scratch_shapes=[
            pltpu.VMEM((cells, levels), BF16),
            pltpu.VMEM((den_rows, cells // den_rows), BF16),
            pltpu.VMEM((1, cells), I32),
            pltpu.VMEM((1, cells), I32),
            pltpu.SemaphoreType.DMA((6,)),
        ],
        compiler_params=params,
    )(
        me,
        in_hbm(sources),
        in_hbm(density.reshape(den_rows, cells // den_rows)),
        in_hbm(temp_bins.reshape(1, cells)),
        in_hbm(ray_index.reshape(1, cells)),
        in_hbm(rate_tables[0]),
        in_hbm(line_table),
    )
    got = [outgoing[0]] + [
        lax.ppermute(outgoing[k], both, plan.plane_moves(k)) for k in range(1, plan.targets)
    ]
    ray_rows = RAY_DEV
    rays = ray_rows * bin_total
    partial_sums = pl.pallas_call(
        functools.partial(level_kernel, plan, rays),
        out_shape=jax.ShapeDtypeStruct((rays, levels), BF16),
        in_specs=[smem] + [vmem] * (1 + plan.targets + plan.parts),
        out_specs=vmem,
        compiler_params=params,
    )(me, own, *got, *tables)
    held = lax.all_to_all(
        partial_sums.reshape(bin_total, ray_rows, levels),
        "bin",
        split_axis=0,
        concat_axis=0,
        tiled=True,
    )
    total = jnp.sum(held.astype(F32), axis=0)
    theirs = jnp.zeros_like(total)
    step = 1
    while step < wave_total:
        total = total + theirs if step > 1 else total
        theirs = lax.ppermute(total, "wave", [(i, i ^ step) for i in range(wave_total)])
        step *= 2
    return pl.pallas_call(
        line_kernel,
        out_shape=jax.ShapeDtypeStruct((ray_rows, line_table.shape[1]), F32),
        in_specs=[vmem, vmem, vmem],
        out_specs=vmem,
        compiler_params=params,
    )(total, theirs, held_line)


def solution(mesh):
    in_specs = (
        P(("bin", "wave"), None),
        P(("bin", "wave")),
        P(("bin", "wave"), None),
        P(("bin", "wave")),
        P("bin", None, None),
        P(None, "wave"),
    )
    return jax.shard_map(
        per_device, mesh=mesh, in_specs=in_specs, out_specs=P("bin", "wave"), check_vma=False
    )
```

```python
import functools

import jax
import jax.numpy as jnp
from jax import lax
from jax.experimental import pallas as pl
from jax.experimental.pallas import tpu as pltpu
from jax.sharding import PartitionSpec as P

RAY_DEV = 16
META_ROWS = 16
RAY_BASE = 32
LANES = 128
OVERLAP_FLOPS = 10**10
VMEM_LIMIT = 32 * 1024 * 1024
F32 = jnp.float32
BF16 = jnp.bfloat16
I32 = jnp.int32


def nt_dot(a, b):
    return lax.dot_general(a, b, (((1,), (1,)), ((), ())), preferred_element_type=F32)


def iota(shape, dim):
    return lax.broadcasted_iota(I32, shape, dim)


def pack_kernel(plan, me_ref, src_hbm, den_hbm, bin_hbm, ray_hbm, table_hbm, line_hbm, *rest):
    targets, block = plan.targets, plan.block
    outs, table_out, line_out = rest[:targets], rest[targets], rest[targets + 1]
    src_ref, den_ref, bin_ref, ray_ref, sems = rest[targets + 2 :]
    copies = [
        pltpu.make_async_copy(a, b, sems.at[i])
        for i, (a, b) in enumerate(
            (
                (bin_hbm, bin_ref),
                (ray_hbm, ray_ref),
                (den_hbm, den_ref),
                (src_hbm, src_ref),
                (table_hbm, table_out),
                (line_hbm, line_out),
            )
        )
    ]
    for copy in copies:
        copy.start()
    cells, levels = src_ref.shape
    earlier = (iota((cells, cells), 0) < iota((cells, cells), 1)).astype(F32).astype(BF16)
    my_high = me_ref[0] // targets
    my_place = me_ref[0] - my_high * targets
    for copy in copies[:3]:
        copy.wait()
    bins = bin_ref[...]
    hot = (iota((plan.low * plan.high, cells), 0) == bins).astype(F32)
    before = jnp.dot(hot.astype(BF16), earlier, preferred_element_type=F32)
    position = jnp.sum(hot * before, axis=0, keepdims=True).astype(I32)
    high = bins // plan.low
    turn = high ^ my_high
    core = turn // plan.parts
    target = ((bins - high * plan.low) * plan.wave + core) ^ my_place
    slot = target * block + (turn - core * plan.parts) * plan.capacity + position
    rays = ray_ref[...]
    ray_high = rays // RAY_BASE
    ray_low = rays - ray_high * RAY_BASE
    den = den_ref[...].astype(F32)
    den_row = jnp.concatenate([den[i : i + 1] for i in range(den.shape[0])], axis=1)
    meta = jnp.concatenate(
        [den_row, ray_high.astype(F32), ray_low.astype(F32), jnp.zeros((META_ROWS - 3, cells), F32)],
        axis=0,
    ).astype(BF16)
    place = (iota((targets * block, cells), 0) == slot).astype(F32).astype(BF16)
    moved = nt_dot(meta, place).astype(BF16)
    copies[3].wait()
    rows = jnp.dot(place, src_ref[...], preferred_element_type=F32).astype(BF16)
    for t in range(targets):
        first, last = t * block, (t + 1) * block
        outs[t][:block, :] = rows[first:last]
        outs[t][block:, :] = jnp.zeros((META_ROWS, levels), BF16)
        outs[t][block:, :block] = moved[:, first:last]
    for copy in copies[4:]:
        copy.wait()


def choose_kernel(plan, me_ref, own_ref, *refs):
    tables, outs = refs[: plan.parts], refs[plan.parts :]
    outs[0][...] = jnp.where(me_ref[0] % plan.wave == 0, own_ref[...], tables[0][...])
    for table, out in zip(tables[1:], outs[1:]):
        out[...] = table[...]


def level_kernel(plan, rays, *refs):
    got, table_refs, out_ref = refs[: plan.targets], refs[plan.targets : -1], refs[-1]
    block = plan.block
    meta = [g[block:, :block].astype(F32) for g in got]
    columns = [jnp.transpose(m[:8]) for m in meta]
    total = jnp.zeros(out_ref.shape, F32)
    for part, table_ref in enumerate(table_refs):
        low, high = part * plan.capacity, (part + 1) * plan.capacity
        src = jnp.concatenate([g[low:high, :] for g in got], axis=0)
        den = jnp.concatenate([c[low:high, 0:1] for c in columns], axis=0)
        ray = jnp.concatenate(
            [m[1:2, low:high] * RAY_BASE + m[2:3, low:high] for m in meta], axis=1
        ).astype(I32)
        wide = src.astype(F32)
        table = table_ref[...]
        first = (den * jnp.dot(src, table, preferred_element_type=F32) + wide).astype(BF16)
        pops = (den * jnp.dot(first, table, preferred_element_type=F32) + wide).astype(BF16)
        pick = (iota((rays, src.shape[0]), 0) == ray).astype(F32).astype(BF16)
        total = total + jnp.dot(pick, pops, preferred_element_type=F32)
    out_ref[...] = total.astype(BF16)


def line_kernel(mine_ref, theirs_ref, line_ref, out_ref):
    sums = mine_ref[...] + theirs_ref[...]
    rows = sums.shape[0]
    high = sums.astype(BF16)
    low = (sums - high.astype(F32)).astype(BF16)
    both = jnp.concatenate([high, low], axis=0)
    got = jnp.dot(both, line_ref[...], preferred_element_type=F32)
    out_ref[...] = got[:rows] + got[rows:]


class Plan:
    def __init__(self, bin_total, wave_total, cells):
        self.wave = wave_total
        self.high = max(wave_total, 1 << (bin_total.bit_length() // 2))
        self.low = bin_total // self.high
        self.parts = self.high // wave_total
        self.targets = self.low * wave_total
        self.capacity = max(2, 2 * cells // bin_total)
        self.block = self.parts * self.capacity

    def device(self, high, low, wave):
        return (high * self.low + low) * self.wave + wave

    def table_moves(self, k):
        moves = []
        for high in range(self.high):
            for low in range(self.low):
                for core in range(self.wave):
                    turn = core * self.parts + k
                    if turn:
                        moves.append(
                            (self.device(high, low, core), self.device(high ^ turn, low, core))
                        )
        return moves

    def order(self):
        across = range(self.wave, self.targets)
        return sorted(across, key=lambda k: (k % self.wave, k)) + list(range(1, self.wave))

    def plane_moves(self, k):
        return [(i, i ^ k) for i in range(self.high * self.targets)]


def per_device(sources, density, temp_bins, ray_index, rate_tables, line_table):
    cells, levels = sources.shape
    bin_total = lax.axis_size("bin")
    wave_total = lax.axis_size("wave")
    plan = Plan(bin_total, wave_total, cells)
    rows = plan.block + META_ROWS
    params = pltpu.CompilerParams(vmem_limit_bytes=VMEM_LIMIT)
    vmem = pl.BlockSpec(memory_space=pltpu.VMEM)
    smem = pl.BlockSpec(memory_space=pltpu.SMEM)
    hbm = pl.BlockSpec(memory_space=pltpu.HBM)
    both = ("bin", "wave")

    def in_hbm(x):
        return pltpu.with_memory_space_constraint(x, pltpu.HBM)

    tables = [
        lax.ppermute(rate_tables[0], both, plan.table_moves(k)) for k in reversed(range(plan.parts))
    ][::-1]
    me = lax.axis_index(both).astype(I32).reshape(1)
    den_rows = cells // min(cells, LANES)
    *outgoing, own, held_line = pl.pallas_call(
        functools.partial(pack_kernel, plan),
        out_shape=[jax.ShapeDtypeStruct((rows, levels), BF16)] * plan.targets
        + [jax.ShapeDtypeStruct(a, BF16) for a in (rate_tables.shape[1:], line_table.shape)],
        in_specs=[smem] + [hbm] * 6,
        out_specs=[vmem] * (plan.targets + 2),
        scratch_shapes=[
            pltpu.VMEM((cells, levels), BF16),
            pltpu.VMEM((den_rows, cells // den_rows), BF16),
            pltpu.VMEM((1, cells), I32),
            pltpu.VMEM((1, cells), I32),
            pltpu.SemaphoreType.DMA((6,)),
        ],
        compiler_params=params,
    )(
        me,
        in_hbm(sources),
        in_hbm(density.reshape(den_rows, cells // den_rows)),
        in_hbm(temp_bins.reshape(1, cells)),
        in_hbm(ray_index.reshape(1, cells)),
        in_hbm(rate_tables[0]),
        in_hbm(line_table),
    )
    got = list(outgoing)
    for k in plan.order():
        got[k] = lax.ppermute(outgoing[k], both, plan.plane_moves(k))
    tables = pl.pallas_call(
        functools.partial(choose_kernel, plan),
        out_shape=[jax.ShapeDtypeStruct(rate_tables.shape[1:], BF16)] * plan.parts,
        in_specs=[smem] + [vmem] * (1 + plan.parts),
        out_specs=[vmem] * plan.parts,
        compiler_params=params,
        cost_estimate=pl.CostEstimate(
            flops=OVERLAP_FLOPS, bytes_accessed=2 * own.size * 2 * plan.parts, transcendentals=0
        ),
    )(me, own, *tables)
    ray_rows = RAY_DEV
    rays = ray_rows * bin_total
    partial_sums = pl.pallas_call(
        functools.partial(level_kernel, plan, rays),
        out_shape=jax.ShapeDtypeStruct((rays, levels), BF16),
        in_specs=[vmem] * (plan.targets + plan.parts),
        out_specs=vmem,
        compiler_params=params,
    )(*got, *tables)
    held = lax.all_to_all(
        partial_sums.reshape(bin_total, ray_rows, levels),
        "bin",
        split_axis=0,
        concat_axis=0,
        tiled=True,
    )
    total = jnp.sum(held.astype(F32), axis=0)
    theirs = jnp.zeros_like(total)
    step = 1
    while step < wave_total:
        total = total + theirs if step > 1 else total
        theirs = lax.ppermute(total, "wave", [(i, i ^ step) for i in range(wave_total)])
        step *= 2
    return pl.pallas_call(
        line_kernel,
        out_shape=jax.ShapeDtypeStruct((ray_rows, line_table.shape[1]), F32),
        in_specs=[vmem, vmem, vmem],
        out_specs=vmem,
        compiler_params=params,
    )(total, theirs, held_line)


def solution(mesh):
    in_specs = (
        P(("bin", "wave"), None),
        P(("bin", "wave")),
        P(("bin", "wave"), None),
        P(("bin", "wave")),
        P("bin", None, None),
        P(None, "wave"),
    )
    return jax.shard_map(
        per_device, mesh=mesh, in_specs=in_specs, out_specs=P("bin", "wave"), check_vma=False
    )
```

```python
import functools

import jax
import jax.numpy as jnp
from jax import lax
from jax.experimental import pallas as pl
from jax.experimental.pallas import tpu as pltpu
from jax.sharding import PartitionSpec as P

RAY_DEV = 16
META_ROWS = 16
RAY_BASE = 32
LANES = 128
OVERLAP_FLOPS = 10**10
VMEM_LIMIT = 32 * 1024 * 1024
F32 = jnp.float32
BF16 = jnp.bfloat16
I32 = jnp.int32


def nt_dot(a, b):
    return lax.dot_general(a, b, (((1,), (1,)), ((), ())), preferred_element_type=F32)


def iota(shape, dim):
    return lax.broadcasted_iota(I32, shape, dim)


def pack_kernel(plan, me_ref, src_hbm, den_hbm, bin_hbm, ray_hbm, table_hbm, line_hbm, *rest):
    targets, block = plan.targets, plan.block
    out, table_out, line_out, src_ref, den_ref, bin_ref, ray_ref, sems = rest
    copies = [
        pltpu.make_async_copy(a, b, sems.at[i])
        for i, (a, b) in enumerate(
            (
                (bin_hbm, bin_ref),
                (ray_hbm, ray_ref),
                (den_hbm, den_ref),
                (src_hbm, src_ref),
                (table_hbm, table_out),
                (line_hbm, line_out),
            )
        )
    ]
    for copy in copies:
        copy.start()
    cells, levels = src_ref.shape
    earlier = (iota((cells, cells), 0) < iota((cells, cells), 1)).astype(F32).astype(BF16)
    my_half = me_ref[0] // targets
    for copy in copies[:3]:
        copy.wait()
    bins = bin_ref[...]
    hot = (iota((plan.bins, cells), 0) == bins).astype(F32)
    before = jnp.dot(hot.astype(BF16), earlier, preferred_element_type=F32)
    position = jnp.sum(hot * before, axis=0, keepdims=True).astype(I32)
    half = bins // targets
    slot = (bins - half * targets) * block + (half ^ my_half) * plan.capacity + position
    rays = ray_ref[...]
    ray_high = rays // RAY_BASE
    ray_low = rays - ray_high * RAY_BASE
    den = den_ref[...].astype(F32)
    den_row = jnp.concatenate([den[i : i + 1] for i in range(den.shape[0])], axis=1)
    meta = jnp.concatenate(
        [den_row, ray_high.astype(F32), ray_low.astype(F32), jnp.zeros((META_ROWS - 3, cells), F32)],
        axis=0,
    ).astype(BF16)
    place = (iota((targets * block, cells), 0) == slot).astype(F32).astype(BF16)
    moved = nt_dot(meta, place).astype(BF16)
    copies[3].wait()
    rows = jnp.dot(place, src_ref[...], preferred_element_type=F32).astype(BF16)
    out[:, :block, :] = rows.reshape(targets, block, levels)
    out[:, block:, :] = jnp.zeros((targets, META_ROWS, levels), BF16)
    for t in range(targets):
        out[t, block:, :block] = moved[:, t * block : (t + 1) * block]
    for copy in copies[4:]:
        copy.wait()


def keep_kernel(table_ref, out_ref):
    out_ref[...] = table_ref[...]


def level_kernel(plan, rays, got_ref, *refs):
    table_refs, out_ref = refs[:-1], refs[-1]
    targets, block = plan.targets, plan.block
    meta = [got_ref[s, block:, :block].astype(F32) for s in range(targets)]
    columns = [jnp.transpose(m[:8]) for m in meta]
    total = jnp.zeros(out_ref.shape, F32)
    for part, table_ref in enumerate(table_refs):
        low, high = part * plan.capacity, (part + 1) * plan.capacity
        src = got_ref[:, low:high, :].reshape(targets * plan.capacity, got_ref.shape[2])
        den = jnp.concatenate([c[low:high, 0:1] for c in columns], axis=0)
        ray = jnp.concatenate(
            [m[1:2, low:high] * RAY_BASE + m[2:3, low:high] for m in meta], axis=1
        ).astype(I32)
        wide = src.astype(F32)
        table = table_ref[...]
        first = (den * jnp.dot(src, table, preferred_element_type=F32) + wide).astype(BF16)
        pops = (den * jnp.dot(first, table, preferred_element_type=F32) + wide).astype(BF16)
        pick = (iota((rays, src.shape[0]), 0) == ray).astype(F32).astype(BF16)
        total = total + jnp.dot(pick, pops, preferred_element_type=F32)
    out_ref[...] = total.astype(BF16)


def line_kernel(mine_ref, theirs_ref, line_ref, out_ref):
    sums = mine_ref[...] + theirs_ref[...]
    rows = sums.shape[0]
    high = sums.astype(BF16)
    low = (sums - high.astype(F32)).astype(BF16)
    both = jnp.concatenate([high, low], axis=0)
    got = jnp.dot(both, line_ref[...], preferred_element_type=F32)
    out_ref[...] = got[:rows] + got[rows:]


class Plan:
    def __init__(self, bin_total, cells):
        self.bins = bin_total
        self.targets = bin_total // 2
        self.capacity = max(2, 2 * cells // bin_total)
        self.block = 2 * self.capacity

    def table_moves(self):
        return [(i, (i + self.targets) % self.bins) for i in range(self.bins)]

    def halves(self):
        return [list(range(self.targets)), list(range(self.targets, self.bins))]


def per_device(sources, density, temp_bins, ray_index, rate_tables, line_table):
    cells, levels = sources.shape
    bin_total = lax.axis_size("bin")
    wave_total = lax.axis_size("wave")
    plan = Plan(bin_total, cells)
    rows = plan.block + META_ROWS
    params = pltpu.CompilerParams(vmem_limit_bytes=VMEM_LIMIT)
    vmem = pl.BlockSpec(memory_space=pltpu.VMEM)
    smem = pl.BlockSpec(memory_space=pltpu.SMEM)
    hbm = pl.BlockSpec(memory_space=pltpu.HBM)

    def in_hbm(x):
        return pltpu.with_memory_space_constraint(x, pltpu.HBM)

    arrived = lax.ppermute(rate_tables[0], "bin", plan.table_moves())
    me = lax.axis_index("bin").astype(I32).reshape(1)
    den_rows = cells // min(cells, LANES)
    outgoing, own, held_line = pl.pallas_call(
        functools.partial(pack_kernel, plan),
        out_shape=[
            jax.ShapeDtypeStruct(a, BF16)
            for a in ((plan.targets, rows, levels), rate_tables.shape[1:], line_table.shape)
        ],
        in_specs=[smem] + [hbm] * 6,
        out_specs=[vmem] * 3,
        scratch_shapes=[
            pltpu.VMEM((cells, levels), BF16),
            pltpu.VMEM((den_rows, cells // den_rows), BF16),
            pltpu.VMEM((1, cells), I32),
            pltpu.VMEM((1, cells), I32),
            pltpu.SemaphoreType.DMA((6,)),
        ],
        compiler_params=params,
    )(
        me,
        in_hbm(sources),
        in_hbm(density.reshape(den_rows, cells // den_rows)),
        in_hbm(temp_bins.reshape(1, cells)),
        in_hbm(ray_index.reshape(1, cells)),
        in_hbm(rate_tables[0]),
        in_hbm(line_table),
    )
    got = lax.all_to_all(
        outgoing, "bin", split_axis=0, concat_axis=0, tiled=True, axis_index_groups=plan.halves()
    )
    other = pl.pallas_call(
        keep_kernel,
        out_shape=jax.ShapeDtypeStruct(arrived.shape, BF16),
        in_specs=[vmem],
        out_specs=vmem,
        compiler_params=params,
        cost_estimate=pl.CostEstimate(
            flops=OVERLAP_FLOPS, bytes_accessed=4 * arrived.size, transcendentals=0
        ),
    )(arrived)
    ray_rows = RAY_DEV
    rays = ray_rows * bin_total
    partial_sums = pl.pallas_call(
        functools.partial(level_kernel, plan, rays),
        out_shape=jax.ShapeDtypeStruct((rays, levels), BF16),
        in_specs=[vmem] * 3,
        out_specs=vmem,
        compiler_params=params,
    )(got, own, other)
    held = lax.all_to_all(
        partial_sums.reshape(bin_total, ray_rows, levels),
        "bin",
        split_axis=0,
        concat_axis=0,
        tiled=True,
    )
    total = jnp.sum(held.astype(F32), axis=0)
    theirs = jnp.zeros_like(total)
    step = 1
    while step < wave_total:
        total = total + theirs if step > 1 else total
        theirs = lax.ppermute(total, "wave", [(i, i ^ step) for i in range(wave_total)])
        step *= 2
    return pl.pallas_call(
        line_kernel,
        out_shape=jax.ShapeDtypeStruct((ray_rows, line_table.shape[1]), F32),
        in_specs=[vmem, vmem, vmem],
        out_specs=vmem,
        compiler_params=params,
    )(total, theirs, held_line)


def solution(mesh):
    in_specs = (
        P(("bin", "wave"), None),
        P(("bin", "wave")),
        P(("bin", "wave"), None),
        P(("bin", "wave")),
        P("bin", None, None),
        P(None, "wave"),
    )
    return jax.shard_map(
        per_device, mesh=mesh, in_specs=in_specs, out_specs=P("bin", "wave"), check_vma=False
    )
```

```python
import functools

import jax
import jax.numpy as jnp
from jax import lax
from jax.experimental import pallas as pl
from jax.experimental.pallas import tpu as pltpu
from jax.sharding import PartitionSpec as P

RAY_DEV = 16
META_ROWS = 16
RAY_BASE = 32
LANES = 128
OVERLAP_FLOPS = 10**10
VMEM_LIMIT = 32 * 1024 * 1024
F32 = jnp.float32
BF16 = jnp.bfloat16
I32 = jnp.int32


def nt_dot(a, b):
    return lax.dot_general(a, b, (((1,), (1,)), ((), ())), preferred_element_type=F32)


def iota(shape, dim):
    return lax.broadcasted_iota(I32, shape, dim)


def pack_kernel(plan, me_ref, src_hbm, den_hbm, bin_hbm, ray_hbm, table_hbm, line_hbm, *rest):
    targets, block = plan.targets, plan.block
    out, table_out, line_out, src_ref, den_ref, bin_ref, ray_ref, sems = rest
    copies = [
        pltpu.make_async_copy(a, b, sems.at[i])
        for i, (a, b) in enumerate(
            (
                (bin_hbm, bin_ref),
                (ray_hbm, ray_ref),
                (den_hbm, den_ref),
                (src_hbm, src_ref),
                (table_hbm, table_out),
                (line_hbm, line_out),
            )
        )
    ]
    for copy in copies:
        copy.start()
    cells, levels = src_ref.shape
    earlier = (iota((cells, cells), 0) < iota((cells, cells), 1)).astype(F32).astype(BF16)
    my_half = me_ref[0] // targets
    for copy in copies[:3]:
        copy.wait()
    bins = bin_ref[...]
    hot = (iota((plan.bins, cells), 0) == bins).astype(F32)
    before = jnp.dot(hot.astype(BF16), earlier, preferred_element_type=F32)
    position = jnp.sum(hot * before, axis=0, keepdims=True).astype(I32)
    half = bins // targets
    slot = (bins - half * targets) * block + (half ^ my_half) * plan.capacity + position
    rays = ray_ref[...]
    ray_high = rays // RAY_BASE
    ray_low = rays - ray_high * RAY_BASE
    den = den_ref[...].astype(F32)
    den_row = jnp.concatenate([den[i : i + 1] for i in range(den.shape[0])], axis=1)
    meta = jnp.concatenate(
        [den_row, ray_high.astype(F32), ray_low.astype(F32), jnp.zeros((META_ROWS - 3, cells), F32)],
        axis=0,
    ).astype(BF16)
    place = (iota((targets * block, cells), 0) == slot).astype(F32).astype(BF16)
    moved = nt_dot(meta, place).astype(BF16)
    copies[3].wait()
    rows = jnp.dot(place, src_ref[...], preferred_element_type=F32).astype(BF16)
    out[:, :block, :] = rows.reshape(targets, block, levels)
    out[:, block:, :] = jnp.zeros((targets, META_ROWS, levels), BF16)
    for t in range(targets):
        out[t, block:, :block] = moved[:, t * block : (t + 1) * block]
    for copy in copies[4:]:
        copy.wait()


def keep_kernel(table_ref, out_ref):
    out_ref[...] = table_ref[...]


def level_kernel(plan, rays, got_ref, *refs):
    table_refs, out_ref = refs[:-1], refs[-1]
    targets, block = plan.targets, plan.block
    meta = [got_ref[s, block:, :block].astype(F32) for s in range(targets)]
    columns = [jnp.transpose(m[:8]) for m in meta]
    total = jnp.zeros((rays, got_ref.shape[2]), F32)
    for part, table_ref in enumerate(table_refs):
        low, high = part * plan.capacity, (part + 1) * plan.capacity
        src = got_ref[:, low:high, :].reshape(targets * plan.capacity, got_ref.shape[2])
        den = jnp.concatenate([c[low:high, 0:1] for c in columns], axis=0)
        ray = jnp.concatenate(
            [m[1:2, low:high] * RAY_BASE + m[2:3, low:high] for m in meta], axis=1
        ).astype(I32)
        wide = src.astype(F32)
        table = table_ref[...]
        first = (den * jnp.dot(src, table, preferred_element_type=F32) + wide).astype(BF16)
        pops = (den * jnp.dot(first, table, preferred_element_type=F32) + wide).astype(BF16)
        pick = (iota((rays, src.shape[0]), 0) == ray).astype(F32).astype(BF16)
        total = total + jnp.dot(pick, pops, preferred_element_type=F32)
    blocks = total.astype(BF16).reshape(out_ref.shape[0], *out_ref.shape[2:])
    for core in range(out_ref.shape[1]):
        out_ref[:, core] = blocks


def line_kernel(sums_ref, line_ref, out_ref):
    sums = sums_ref[...]
    rows = sums.shape[0]
    high = sums.astype(BF16)
    low = (sums - high.astype(F32)).astype(BF16)
    both = jnp.concatenate([high, low], axis=0)
    got = jnp.dot(both, line_ref[...], preferred_element_type=F32)
    out_ref[...] = got[:rows] + got[rows:]


class Plan:
    def __init__(self, bin_total, cells):
        self.bins = bin_total
        self.targets = bin_total // 2
        self.capacity = max(2, 2 * cells // bin_total)
        self.block = 2 * self.capacity

    def table_moves(self):
        return [(i, (i + self.targets) % self.bins) for i in range(self.bins)]

    def halves(self):
        return [list(range(self.targets)), list(range(self.targets, self.bins))]


def per_device(sources, density, temp_bins, ray_index, rate_tables, line_table):
    cells, levels = sources.shape
    bin_total = lax.axis_size("bin")
    wave_total = lax.axis_size("wave")
    plan = Plan(bin_total, cells)
    rows = plan.block + META_ROWS
    params = pltpu.CompilerParams(vmem_limit_bytes=VMEM_LIMIT)
    vmem = pl.BlockSpec(memory_space=pltpu.VMEM)
    smem = pl.BlockSpec(memory_space=pltpu.SMEM)
    hbm = pl.BlockSpec(memory_space=pltpu.HBM)

    def in_hbm(x):
        return pltpu.with_memory_space_constraint(x, pltpu.HBM)

    arrived = lax.ppermute(rate_tables[0], "bin", plan.table_moves())
    me = lax.axis_index("bin").astype(I32).reshape(1)
    den_rows = cells // min(cells, LANES)
    outgoing, own, held_line = pl.pallas_call(
        functools.partial(pack_kernel, plan),
        out_shape=[
            jax.ShapeDtypeStruct(a, BF16)
            for a in ((plan.targets, rows, levels), rate_tables.shape[1:], line_table.shape)
        ],
        in_specs=[smem] + [hbm] * 6,
        out_specs=[vmem] * 3,
        scratch_shapes=[
            pltpu.VMEM((cells, levels), BF16),
            pltpu.VMEM((den_rows, cells // den_rows), BF16),
            pltpu.VMEM((1, cells), I32),
            pltpu.VMEM((1, cells), I32),
            pltpu.SemaphoreType.DMA((6,)),
        ],
        compiler_params=params,
    )(
        me,
        in_hbm(sources),
        in_hbm(density.reshape(den_rows, cells // den_rows)),
        in_hbm(temp_bins.reshape(1, cells)),
        in_hbm(ray_index.reshape(1, cells)),
        in_hbm(rate_tables[0]),
        in_hbm(line_table),
    )
    got = lax.all_to_all(
        outgoing, "bin", split_axis=0, concat_axis=0, tiled=True, axis_index_groups=plan.halves()
    )
    other = pl.pallas_call(
        keep_kernel,
        out_shape=jax.ShapeDtypeStruct(arrived.shape, BF16),
        in_specs=[vmem],
        out_specs=vmem,
        compiler_params=params,
        cost_estimate=pl.CostEstimate(
            flops=OVERLAP_FLOPS, bytes_accessed=4 * arrived.size, transcendentals=0
        ),
    )(arrived)
    ray_rows = RAY_DEV
    rays = ray_rows * bin_total
    partial_sums = pl.pallas_call(
        functools.partial(level_kernel, plan, rays),
        out_shape=jax.ShapeDtypeStruct((bin_total, wave_total, ray_rows, levels), BF16),
        in_specs=[vmem] * 3,
        out_specs=vmem,
        compiler_params=params,
    )(got, own, other)
    held = lax.all_to_all(
        partial_sums.reshape(bin_total * wave_total, ray_rows, levels),
        ("bin", "wave"),
        split_axis=0,
        concat_axis=0,
        tiled=True,
    )
    total = jnp.sum(held.astype(F32), axis=0)
    return pl.pallas_call(
        line_kernel,
        out_shape=jax.ShapeDtypeStruct((ray_rows, line_table.shape[1]), F32),
        in_specs=[vmem, vmem],
        out_specs=vmem,
        compiler_params=params,
    )(total, held_line)


def solution(mesh):
    in_specs = (
        P(("bin", "wave"), None),
        P(("bin", "wave")),
        P(("bin", "wave"), None),
        P(("bin", "wave")),
        P("bin", None, None),
        P(None, "wave"),
    )
    return jax.shard_map(
        per_device, mesh=mesh, in_specs=in_specs, out_specs=P("bin", "wave"), check_vma=False
    )
```

```python
import functools

import jax
import jax.numpy as jnp
from jax import lax
from jax.experimental import pallas as pl
from jax.experimental.pallas import tpu as pltpu
from jax.sharding import PartitionSpec as P

RAY_DEV = 16
META_ROWS = 16
RAY_BASE = 32
LANES = 128
OVERLAP_FLOPS = 10**10
VMEM_LIMIT = 32 * 1024 * 1024
F32 = jnp.float32
BF16 = jnp.bfloat16
I32 = jnp.int32


def nt_dot(a, b):
    return lax.dot_general(a, b, (((1,), (1,)), ((), ())), preferred_element_type=F32)


def iota(shape, dim):
    return lax.broadcasted_iota(I32, shape, dim)


def pack_kernel(plan, src_hbm, den_hbm, bin_hbm, ray_hbm, line_hbm, *rest):
    targets, block = plan.targets, plan.block
    out, line_out, src_ref, den_ref, bin_ref, ray_ref, sems = rest
    copies = [
        pltpu.make_async_copy(a, b, sems.at[i])
        for i, (a, b) in enumerate(
            (
                (bin_hbm, bin_ref),
                (ray_hbm, ray_ref),
                (den_hbm, den_ref),
                (src_hbm, src_ref),
                (line_hbm, line_out),
            )
        )
    ]
    for copy in copies:
        copy.start()
    cells, levels = src_ref.shape
    earlier = (iota((cells, cells), 0) < iota((cells, cells), 1)).astype(F32).astype(BF16)
    for copy in copies[:3]:
        copy.wait()
    bins = bin_ref[...]
    hot = (iota((plan.bins, cells), 0) == bins).astype(F32)
    before = jnp.dot(hot.astype(BF16), earlier, preferred_element_type=F32)
    position = jnp.sum(hot * before, axis=0, keepdims=True).astype(I32)
    half = bins // targets
    slot = (bins - half * targets) * block + half * plan.capacity + position
    rays = ray_ref[...]
    ray_high = rays // RAY_BASE
    ray_low = rays - ray_high * RAY_BASE
    den = den_ref[...].astype(F32)
    den_row = jnp.concatenate([den[i : i + 1] for i in range(den.shape[0])], axis=1)
    meta = jnp.concatenate(
        [den_row, ray_high.astype(F32), ray_low.astype(F32), jnp.zeros((META_ROWS - 3, cells), F32)],
        axis=0,
    ).astype(BF16)
    place = (iota((targets * block, cells), 0) == slot).astype(F32).astype(BF16)
    moved = nt_dot(meta, place).astype(BF16)
    copies[3].wait()
    rows = jnp.dot(place, src_ref[...], preferred_element_type=F32).astype(BF16)
    out[:, :block, :] = rows.reshape(targets, block, levels)
    out[:, block:, :] = jnp.zeros((targets, META_ROWS, levels), BF16)
    for t in range(targets):
        out[t, block:, :block] = moved[:, t * block : (t + 1) * block]
    for copy in copies[4:]:
        copy.wait()


def keep_kernel(tables_ref, out_ref):
    out_ref[...] = tables_ref[...]


def level_kernel(plan, rays, got_ref, tables_ref, out_ref):
    targets, block = plan.targets, plan.block
    meta = [got_ref[s, block:, :block].astype(F32) for s in range(targets)]
    columns = [jnp.transpose(m[:8]) for m in meta]
    total = jnp.zeros(out_ref.shape, F32)
    for part in range(2):
        low, high = part * plan.capacity, (part + 1) * plan.capacity
        src = got_ref[:, low:high, :].reshape(targets * plan.capacity, got_ref.shape[2])
        den = jnp.concatenate([c[low:high, 0:1] for c in columns], axis=0)
        ray = jnp.concatenate(
            [m[1:2, low:high] * RAY_BASE + m[2:3, low:high] for m in meta], axis=1
        ).astype(I32)
        wide = src.astype(F32)
        table = tables_ref[part]
        first = (den * jnp.dot(src, table, preferred_element_type=F32) + wide).astype(BF16)
        pops = (den * jnp.dot(first, table, preferred_element_type=F32) + wide).astype(BF16)
        pick = (iota((rays, src.shape[0]), 0) == ray).astype(F32).astype(BF16)
        total = total + jnp.dot(pick, pops, preferred_element_type=F32)
    out_ref[...] = total.astype(BF16)


def line_kernel(mine_ref, theirs_ref, line_ref, out_ref):
    sums = mine_ref[...] + theirs_ref[...]
    rows = sums.shape[0]
    high = sums.astype(BF16)
    low = (sums - high.astype(F32)).astype(BF16)
    both = jnp.concatenate([high, low], axis=0)
    got = jnp.dot(both, line_ref[...], preferred_element_type=F32)
    out_ref[...] = got[:rows] + got[rows:]


class Plan:
    def __init__(self, bin_total, cells):
        self.bins = bin_total
        self.targets = bin_total // 2
        self.capacity = max(2, 2 * cells // bin_total)
        self.block = 2 * self.capacity

    def pairs(self):
        return [[i, i + self.targets] for i in range(self.targets)]

    def halves(self):
        return [list(range(self.targets)), list(range(self.targets, self.bins))]


def per_device(sources, density, temp_bins, ray_index, rate_tables, line_table):
    cells, levels = sources.shape
    bin_total = lax.axis_size("bin")
    wave_total = lax.axis_size("wave")
    plan = Plan(bin_total, cells)
    rows = plan.block + META_ROWS
    params = pltpu.CompilerParams(vmem_limit_bytes=VMEM_LIMIT)
    vmem = pl.BlockSpec(memory_space=pltpu.VMEM)
    hbm = pl.BlockSpec(memory_space=pltpu.HBM)

    def in_hbm(x):
        return pltpu.with_memory_space_constraint(x, pltpu.HBM)

    arrived = lax.all_gather(rate_tables[0], "bin", axis_index_groups=plan.pairs())
    den_rows = cells // min(cells, LANES)
    outgoing, held_line = pl.pallas_call(
        functools.partial(pack_kernel, plan),
        out_shape=[
            jax.ShapeDtypeStruct(a, BF16)
            for a in ((plan.targets, rows, levels), line_table.shape)
        ],
        in_specs=[hbm] * 5,
        out_specs=[vmem] * 2,
        scratch_shapes=[
            pltpu.VMEM((cells, levels), BF16),
            pltpu.VMEM((den_rows, cells // den_rows), BF16),
            pltpu.VMEM((1, cells), I32),
            pltpu.VMEM((1, cells), I32),
            pltpu.SemaphoreType.DMA((5,)),
        ],
        compiler_params=params,
    )(
        in_hbm(sources),
        in_hbm(density.reshape(den_rows, cells // den_rows)),
        in_hbm(temp_bins.reshape(1, cells)),
        in_hbm(ray_index.reshape(1, cells)),
        in_hbm(line_table),
    )
    got = lax.all_to_all(
        outgoing, "bin", split_axis=0, concat_axis=0, tiled=True, axis_index_groups=plan.halves()
    )
    tables = pl.pallas_call(
        keep_kernel,
        out_shape=jax.ShapeDtypeStruct(arrived.shape, BF16),
        in_specs=[vmem],
        out_specs=vmem,
        compiler_params=params,
        cost_estimate=pl.CostEstimate(
            flops=OVERLAP_FLOPS, bytes_accessed=4 * arrived.size, transcendentals=0
        ),
    )(arrived)
    ray_rows = RAY_DEV
    rays = ray_rows * bin_total
    partial_sums = pl.pallas_call(
        functools.partial(level_kernel, plan, rays),
        out_shape=jax.ShapeDtypeStruct((rays, levels), BF16),
        in_specs=[vmem] * 2,
        out_specs=vmem,
        compiler_params=params,
    )(got, tables)
    held = lax.all_to_all(
        partial_sums.reshape(bin_total, ray_rows, levels),
        "bin",
        split_axis=0,
        concat_axis=0,
        tiled=True,
    )
    total = jnp.sum(held.astype(F32), axis=0)
    theirs = jnp.zeros_like(total)
    step = 1
    while step < wave_total:
        total = total + theirs if step > 1 else total
        theirs = lax.ppermute(total, "wave", [(i, i ^ step) for i in range(wave_total)])
        step *= 2
    return pl.pallas_call(
        line_kernel,
        out_shape=jax.ShapeDtypeStruct((ray_rows, line_table.shape[1]), F32),
        in_specs=[vmem, vmem, vmem],
        out_specs=vmem,
        compiler_params=params,
    )(total, theirs, held_line)


def solution(mesh):
    in_specs = (
        P(("bin", "wave"), None),
        P(("bin", "wave")),
        P(("bin", "wave"), None),
        P(("bin", "wave")),
        P("bin", None, None),
        P(None, "wave"),
    )
    return jax.shard_map(
        per_device, mesh=mesh, in_specs=in_specs, out_specs=P("bin", "wave"), check_vma=False
    )
```

```python
import functools

import jax
import jax.numpy as jnp
from jax import lax
from jax.experimental import pallas as pl
from jax.experimental.pallas import tpu as pltpu
from jax.sharding import PartitionSpec as P

RAY_DEV = 16
META_ROWS = 16
RAY_BASE = 32
LANES = 128
OVERLAP_FLOPS = 10**10
VMEM_LIMIT = 32 * 1024 * 1024
F32 = jnp.float32
BF16 = jnp.bfloat16
I32 = jnp.int32


def nt_dot(a, b):
    return lax.dot_general(a, b, (((1,), (1,)), ((), ())), preferred_element_type=F32)


def iota(shape, dim):
    return lax.broadcasted_iota(I32, shape, dim)


def pack_kernel(plan, me_ref, src_hbm, den_hbm, bin_hbm, ray_hbm, table_hbm, line_hbm, *rest):
    targets, block = plan.targets, plan.block
    out, table_out, line_out, src_ref, den_ref, bin_ref, ray_ref, sems = rest
    copies = [
        pltpu.make_async_copy(a, b, sems.at[i])
        for i, (a, b) in enumerate(
            (
                (bin_hbm, bin_ref),
                (ray_hbm, ray_ref),
                (den_hbm, den_ref),
                (src_hbm, src_ref),
                (table_hbm, table_out),
                (line_hbm, line_out),
            )
        )
    ]
    for copy in copies:
        copy.start()
    cells, levels = src_ref.shape
    earlier = (iota((cells, cells), 0) < iota((cells, cells), 1)).astype(F32).astype(BF16)
    my_half = me_ref[0] // targets
    for copy in copies[:3]:
        copy.wait()
    bins = bin_ref[...]
    hot = (iota((plan.bins, cells), 0) == bins).astype(F32)
    before = jnp.dot(hot.astype(BF16), earlier, preferred_element_type=F32)
    position = jnp.sum(hot * before, axis=0, keepdims=True).astype(I32)
    half = bins // targets
    slot = (bins - half * targets) * block + (half ^ my_half) * plan.capacity + position
    rays = ray_ref[...]
    ray_high = rays // RAY_BASE
    ray_low = rays - ray_high * RAY_BASE
    den = den_ref[...].astype(F32)
    den_row = jnp.concatenate([den[i : i + 1] for i in range(den.shape[0])], axis=1)
    meta = jnp.concatenate(
        [den_row, ray_high.astype(F32), ray_low.astype(F32), jnp.zeros((META_ROWS - 3, cells), F32)],
        axis=0,
    ).astype(BF16)
    place = (iota((targets * block, cells), 0) == slot).astype(F32).astype(BF16)
    moved = nt_dot(meta, place).astype(BF16)
    copies[3].wait()
    rows = jnp.dot(place, src_ref[...], preferred_element_type=F32).astype(BF16)
    out[:, :block, :] = rows.reshape(targets, block, levels)
    out[:, block:, :] = jnp.zeros((targets, META_ROWS, levels), BF16)
    for t in range(targets):
        out[t, block:, :block] = moved[:, t * block : (t + 1) * block]
    for copy in copies[4:]:
        copy.wait()


def keep_kernel(table_ref, out_ref):
    out_ref[...] = table_ref[...]


def level_kernel(plan, ray_rows, me_ref, got_ref, *refs):
    table_refs, out_ref = refs[:-1], refs[-1]
    targets, block = plan.targets, plan.block
    rays = plan.bins * ray_rows
    my_half = me_ref[0] // targets
    meta = [got_ref[s, block:, :block].astype(F32) for s in range(targets)]
    columns = [jnp.transpose(m[:8]) for m in meta]
    total = jnp.zeros((rays, got_ref.shape[2]), F32)
    for part, table_ref in enumerate(table_refs):
        low, high = part * plan.capacity, (part + 1) * plan.capacity
        src = got_ref[:, low:high, :].reshape(targets * plan.capacity, got_ref.shape[2])
        den = jnp.concatenate([c[low:high, 0:1] for c in columns], axis=0)
        ray = jnp.concatenate(
            [m[1:2, low:high] * RAY_BASE + m[2:3, low:high] for m in meta], axis=1
        ).astype(I32)
        owner = ray // ray_rows
        half = owner // targets
        place = (owner - half * targets) * 2 + (half ^ my_half)
        row = place * ray_rows + (ray - owner * ray_rows)
        wide = src.astype(F32)
        table = table_ref[...]
        first = (den * jnp.dot(src, table, preferred_element_type=F32) + wide).astype(BF16)
        pops = (den * jnp.dot(first, table, preferred_element_type=F32) + wide).astype(BF16)
        pick = (iota((rays, src.shape[0]), 0) == row).astype(F32).astype(BF16)
        total = total + jnp.dot(pick, pops, preferred_element_type=F32)
    out_ref[...] = total.astype(BF16).reshape(out_ref.shape)


def line_kernel(mine_ref, *refs):
    theirs, line_ref, out_ref = refs[:-2], refs[-2], refs[-1]
    sums = mine_ref[...]
    for their in theirs:
        sums = sums + their[...].astype(F32)
    rows = sums.shape[0]
    high = sums.astype(BF16)
    low = (sums - high.astype(F32)).astype(BF16)
    both = jnp.concatenate([high, low], axis=0)
    got = jnp.dot(both, line_ref[...], preferred_element_type=F32)
    out_ref[...] = got[:rows] + got[rows:]


class Plan:
    def __init__(self, bin_total, cells):
        self.bins = bin_total
        self.targets = bin_total // 2
        self.capacity = max(2, 2 * cells // bin_total)
        self.block = 2 * self.capacity

    def table_moves(self):
        return [(i, (i + self.targets) % self.bins) for i in range(self.bins)]

    def sum_moves(self, wave_total, flip, turn):
        return [
            (b * wave_total + w, (b + flip * self.targets) % self.bins * wave_total + (w ^ turn))
            for b in range(self.bins)
            for w in range(wave_total)
        ]

    def halves(self):
        return [list(range(self.targets)), list(range(self.targets, self.bins))]


def per_device(sources, density, temp_bins, ray_index, rate_tables, line_table):
    cells, levels = sources.shape
    bin_total = lax.axis_size("bin")
    wave_total = lax.axis_size("wave")
    plan = Plan(bin_total, cells)
    rows = plan.block + META_ROWS
    params = pltpu.CompilerParams(vmem_limit_bytes=VMEM_LIMIT)
    vmem = pl.BlockSpec(memory_space=pltpu.VMEM)
    smem = pl.BlockSpec(memory_space=pltpu.SMEM)
    hbm = pl.BlockSpec(memory_space=pltpu.HBM)

    def in_hbm(x):
        return pltpu.with_memory_space_constraint(x, pltpu.HBM)

    arrived = lax.ppermute(rate_tables[0], "bin", plan.table_moves())
    me = lax.axis_index("bin").astype(I32).reshape(1)
    den_rows = cells // min(cells, LANES)
    outgoing, own, held_line = pl.pallas_call(
        functools.partial(pack_kernel, plan),
        out_shape=[
            jax.ShapeDtypeStruct(a, BF16)
            for a in ((plan.targets, rows, levels), rate_tables.shape[1:], line_table.shape)
        ],
        in_specs=[smem] + [hbm] * 6,
        out_specs=[vmem] * 3,
        scratch_shapes=[
            pltpu.VMEM((cells, levels), BF16),
            pltpu.VMEM((den_rows, cells // den_rows), BF16),
            pltpu.VMEM((1, cells), I32),
            pltpu.VMEM((1, cells), I32),
            pltpu.SemaphoreType.DMA((6,)),
        ],
        compiler_params=params,
    )(
        me,
        in_hbm(sources),
        in_hbm(density.reshape(den_rows, cells // den_rows)),
        in_hbm(temp_bins.reshape(1, cells)),
        in_hbm(ray_index.reshape(1, cells)),
        in_hbm(rate_tables[0]),
        in_hbm(line_table),
    )
    got = lax.all_to_all(
        outgoing, "bin", split_axis=0, concat_axis=0, tiled=True, axis_index_groups=plan.halves()
    )
    other = pl.pallas_call(
        keep_kernel,
        out_shape=jax.ShapeDtypeStruct(arrived.shape, BF16),
        in_specs=[vmem],
        out_specs=vmem,
        compiler_params=params,
        cost_estimate=pl.CostEstimate(
            flops=OVERLAP_FLOPS, bytes_accessed=4 * arrived.size, transcendentals=0
        ),
    )(arrived)
    ray_rows = RAY_DEV
    partial_sums = pl.pallas_call(
        functools.partial(level_kernel, plan, ray_rows),
        out_shape=jax.ShapeDtypeStruct((plan.targets, 2 * ray_rows, levels), BF16),
        in_specs=[smem] + [vmem] * 3,
        out_specs=vmem,
        compiler_params=params,
    )(me, got, own, other)
    held = lax.all_to_all(
        partial_sums, "bin", split_axis=0, concat_axis=0, tiled=True, axis_index_groups=plan.halves()
    )
    sums = jnp.sum(held.astype(F32), axis=0)
    mine, opposite = sums[:ray_rows], sums[ray_rows:].astype(BF16)
    near = sums[:ray_rows].astype(BF16)
    theirs = [
        lax.ppermute(value, ("bin", "wave"), plan.sum_moves(wave_total, flip, turn))
        for value, flip, turn in [(opposite, 1, w) for w in range(wave_total)]
        + [(near, 0, w) for w in range(1, wave_total)]
    ]
    return pl.pallas_call(
        line_kernel,
        out_shape=jax.ShapeDtypeStruct((ray_rows, line_table.shape[1]), F32),
        in_specs=[vmem] * (2 + len(theirs)),
        out_specs=vmem,
        compiler_params=params,
    )(mine, *theirs, held_line)


def solution(mesh):
    in_specs = (
        P(("bin", "wave"), None),
        P(("bin", "wave")),
        P(("bin", "wave"), None),
        P(("bin", "wave")),
        P("bin", None, None),
        P(None, "wave"),
    )
    return jax.shard_map(
        per_device, mesh=mesh, in_specs=in_specs, out_specs=P("bin", "wave"), check_vma=False
    )
```

```python
import functools

import jax
import jax.numpy as jnp
from jax import lax
from jax.experimental import pallas as pl
from jax.experimental.pallas import tpu as pltpu
from jax.sharding import PartitionSpec as P

RAY_DEV = 16
META_ROWS = 16
RAY_BASE = 32
LANES = 128
LINE_CHUNKS = 4
OVERLAP_FLOPS = 10**10
VMEM_LIMIT = 32 * 1024 * 1024
F32 = jnp.float32
BF16 = jnp.bfloat16
I32 = jnp.int32


def nt_dot(a, b):
    return lax.dot_general(a, b, (((1,), (1,)), ((), ())), preferred_element_type=F32)


def iota(shape, dim):
    return lax.broadcasted_iota(I32, shape, dim)


def pack_kernel(plan, me_ref, src_hbm, den_hbm, bin_hbm, ray_hbm, table_hbm, line_hbm, *rest):
    targets, block = plan.targets, plan.block
    out, table_out, line_out, src_ref, den_ref, bin_ref, ray_ref, sems = rest
    copies = [
        pltpu.make_async_copy(a, b, sems.at[i])
        for i, (a, b) in enumerate(
            (
                (bin_hbm, bin_ref),
                (ray_hbm, ray_ref),
                (den_hbm, den_ref),
                (src_hbm, src_ref),
                (table_hbm, table_out),
                (line_hbm, line_out),
            )
        )
    ]
    for copy in copies:
        copy.start()
    cells, levels = src_ref.shape
    earlier = (iota((cells, cells), 0) < iota((cells, cells), 1)).astype(F32).astype(BF16)
    my_half = me_ref[0] // targets
    for copy in copies[:3]:
        copy.wait()
    bins = bin_ref[...]
    hot = (iota((plan.bins, cells), 0) == bins).astype(F32)
    before = jnp.dot(hot.astype(BF16), earlier, preferred_element_type=F32)
    position = jnp.sum(hot * before, axis=0, keepdims=True).astype(I32)
    half = bins // targets
    slot = (bins - half * targets) * block + (half ^ my_half) * plan.capacity + position
    rays = ray_ref[...]
    ray_high = rays // RAY_BASE
    ray_low = rays - ray_high * RAY_BASE
    den = den_ref[...].astype(F32)
    den_row = jnp.concatenate([den[i : i + 1] for i in range(den.shape[0])], axis=1)
    meta = jnp.concatenate(
        [den_row, ray_high.astype(F32), ray_low.astype(F32), jnp.zeros((META_ROWS - 3, cells), F32)],
        axis=0,
    ).astype(BF16)
    place = (iota((targets * block, cells), 0) == slot).astype(F32).astype(BF16)
    moved = nt_dot(meta, place).astype(BF16)
    copies[3].wait()
    rows = jnp.dot(place, src_ref[...], preferred_element_type=F32).astype(BF16)
    out[:, :block, :] = rows.reshape(targets, block, levels)
    out[:, block:, :] = jnp.zeros((targets, META_ROWS, levels), BF16)
    for t in range(targets):
        out[t, block:, :block] = moved[:, t * block : (t + 1) * block]
    for copy in copies[4:]:
        copy.wait()


def keep_kernel(table_ref, out_ref):
    out_ref[...] = table_ref[...]


def level_kernel(plan, rays, got_ref, *refs):
    table_refs, out_ref = refs[:-1], refs[-1]
    targets, block = plan.targets, plan.block
    meta = [got_ref[s, block:, :block].astype(F32) for s in range(targets)]
    columns = [jnp.transpose(m[:8]) for m in meta]
    total = jnp.zeros(out_ref.shape, F32)
    for part, table_ref in enumerate(table_refs):
        low, high = part * plan.capacity, (part + 1) * plan.capacity
        src = got_ref[:, low:high, :].reshape(targets * plan.capacity, got_ref.shape[2])
        den = jnp.concatenate([c[low:high, 0:1] for c in columns], axis=0)
        ray = jnp.concatenate(
            [m[1:2, low:high] * RAY_BASE + m[2:3, low:high] for m in meta], axis=1
        ).astype(I32)
        wide = src.astype(F32)
        table = table_ref[...]
        first = (den * jnp.dot(src, table, preferred_element_type=F32) + wide).astype(BF16)
        pops = (den * jnp.dot(first, table, preferred_element_type=F32) + wide).astype(BF16)
        pick = (iota((rays, src.shape[0]), 0) == ray).astype(F32).astype(BF16)
        total = total + jnp.dot(pick, pops, preferred_element_type=F32)
    out_ref[...] = total.astype(BF16)


def line_kernel(mine_ref, theirs_ref, line_ref, out_hbm, out_ref, sems):
    sums = mine_ref[...] + theirs_ref[...]
    rows = sums.shape[0]
    high = sums.astype(BF16)
    low = (sums - high.astype(F32)).astype(BF16)
    both = jnp.concatenate([high, low], axis=0)
    chunks = sems.shape[0]
    width = out_ref.shape[1] // chunks
    copies = []
    for i in range(chunks):
        part = pl.ds(i * width, width)
        got = jnp.dot(both, line_ref[:, part], preferred_element_type=F32)
        out_ref[:, part] = got[:rows] + got[rows:]
        copies.append(pltpu.make_async_copy(out_ref.at[:, part], out_hbm.at[:, part], sems.at[i]))
        copies[-1].start()
    for copy in copies:
        copy.wait()


class Plan:
    def __init__(self, bin_total, cells):
        self.bins = bin_total
        self.targets = bin_total // 2
        self.capacity = max(2, 2 * cells // bin_total)
        self.block = 2 * self.capacity

    def table_moves(self):
        return [(i, (i + self.targets) % self.bins) for i in range(self.bins)]

    def halves(self):
        return [list(range(self.targets)), list(range(self.targets, self.bins))]


def per_device(sources, density, temp_bins, ray_index, rate_tables, line_table):
    cells, levels = sources.shape
    bin_total = lax.axis_size("bin")
    wave_total = lax.axis_size("wave")
    plan = Plan(bin_total, cells)
    rows = plan.block + META_ROWS
    params = pltpu.CompilerParams(vmem_limit_bytes=VMEM_LIMIT)
    vmem = pl.BlockSpec(memory_space=pltpu.VMEM)
    smem = pl.BlockSpec(memory_space=pltpu.SMEM)
    hbm = pl.BlockSpec(memory_space=pltpu.HBM)

    def in_hbm(x):
        return pltpu.with_memory_space_constraint(x, pltpu.HBM)

    arrived = lax.ppermute(rate_tables[0], "bin", plan.table_moves())
    me = lax.axis_index("bin").astype(I32).reshape(1)
    den_rows = cells // min(cells, LANES)
    outgoing, own, held_line = pl.pallas_call(
        functools.partial(pack_kernel, plan),
        out_shape=[
            pltpu.VMEM(a, BF16)
            for a in ((plan.targets, rows, levels), rate_tables.shape[1:], line_table.shape)
        ],
        in_specs=[smem] + [hbm] * 6,
        out_specs=[vmem] * 3,
        scratch_shapes=[
            pltpu.VMEM((cells, levels), BF16),
            pltpu.VMEM((den_rows, cells // den_rows), BF16),
            pltpu.VMEM((1, cells), I32),
            pltpu.VMEM((1, cells), I32),
            pltpu.SemaphoreType.DMA((6,)),
        ],
        compiler_params=params,
    )(
        me,
        in_hbm(sources),
        in_hbm(density.reshape(den_rows, cells // den_rows)),
        in_hbm(temp_bins.reshape(1, cells)),
        in_hbm(ray_index.reshape(1, cells)),
        in_hbm(rate_tables[0]),
        in_hbm(line_table),
    )
    got = lax.all_to_all(
        outgoing, "bin", split_axis=0, concat_axis=0, tiled=True, axis_index_groups=plan.halves()
    )
    other = pl.pallas_call(
        keep_kernel,
        out_shape=jax.ShapeDtypeStruct(arrived.shape, BF16),
        in_specs=[vmem],
        out_specs=vmem,
        compiler_params=params,
        cost_estimate=pl.CostEstimate(
            flops=OVERLAP_FLOPS, bytes_accessed=4 * arrived.size, transcendentals=0
        ),
    )(arrived)
    ray_rows = RAY_DEV
    rays = ray_rows * bin_total
    partial_sums = pl.pallas_call(
        functools.partial(level_kernel, plan, rays),
        out_shape=jax.ShapeDtypeStruct((rays, levels), BF16),
        in_specs=[vmem] * 3,
        out_specs=vmem,
        compiler_params=params,
    )(got, own, other)
    held = lax.all_to_all(
        partial_sums.reshape(bin_total, ray_rows, levels),
        "bin",
        split_axis=0,
        concat_axis=0,
        tiled=True,
    )
    total = jnp.sum(held.astype(F32), axis=0)
    theirs = jnp.zeros_like(total)
    step = 1
    while step < wave_total:
        total = total + theirs if step > 1 else total
        theirs = lax.ppermute(total, "wave", [(i, i ^ step) for i in range(wave_total)])
        step *= 2
    out_shape = (ray_rows, line_table.shape[1])
    return pl.pallas_call(
        line_kernel,
        out_shape=jax.ShapeDtypeStruct(out_shape, F32),
        in_specs=[vmem, vmem, vmem],
        out_specs=hbm,
        scratch_shapes=[pltpu.VMEM(out_shape, F32), pltpu.SemaphoreType.DMA((LINE_CHUNKS,))],
        compiler_params=params,
    )(total, theirs, held_line)


def solution(mesh):
    in_specs = (
        P(("bin", "wave"), None),
        P(("bin", "wave")),
        P(("bin", "wave"), None),
        P(("bin", "wave")),
        P("bin", None, None),
        P(None, "wave"),
    )
    return jax.shard_map(
        per_device, mesh=mesh, in_specs=in_specs, out_specs=P("bin", "wave"), check_vma=False
    )
```

```python
import functools

import jax
import jax.numpy as jnp
from jax import lax
from jax.experimental import pallas as pl
from jax.experimental.pallas import tpu as pltpu
from jax.sharding import PartitionSpec as P

RAY_DEV = 16
META_ROWS = 16
RAY_BASE = 32
LANES = 128
OVERLAP_FLOPS = 10**10
VMEM_LIMIT = 32 * 1024 * 1024
F32 = jnp.float32
BF16 = jnp.bfloat16
I32 = jnp.int32


def nt_dot(a, b):
    return lax.dot_general(a, b, (((1,), (1,)), ((), ())), preferred_element_type=F32)


def iota(shape, dim):
    return lax.broadcasted_iota(I32, shape, dim)


def pack_kernel(plan, me_ref, src_hbm, den_hbm, bin_hbm, ray_hbm, table_hbm, line_hbm, *rest):
    targets, block = plan.targets, plan.block
    outs, table_out, line_out = rest[:targets], rest[targets], rest[targets + 1]
    src_ref, den_ref, bin_ref, ray_ref, sems = rest[targets + 2 :]
    copies = [
        pltpu.make_async_copy(a, b, sems.at[i])
        for i, (a, b) in enumerate(
            (
                (bin_hbm, bin_ref),
                (ray_hbm, ray_ref),
                (den_hbm, den_ref),
                (src_hbm, src_ref),
                (table_hbm, table_out),
                (line_hbm, line_out),
            )
        )
    ]
    for copy in copies:
        copy.start()
    cells, levels = src_ref.shape
    earlier = (iota((cells, cells), 0) < iota((cells, cells), 1)).astype(F32).astype(BF16)
    for copy in copies[:3]:
        copy.wait()
    bins = bin_ref[...]
    hot = (iota((plan.bins, cells), 0) == bins).astype(F32)
    before = jnp.dot(hot.astype(BF16), earlier, preferred_element_type=F32)
    position = jnp.sum(hot * before, axis=0, keepdims=True).astype(I32)
    turn = bins ^ me_ref[0]
    half = turn // targets
    slot = (turn - half * targets) * block + half * plan.capacity + position
    rays = ray_ref[...]
    ray_high = rays // RAY_BASE
    ray_low = rays - ray_high * RAY_BASE
    den = den_ref[...].astype(F32)
    den_row = jnp.concatenate([den[i : i + 1] for i in range(den.shape[0])], axis=1)
    meta = jnp.concatenate(
        [den_row, ray_high.astype(F32), ray_low.astype(F32), jnp.zeros((META_ROWS - 3, cells), F32)],
        axis=0,
    ).astype(BF16)
    place = (iota((targets * block, cells), 0) == slot).astype(F32).astype(BF16)
    moved = nt_dot(meta, place).astype(BF16)
    copies[3].wait()
    rows = jnp.dot(place, src_ref[...], preferred_element_type=F32).astype(BF16)
    for t in range(targets):
        first, last = t * block, (t + 1) * block
        outs[t][:block, :] = rows[first:last]
        outs[t][block:, :] = jnp.zeros((META_ROWS, levels), BF16)
        outs[t][block:, :block] = moved[:, first:last]
    for copy in copies[4:]:
        copy.wait()


def keep_kernel(table_ref, out_ref):
    out_ref[...] = table_ref[...]


def level_kernel(plan, rays, *refs):
    got, table_refs, out_ref = refs[: plan.targets], refs[plan.targets : -1], refs[-1]
    block = plan.block
    meta = [g[block:, :block].astype(F32) for g in got]
    columns = [jnp.transpose(m[:8]) for m in meta]
    total = jnp.zeros(out_ref.shape, F32)
    for part, table_ref in enumerate(table_refs):
        low, high = part * plan.capacity, (part + 1) * plan.capacity
        src = jnp.concatenate([g[low:high, :] for g in got], axis=0)
        den = jnp.concatenate([c[low:high, 0:1] for c in columns], axis=0)
        ray = jnp.concatenate(
            [m[1:2, low:high] * RAY_BASE + m[2:3, low:high] for m in meta], axis=1
        ).astype(I32)
        wide = src.astype(F32)
        table = table_ref[...]
        first = (den * jnp.dot(src, table, preferred_element_type=F32) + wide).astype(BF16)
        pops = (den * jnp.dot(first, table, preferred_element_type=F32) + wide).astype(BF16)
        pick = (iota((rays, src.shape[0]), 0) == ray).astype(F32).astype(BF16)
        total = total + jnp.dot(pick, pops, preferred_element_type=F32)
    out_ref[...] = total.astype(BF16)


def line_kernel(mine_ref, theirs_ref, line_ref, out_ref):
    sums = mine_ref[...] + theirs_ref[...]
    rows = sums.shape[0]
    high = sums.astype(BF16)
    low = (sums - high.astype(F32)).astype(BF16)
    both = jnp.concatenate([high, low], axis=0)
    got = jnp.dot(both, line_ref[...], preferred_element_type=F32)
    out_ref[...] = got[:rows] + got[rows:]


class Plan:
    def __init__(self, bin_total, cells):
        self.bins = bin_total
        self.targets = bin_total // 2
        self.capacity = max(2, 2 * cells // bin_total)
        self.block = 2 * self.capacity

    def table_moves(self):
        return [(i, (i + self.targets) % self.bins) for i in range(self.bins)]

    def order(self):
        return sorted(range(1, self.targets), key=lambda k: -bin(k).count("1"))

    def moves(self, k):
        return [(i, i ^ k) for i in range(self.bins)]


def per_device(sources, density, temp_bins, ray_index, rate_tables, line_table):
    cells, levels = sources.shape
    bin_total = lax.axis_size("bin")
    wave_total = lax.axis_size("wave")
    plan = Plan(bin_total, cells)
    rows = plan.block + META_ROWS
    params = pltpu.CompilerParams(vmem_limit_bytes=VMEM_LIMIT)
    vmem = pl.BlockSpec(memory_space=pltpu.VMEM)
    smem = pl.BlockSpec(memory_space=pltpu.SMEM)
    hbm = pl.BlockSpec(memory_space=pltpu.HBM)

    def in_hbm(x):
        return pltpu.with_memory_space_constraint(x, pltpu.HBM)

    arrived = lax.ppermute(rate_tables[0], "bin", plan.table_moves())
    me = lax.axis_index("bin").astype(I32).reshape(1)
    den_rows = cells // min(cells, LANES)
    *outgoing, own, held_line = pl.pallas_call(
        functools.partial(pack_kernel, plan),
        out_shape=[
            jax.ShapeDtypeStruct(a, BF16)
            for a in [(rows, levels)] * plan.targets + [rate_tables.shape[1:], line_table.shape]
        ],
        in_specs=[smem] + [hbm] * 6,
        out_specs=[vmem] * (plan.targets + 2),
        scratch_shapes=[
            pltpu.VMEM((cells, levels), BF16),
            pltpu.VMEM((den_rows, cells // den_rows), BF16),
            pltpu.VMEM((1, cells), I32),
            pltpu.VMEM((1, cells), I32),
            pltpu.SemaphoreType.DMA((6,)),
        ],
        compiler_params=params,
    )(
        me,
        in_hbm(sources),
        in_hbm(density.reshape(den_rows, cells // den_rows)),
        in_hbm(temp_bins.reshape(1, cells)),
        in_hbm(ray_index.reshape(1, cells)),
        in_hbm(rate_tables[0]),
        in_hbm(line_table),
    )
    got = [lax.ppermute(outgoing[k], "bin", plan.moves(k)) for k in plan.order()]
    other = pl.pallas_call(
        keep_kernel,
        out_shape=jax.ShapeDtypeStruct(arrived.shape, BF16),
        in_specs=[vmem],
        out_specs=vmem,
        compiler_params=params,
        cost_estimate=pl.CostEstimate(
            flops=OVERLAP_FLOPS, bytes_accessed=4 * arrived.size, transcendentals=0
        ),
    )(arrived)
    ray_rows = RAY_DEV
    rays = ray_rows * bin_total
    partial_sums = pl.pallas_call(
        functools.partial(level_kernel, plan, rays),
        out_shape=jax.ShapeDtypeStruct((rays, levels), BF16),
        in_specs=[vmem] * (plan.targets + 2),
        out_specs=vmem,
        compiler_params=params,
    )(*got, outgoing[0], own, other)
    held = lax.all_to_all(
        partial_sums.reshape(bin_total, ray_rows, levels),
        "bin",
        split_axis=0,
        concat_axis=0,
        tiled=True,
    )
    total = jnp.sum(held.astype(F32), axis=0)
    theirs = jnp.zeros_like(total)
    step = 1
    while step < wave_total:
        total = total + theirs if step > 1 else total
        theirs = lax.ppermute(total, "wave", [(i, i ^ step) for i in range(wave_total)])
        step *= 2
    return pl.pallas_call(
        line_kernel,
        out_shape=jax.ShapeDtypeStruct((ray_rows, line_table.shape[1]), F32),
        in_specs=[vmem, vmem, vmem],
        out_specs=vmem,
        compiler_params=params,
    )(total, theirs, held_line)


def solution(mesh):
    in_specs = (
        P(("bin", "wave"), None),
        P(("bin", "wave")),
        P(("bin", "wave"), None),
        P(("bin", "wave")),
        P("bin", None, None),
        P(None, "wave"),
    )
    return jax.shard_map(
        per_device, mesh=mesh, in_specs=in_specs, out_specs=P("bin", "wave"), check_vma=False
    )
```

```python
import functools

import jax
import jax.numpy as jnp
from jax import lax
from jax.experimental import pallas as pl
from jax.experimental.pallas import tpu as pltpu
from jax.sharding import PartitionSpec as P

RAY_DEV = 16
META_ROWS = 16
RAY_BASE = 32
LANES = 128
PACK_GROUPS = 2
OVERLAP_FLOPS = 10**10
VMEM_LIMIT = 32 * 1024 * 1024
F32 = jnp.float32
BF16 = jnp.bfloat16
I32 = jnp.int32


def nt_dot(a, b):
    return lax.dot_general(a, b, (((1,), (1,)), ((), ())), preferred_element_type=F32)


def iota(shape, dim):
    return lax.broadcasted_iota(I32, shape, dim)


def load_kernel(plan, me_ref, *refs):
    hbm_refs, vmem_refs, out_hbm = refs[:5], refs[5:10], refs[10]
    held, in_sems, out_sems = refs[11:]
    copies = [
        pltpu.make_async_copy(a, b, in_sems.at[i])
        for i, (a, b) in enumerate(zip(hbm_refs, vmem_refs))
    ]
    for copy in copies:
        copy.start()
    for copy in copies:
        copy.wait()

    @pl.when(me_ref[0] < plan.targets)
    def _():
        pack(plan, 0, *vmem_refs[:4], out_hbm, held, out_sems)


def pack_kernel(plan, me_ref, src_ref, den_ref, bin_ref, ray_ref, _, out_hbm, held, out_sems):
    @pl.when(me_ref[0] >= plan.targets)
    def _():
        pack(plan, 1, src_ref, den_ref, bin_ref, ray_ref, out_hbm, held, out_sems)


def pack(plan, my_half, src_ref, den_ref, bin_ref, ray_ref, out_hbm, held, out_sems):
    targets, block = plan.targets, plan.block
    cells, levels = src_ref.shape
    earlier = (iota((cells, cells), 0) < iota((cells, cells), 1)).astype(F32).astype(BF16)
    held[:, block:, :] = jnp.zeros((targets, META_ROWS, levels), BF16)
    bins = bin_ref[...]
    hot = (iota((plan.bins, cells), 0) == bins).astype(F32)
    before = jnp.dot(hot.astype(BF16), earlier, preferred_element_type=F32)
    position = jnp.sum(hot * before, axis=0, keepdims=True).astype(I32)
    half = bins // targets
    slot = (bins - half * targets) * block + (half ^ my_half) * plan.capacity + position
    rays = ray_ref[...]
    ray_high = rays // RAY_BASE
    ray_low = rays - ray_high * RAY_BASE
    den = den_ref[...].astype(F32)
    den_row = jnp.concatenate([den[i : i + 1] for i in range(den.shape[0])], axis=1)
    meta = jnp.concatenate(
        [den_row, ray_high.astype(F32), ray_low.astype(F32), jnp.zeros((META_ROWS - 3, cells), F32)],
        axis=0,
    ).astype(BF16)
    place = (iota((targets * block, cells), 0) == slot).astype(F32).astype(BF16)
    moved = nt_dot(meta, place).astype(BF16)
    src = src_ref[...]
    leaving = []
    group = max(1, targets // PACK_GROUPS)
    for first in range(0, targets, group):
        last = first + group
        rows = jnp.dot(place[first * block : last * block], src, preferred_element_type=F32)
        held[first:last, :block, :] = rows.astype(BF16).reshape(group, block, levels)
        for t in range(first, last):
            held[t, block:, :block] = moved[:, t * block : (t + 1) * block]
        part = pl.ds(first, group)
        copy = pltpu.make_async_copy(held.at[part], out_hbm.at[part], out_sems.at[len(leaving)])
        copy.start()
        leaving.append(copy)
    for copy in leaving:
        copy.wait()


def keep_kernel(arrived_ref, line_hbm, other_ref, line_ref, sem):
    copy = pltpu.make_async_copy(line_hbm, line_ref, sem)
    copy.start()
    other_ref[...] = arrived_ref[...]
    copy.wait()


def level_kernel(plan, rays, got_ref, *refs):
    table_refs, out_ref = refs[:-1], refs[-1]
    targets, block = plan.targets, plan.block
    meta = [got_ref[s, block:, :block].astype(F32) for s in range(targets)]
    columns = [jnp.transpose(m[:8]) for m in meta]
    total = jnp.zeros(out_ref.shape, F32)
    for part, table_ref in enumerate(table_refs):
        low, high = part * plan.capacity, (part + 1) * plan.capacity
        src = got_ref[:, low:high, :].reshape(targets * plan.capacity, got_ref.shape[2])
        den = jnp.concatenate([c[low:high, 0:1] for c in columns], axis=0)
        ray = jnp.concatenate(
            [m[1:2, low:high] * RAY_BASE + m[2:3, low:high] for m in meta], axis=1
        ).astype(I32)
        wide = src.astype(F32)
        table = table_ref[...]
        first = (den * jnp.dot(src, table, preferred_element_type=F32) + wide).astype(BF16)
        pops = (den * jnp.dot(first, table, preferred_element_type=F32) + wide).astype(BF16)
        pick = (iota((rays, src.shape[0]), 0) == ray).astype(F32).astype(BF16)
        total = total + jnp.dot(pick, pops, preferred_element_type=F32)
    out_ref[...] = total.astype(BF16)


def line_kernel(mine_ref, theirs_ref, line_ref, out_ref):
    sums = mine_ref[...] + theirs_ref[...]
    rows = sums.shape[0]
    high = sums.astype(BF16)
    low = (sums - high.astype(F32)).astype(BF16)
    both = jnp.concatenate([high, low], axis=0)
    got = jnp.dot(both, line_ref[...], preferred_element_type=F32)
    out_ref[...] = got[:rows] + got[rows:]


class Plan:
    def __init__(self, bin_total, cells):
        self.bins = bin_total
        self.targets = bin_total // 2
        self.capacity = max(2, 2 * cells // bin_total)
        self.block = 2 * self.capacity

    def table_moves(self):
        return [(i, (i + self.targets) % self.bins) for i in range(self.bins)]

    def halves(self):
        return [list(range(self.targets)), list(range(self.targets, self.bins))]


def per_device(sources, density, temp_bins, ray_index, rate_tables, line_table):
    cells, levels = sources.shape
    bin_total = lax.axis_size("bin")
    wave_total = lax.axis_size("wave")
    plan = Plan(bin_total, cells)
    rows = plan.block + META_ROWS
    params = pltpu.CompilerParams(vmem_limit_bytes=VMEM_LIMIT)
    vmem = pl.BlockSpec(memory_space=pltpu.VMEM)
    smem = pl.BlockSpec(memory_space=pltpu.SMEM)
    hbm = pl.BlockSpec(memory_space=pltpu.HBM)

    def in_hbm(x):
        return pltpu.with_memory_space_constraint(x, pltpu.HBM)

    me = lax.axis_index("bin").astype(I32).reshape(1)
    den_rows = cells // min(cells, LANES)
    inputs = [
        in_hbm(x)
        for x in (
            sources,
            density.reshape(den_rows, cells // den_rows),
            temp_bins.reshape(1, cells),
            ray_index.reshape(1, cells),
            rate_tables[0],
        )
    ]
    blocks = jax.ShapeDtypeStruct((plan.targets, rows, levels), BF16)
    scratch = [
        pltpu.VMEM(blocks.shape, BF16),
        pltpu.SemaphoreType.DMA((len(inputs),)),
        pltpu.SemaphoreType.DMA((PACK_GROUPS,)),
    ]
    *loaded, own, outgoing = pl.pallas_call(
        functools.partial(load_kernel, plan),
        out_shape=[jax.ShapeDtypeStruct(x.shape, x.dtype) for x in inputs] + [blocks],
        in_specs=[smem] + [hbm] * len(inputs),
        out_specs=[vmem] * len(inputs) + [hbm],
        scratch_shapes=scratch,
        compiler_params=params,
    )(me, *inputs)
    arrived = lax.ppermute(own, "bin", plan.table_moves())
    outgoing = pl.pallas_call(
        functools.partial(pack_kernel, plan),
        out_shape=blocks,
        in_specs=[smem] + [vmem] * len(loaded) + [hbm],
        out_specs=hbm,
        input_output_aliases={1 + len(loaded): 0},
        scratch_shapes=[scratch[0], scratch[2]],
        compiler_params=params,
    )(me, *loaded, outgoing)
    got = lax.all_to_all(
        outgoing, "bin", split_axis=0, concat_axis=0, tiled=True, axis_index_groups=plan.halves()
    )
    other, held_line = pl.pallas_call(
        keep_kernel,
        out_shape=[jax.ShapeDtypeStruct(a, BF16) for a in (arrived.shape, line_table.shape)],
        in_specs=[vmem, hbm],
        out_specs=[vmem] * 2,
        scratch_shapes=[pltpu.SemaphoreType.DMA],
        compiler_params=params,
        cost_estimate=pl.CostEstimate(
            flops=OVERLAP_FLOPS, bytes_accessed=4 * arrived.size, transcendentals=0
        ),
    )(arrived, in_hbm(line_table))
    ray_rows = RAY_DEV
    rays = ray_rows * bin_total
    partial_sums = pl.pallas_call(
        functools.partial(level_kernel, plan, rays),
        out_shape=jax.ShapeDtypeStruct((rays, levels), BF16),
        in_specs=[vmem] * 3,
        out_specs=vmem,
        compiler_params=params,
    )(got, own, other)
    held = lax.all_to_all(
        partial_sums.reshape(bin_total, ray_rows, levels),
        "bin",
        split_axis=0,
        concat_axis=0,
        tiled=True,
    )
    total = jnp.sum(held.astype(F32), axis=0)
    theirs = jnp.zeros_like(total)
    step = 1
    while step < wave_total:
        total = total + theirs if step > 1 else total
        theirs = lax.ppermute(total, "wave", [(i, i ^ step) for i in range(wave_total)])
        step *= 2
    return pl.pallas_call(
        line_kernel,
        out_shape=jax.ShapeDtypeStruct((ray_rows, line_table.shape[1]), F32),
        in_specs=[vmem, vmem, vmem],
        out_specs=vmem,
        compiler_params=params,
    )(total, theirs, held_line)


def solution(mesh):
    in_specs = (
        P(("bin", "wave"), None),
        P(("bin", "wave")),
        P(("bin", "wave"), None),
        P(("bin", "wave")),
        P("bin", None, None),
        P(None, "wave"),
    )
    return jax.shard_map(
        per_device, mesh=mesh, in_specs=in_specs, out_specs=P("bin", "wave"), check_vma=False
    )
```

```python
import functools

import jax
import jax.numpy as jnp
from jax import lax
from jax.experimental import pallas as pl
from jax.experimental.pallas import tpu as pltpu
from jax.sharding import PartitionSpec as P

RAY_DEV = 16
META_ROWS = 16
RAY_BASE = 32
LANES = 128
OVERLAP_FLOPS = 10**10
VMEM_LIMIT = 32 * 1024 * 1024
F32 = jnp.float32
BF16 = jnp.bfloat16
I32 = jnp.int32


def nt_dot(a, b):
    return lax.dot_general(a, b, (((1,), (1,)), ((), ())), preferred_element_type=F32)


def iota(shape, dim):
    return lax.broadcasted_iota(I32, shape, dim)


def pack_kernel(plan, me_ref, src_hbm, den_hbm, bin_hbm, ray_hbm, table_hbm, line_hbm, *rest):
    targets, block = plan.targets, plan.block
    outs, table_out, line_out = rest[:targets], rest[targets], rest[targets + 1]
    src_ref, den_ref, bin_ref, ray_ref, sems = rest[targets + 2 :]
    copies = [
        pltpu.make_async_copy(a, b, sems.at[i])
        for i, (a, b) in enumerate(
            (
                (bin_hbm, bin_ref),
                (ray_hbm, ray_ref),
                (den_hbm, den_ref),
                (src_hbm, src_ref),
                (table_hbm, table_out),
                (line_hbm, line_out),
            )
        )
    ]
    for copy in copies:
        copy.start()
    cells, levels = src_ref.shape
    earlier = (iota((cells, cells), 0) < iota((cells, cells), 1)).astype(F32).astype(BF16)
    for copy in copies[:3]:
        copy.wait()
    bins = bin_ref[...]
    hot = (iota((plan.bins, cells), 0) == bins).astype(F32)
    before = jnp.dot(hot.astype(BF16), earlier, preferred_element_type=F32)
    position = jnp.sum(hot * before, axis=0, keepdims=True).astype(I32)
    turn = bins ^ me_ref[0]
    half = turn // targets
    slot = (turn - half * targets) * block + half * plan.capacity + position
    rays = ray_ref[...]
    ray_high = rays // RAY_BASE
    ray_low = rays - ray_high * RAY_BASE
    den = den_ref[...].astype(F32)
    den_row = jnp.concatenate([den[i : i + 1] for i in range(den.shape[0])], axis=1)
    meta = jnp.concatenate(
        [den_row, ray_high.astype(F32), ray_low.astype(F32), jnp.zeros((META_ROWS - 3, cells), F32)],
        axis=0,
    ).astype(BF16)
    place = (iota((targets * block, cells), 0) == slot).astype(F32).astype(BF16)
    moved = nt_dot(meta, place).astype(BF16)
    copies[3].wait()
    rows = jnp.dot(place, src_ref[...], preferred_element_type=F32).astype(BF16)
    for t in range(targets):
        first, last = t * block, (t + 1) * block
        outs[t][:block, :] = rows[first:last]
        outs[t][block:, :] = jnp.zeros((META_ROWS, levels), BF16)
        outs[t][block:, :block] = moved[:, first:last]
    for copy in copies[4:]:
        copy.wait()


def keep_kernel(table_ref, out_ref):
    out_ref[...] = table_ref[...]


def level_kernel(plan, rays, *refs):
    got, table_refs, out_ref = refs[: plan.targets], refs[plan.targets : -1], refs[-1]
    block = plan.block
    meta = [g[block:, :block].astype(F32) for g in got]
    columns = [jnp.transpose(m[:8]) for m in meta]
    total = jnp.zeros(out_ref.shape, F32)
    for part, table_ref in enumerate(table_refs):
        low, high = part * plan.capacity, (part + 1) * plan.capacity
        src = jnp.concatenate([g[low:high, :] for g in got], axis=0)
        den = jnp.concatenate([c[low:high, 0:1] for c in columns], axis=0)
        ray = jnp.concatenate(
            [m[1:2, low:high] * RAY_BASE + m[2:3, low:high] for m in meta], axis=1
        ).astype(I32)
        wide = src.astype(F32)
        table = table_ref[...]
        first = (den * jnp.dot(src, table, preferred_element_type=F32) + wide).astype(BF16)
        pops = (den * jnp.dot(first, table, preferred_element_type=F32) + wide).astype(BF16)
        pick = (iota((rays, src.shape[0]), 0) == ray).astype(F32).astype(BF16)
        total = total + jnp.dot(pick, pops, preferred_element_type=F32)
    out_ref[...] = total.astype(BF16)


def line_kernel(mine_ref, theirs_ref, line_ref, out_ref):
    sums = mine_ref[...] + theirs_ref[...]
    rows = sums.shape[0]
    high = sums.astype(BF16)
    low = (sums - high.astype(F32)).astype(BF16)
    both = jnp.concatenate([high, low], axis=0)
    got = jnp.dot(both, line_ref[...], preferred_element_type=F32)
    out_ref[...] = got[:rows] + got[rows:]


class Plan:
    def __init__(self, bin_total, cells):
        self.bins = bin_total
        self.targets = bin_total // 2
        self.capacity = max(2, 2 * cells // bin_total)
        self.block = 2 * self.capacity

    def table_moves(self):
        return [(i, (i + self.targets) % self.bins) for i in range(self.bins)]

    def order(self):
        return sorted(range(1, self.targets), key=lambda k: bin(k).count("1"))

    def moves(self, k):
        return [(i, i ^ k) for i in range(self.bins)]


def per_device(sources, density, temp_bins, ray_index, rate_tables, line_table):
    cells, levels = sources.shape
    bin_total = lax.axis_size("bin")
    wave_total = lax.axis_size("wave")
    plan = Plan(bin_total, cells)
    rows = plan.block + META_ROWS
    params = pltpu.CompilerParams(vmem_limit_bytes=VMEM_LIMIT)
    vmem = pl.BlockSpec(memory_space=pltpu.VMEM)
    smem = pl.BlockSpec(memory_space=pltpu.SMEM)
    hbm = pl.BlockSpec(memory_space=pltpu.HBM)

    def in_hbm(x):
        return pltpu.with_memory_space_constraint(x, pltpu.HBM)

    arrived = lax.ppermute(rate_tables[0], "bin", plan.table_moves())
    me = lax.axis_index("bin").astype(I32).reshape(1)
    den_rows = cells // min(cells, LANES)
    *outgoing, own, held_line = pl.pallas_call(
        functools.partial(pack_kernel, plan),
        out_shape=[
            jax.ShapeDtypeStruct(a, BF16)
            for a in [(rows, levels)] * plan.targets + [rate_tables.shape[1:], line_table.shape]
        ],
        in_specs=[smem] + [hbm] * 6,
        out_specs=[vmem] * (plan.targets + 2),
        scratch_shapes=[
            pltpu.VMEM((cells, levels), BF16),
            pltpu.VMEM((den_rows, cells // den_rows), BF16),
            pltpu.VMEM((1, cells), I32),
            pltpu.VMEM((1, cells), I32),
            pltpu.SemaphoreType.DMA((6,)),
        ],
        compiler_params=params,
    )(
        me,
        in_hbm(sources),
        in_hbm(density.reshape(den_rows, cells // den_rows)),
        in_hbm(temp_bins.reshape(1, cells)),
        in_hbm(ray_index.reshape(1, cells)),
        in_hbm(rate_tables[0]),
        in_hbm(line_table),
    )
    got = [lax.ppermute(outgoing[k], "bin", plan.moves(k)) for k in plan.order()]
    other = pl.pallas_call(
        keep_kernel,
        out_shape=jax.ShapeDtypeStruct(arrived.shape, BF16),
        in_specs=[vmem],
        out_specs=vmem,
        compiler_params=params,
        cost_estimate=pl.CostEstimate(
            flops=OVERLAP_FLOPS, bytes_accessed=4 * arrived.size, transcendentals=0
        ),
    )(arrived)
    ray_rows = RAY_DEV
    rays = ray_rows * bin_total
    partial_sums = pl.pallas_call(
        functools.partial(level_kernel, plan, rays),
        out_shape=jax.ShapeDtypeStruct((rays, levels), BF16),
        in_specs=[vmem] * (plan.targets + 2),
        out_specs=vmem,
        compiler_params=params,
    )(*got, outgoing[0], own, other)
    held = lax.all_to_all(
        partial_sums.reshape(bin_total, ray_rows, levels),
        "bin",
        split_axis=0,
        concat_axis=0,
        tiled=True,
    )
    total = jnp.sum(held.astype(F32), axis=0)
    theirs = jnp.zeros_like(total)
    step = 1
    while step < wave_total:
        total = total + theirs if step > 1 else total
        theirs = lax.ppermute(total, "wave", [(i, i ^ step) for i in range(wave_total)])
        step *= 2
    return pl.pallas_call(
        line_kernel,
        out_shape=jax.ShapeDtypeStruct((ray_rows, line_table.shape[1]), F32),
        in_specs=[vmem, vmem, vmem],
        out_specs=vmem,
        compiler_params=params,
    )(total, theirs, held_line)


def solution(mesh):
    in_specs = (
        P(("bin", "wave"), None),
        P(("bin", "wave")),
        P(("bin", "wave"), None),
        P(("bin", "wave")),
        P("bin", None, None),
        P(None, "wave"),
    )
    return jax.shard_map(
        per_device, mesh=mesh, in_specs=in_specs, out_specs=P("bin", "wave"), check_vma=False
    )
```

```python
import functools

import jax
import jax.numpy as jnp
from jax import lax
from jax.experimental import pallas as pl
from jax.experimental.pallas import tpu as pltpu
from jax.sharding import PartitionSpec as P

RAY_DEV = 16
META_ROWS = 16
RAY_BASE = 32
LANES = 128
OVERLAP_FLOPS = 10**10
VMEM_LIMIT = 32 * 1024 * 1024
F32 = jnp.float32
BF16 = jnp.bfloat16
I32 = jnp.int32


def nt_dot(a, b):
    return lax.dot_general(a, b, (((1,), (1,)), ((), ())), preferred_element_type=F32)


def iota(shape, dim):
    return lax.broadcasted_iota(I32, shape, dim)


def pack_kernel(plan, me_ref, src_hbm, den_hbm, bin_hbm, ray_hbm, table_hbm, line_hbm, *rest):
    targets, block = plan.targets, plan.block
    outs, table_out, line_out = rest[:targets], rest[targets], rest[targets + 1]
    src_ref, den_ref, bin_ref, ray_ref, sems = rest[targets + 2 :]
    copies = [
        pltpu.make_async_copy(a, b, sems.at[i])
        for i, (a, b) in enumerate(
            (
                (bin_hbm, bin_ref),
                (ray_hbm, ray_ref),
                (den_hbm, den_ref),
                (src_hbm, src_ref),
                (table_hbm, table_out),
                (line_hbm, line_out),
            )
        )
    ]
    for copy in copies:
        copy.start()
    cells, levels = src_ref.shape
    earlier = (iota((cells, cells), 0) < iota((cells, cells), 1)).astype(F32).astype(BF16)
    for copy in copies[:3]:
        copy.wait()
    bins = bin_ref[...]
    hot = (iota((plan.bins, cells), 0) == bins).astype(F32)
    before = jnp.dot(hot.astype(BF16), earlier, preferred_element_type=F32)
    position = jnp.sum(hot * before, axis=0, keepdims=True).astype(I32)
    turn = bins ^ me_ref[0]
    half = turn // targets
    slot = (turn - half * targets) * block + half * plan.capacity + position
    rays = ray_ref[...]
    ray_high = rays // RAY_BASE
    ray_low = rays - ray_high * RAY_BASE
    den = den_ref[...].astype(F32)
    den_row = jnp.concatenate([den[i : i + 1] for i in range(den.shape[0])], axis=1)
    meta = jnp.concatenate(
        [den_row, ray_high.astype(F32), ray_low.astype(F32), jnp.zeros((META_ROWS - 3, cells), F32)],
        axis=0,
    ).astype(BF16)
    place = (iota((targets * block, cells), 0) == slot).astype(F32).astype(BF16)
    moved = nt_dot(meta, place).astype(BF16)
    copies[3].wait()
    rows = jnp.dot(place, src_ref[...], preferred_element_type=F32).astype(BF16)
    for t in range(targets):
        first, last = t * block, (t + 1) * block
        outs[t][:block, :] = rows[first:last]
        outs[t][block:, :] = jnp.zeros((META_ROWS, levels), BF16)
        outs[t][block:, :block] = moved[:, first:last]
    for copy in copies[4:]:
        copy.wait()


def keep_kernel(table_ref, *refs):
    out_ref = refs[-1]
    out_ref[...] = table_ref[...]


def level_kernel(plan, rays, *refs):
    got, table_refs, out_ref = refs[: plan.targets], refs[plan.targets : -1], refs[-1]
    block = plan.block
    meta = [g[block:, :block].astype(F32) for g in got]
    columns = [jnp.transpose(m[:8]) for m in meta]
    total = jnp.zeros(out_ref.shape, F32)
    for part, table_ref in enumerate(table_refs):
        low, high = part * plan.capacity, (part + 1) * plan.capacity
        src = jnp.concatenate([g[low:high, :] for g in got], axis=0)
        den = jnp.concatenate([c[low:high, 0:1] for c in columns], axis=0)
        ray = jnp.concatenate(
            [m[1:2, low:high] * RAY_BASE + m[2:3, low:high] for m in meta], axis=1
        ).astype(I32)
        wide = src.astype(F32)
        table = table_ref[...]
        first = (den * jnp.dot(src, table, preferred_element_type=F32) + wide).astype(BF16)
        pops = (den * jnp.dot(first, table, preferred_element_type=F32) + wide).astype(BF16)
        pick = (iota((rays, src.shape[0]), 0) == ray).astype(F32).astype(BF16)
        total = total + jnp.dot(pick, pops, preferred_element_type=F32)
    out_ref[...] = total.astype(BF16)


def line_kernel(mine_ref, theirs_ref, line_ref, out_ref):
    sums = mine_ref[...] + theirs_ref[...]
    rows = sums.shape[0]
    high = sums.astype(BF16)
    low = (sums - high.astype(F32)).astype(BF16)
    both = jnp.concatenate([high, low], axis=0)
    got = jnp.dot(both, line_ref[...], preferred_element_type=F32)
    out_ref[...] = got[:rows] + got[rows:]


class Plan:
    def __init__(self, bin_total, cells):
        self.bins = bin_total
        self.targets = bin_total // 2
        self.capacity = max(2, 2 * cells // bin_total)
        self.block = 2 * self.capacity

    def table_moves(self):
        return [(i, (i + self.targets) % self.bins) for i in range(self.bins)]

    def order(self):
        near = [k for k in range(1, self.targets) if k & (k - 1) == 0]
        far = [k for k in range(1, self.targets) if k & (k - 1)]
        return near + sorted(far, key=lambda k: (k != self.targets - 1, k))

    def moves(self, k):
        return [(i, i ^ k) for i in range(self.bins)]


def per_device(sources, density, temp_bins, ray_index, rate_tables, line_table):
    cells, levels = sources.shape
    bin_total = lax.axis_size("bin")
    wave_total = lax.axis_size("wave")
    plan = Plan(bin_total, cells)
    rows = plan.block + META_ROWS
    params = pltpu.CompilerParams(vmem_limit_bytes=VMEM_LIMIT)
    vmem = pl.BlockSpec(memory_space=pltpu.VMEM)
    smem = pl.BlockSpec(memory_space=pltpu.SMEM)
    hbm = pl.BlockSpec(memory_space=pltpu.HBM)

    def in_hbm(x):
        return pltpu.with_memory_space_constraint(x, pltpu.HBM)

    arrived = lax.ppermute(rate_tables[0], "bin", plan.table_moves())
    me = lax.axis_index("bin").astype(I32).reshape(1)
    den_rows = cells // min(cells, LANES)
    *outgoing, own, held_line = pl.pallas_call(
        functools.partial(pack_kernel, plan),
        out_shape=[
            jax.ShapeDtypeStruct(a, BF16)
            for a in [(rows, levels)] * plan.targets + [rate_tables.shape[1:], line_table.shape]
        ],
        in_specs=[smem] + [hbm] * 6,
        out_specs=[vmem] * (plan.targets + 2),
        scratch_shapes=[
            pltpu.VMEM((cells, levels), BF16),
            pltpu.VMEM((den_rows, cells // den_rows), BF16),
            pltpu.VMEM((1, cells), I32),
            pltpu.VMEM((1, cells), I32),
            pltpu.SemaphoreType.DMA((6,)),
        ],
        compiler_params=params,
    )(
        me,
        in_hbm(sources),
        in_hbm(density.reshape(den_rows, cells // den_rows)),
        in_hbm(temp_bins.reshape(1, cells)),
        in_hbm(ray_index.reshape(1, cells)),
        in_hbm(rate_tables[0]),
        in_hbm(line_table),
    )
    got = [lax.ppermute(outgoing[k], "bin", plan.moves(k)) for k in plan.order()]
    nearest = got[: plan.targets.bit_length() - 1]
    other = pl.pallas_call(
        keep_kernel,
        out_shape=jax.ShapeDtypeStruct(arrived.shape, BF16),
        in_specs=[vmem] * (1 + len(nearest)),
        out_specs=vmem,
        compiler_params=params,
        cost_estimate=pl.CostEstimate(
            flops=OVERLAP_FLOPS, bytes_accessed=4 * arrived.size, transcendentals=0
        ),
    )(arrived, *nearest)
    ray_rows = RAY_DEV
    rays = ray_rows * bin_total
    partial_sums = pl.pallas_call(
        functools.partial(level_kernel, plan, rays),
        out_shape=jax.ShapeDtypeStruct((rays, levels), BF16),
        in_specs=[vmem] * (plan.targets + 2),
        out_specs=vmem,
        compiler_params=params,
    )(*got, outgoing[0], own, other)
    held = lax.all_to_all(
        partial_sums.reshape(bin_total, ray_rows, levels),
        "bin",
        split_axis=0,
        concat_axis=0,
        tiled=True,
    )
    total = jnp.sum(held.astype(F32), axis=0)
    theirs = jnp.zeros_like(total)
    step = 1
    while step < wave_total:
        total = total + theirs if step > 1 else total
        theirs = lax.ppermute(total, "wave", [(i, i ^ step) for i in range(wave_total)])
        step *= 2
    return pl.pallas_call(
        line_kernel,
        out_shape=jax.ShapeDtypeStruct((ray_rows, line_table.shape[1]), F32),
        in_specs=[vmem, vmem, vmem],
        out_specs=vmem,
        compiler_params=params,
    )(total, theirs, held_line)


def solution(mesh):
    in_specs = (
        P(("bin", "wave"), None),
        P(("bin", "wave")),
        P(("bin", "wave"), None),
        P(("bin", "wave")),
        P("bin", None, None),
        P(None, "wave"),
    )
    return jax.shard_map(
        per_device, mesh=mesh, in_specs=in_specs, out_specs=P("bin", "wave"), check_vma=False
    )
```

```python
import functools

import jax
import jax.numpy as jnp
from jax import lax
from jax.experimental import pallas as pl
from jax.experimental.pallas import tpu as pltpu
from jax.sharding import PartitionSpec as P

RAY_DEV = 16
META_ROWS = 16
RAY_BASE = 32
LANES = 128
OVERLAP_FLOPS = 10**10
VMEM_LIMIT = 32 * 1024 * 1024
F32 = jnp.float32
BF16 = jnp.bfloat16
I32 = jnp.int32


def nt_dot(a, b):
    return lax.dot_general(a, b, (((1,), (1,)), ((), ())), preferred_element_type=F32)


def iota(shape, dim):
    return lax.broadcasted_iota(I32, shape, dim)


def pack_kernel(plan, me_ref, src_hbm, den_hbm, bin_hbm, ray_hbm, table_hbm, line_hbm, *rest):
    targets, block = plan.targets, plan.block
    out, table_out, line_out, src_ref, den_ref, bin_ref, ray_ref, sems = rest
    copies = [
        pltpu.make_async_copy(a, b, sems.at[i])
        for i, (a, b) in enumerate(
            (
                (bin_hbm, bin_ref),
                (ray_hbm, ray_ref),
                (den_hbm, den_ref),
                (src_hbm, src_ref),
                (table_hbm, table_out),
                (line_hbm, line_out),
            )
        )
    ]
    for copy in copies:
        copy.start()
    cells, levels = src_ref.shape
    earlier = (iota((cells, cells), 0) < iota((cells, cells), 1)).astype(F32).astype(BF16)
    my_half = me_ref[0] // targets
    for copy in copies[:3]:
        copy.wait()
    bins = bin_ref[...]
    hot = (iota((plan.bins, cells), 0) == bins).astype(F32)
    before = jnp.dot(hot.astype(BF16), earlier, preferred_element_type=F32)
    position = jnp.sum(hot * before, axis=0, keepdims=True).astype(I32)
    half = bins // targets
    slot = (bins - half * targets) * block + (half ^ my_half) * plan.capacity + position
    rays = ray_ref[...]
    ray_high = rays // RAY_BASE
    ray_low = rays - ray_high * RAY_BASE
    den = den_ref[...].astype(F32)
    den_row = jnp.concatenate([den[i : i + 1] for i in range(den.shape[0])], axis=1)
    meta = jnp.concatenate(
        [den_row, ray_high.astype(F32), ray_low.astype(F32), jnp.zeros((META_ROWS - 3, cells), F32)],
        axis=0,
    ).astype(BF16)
    place = (iota((targets * block, cells), 0) == slot).astype(F32).astype(BF16)
    moved = nt_dot(meta, place).astype(BF16)
    copies[3].wait()
    rows = jnp.dot(place, src_ref[...], preferred_element_type=F32).astype(BF16)
    out[:, :block, :] = rows.reshape(targets, block, levels)
    out[:, block:, :] = jnp.zeros((targets, META_ROWS, levels), BF16)
    for t in range(targets):
        out[t, block:, :block] = moved[:, t * block : (t + 1) * block]
    for copy in copies[4:]:
        copy.wait()


def keep_kernel(core_ref, arrived_ref, passed_ref, out_ref):
    out_ref[...] = jnp.where(core_ref[0] % 2 == 1, arrived_ref[...], passed_ref[...])


def level_kernel(plan, rays, got_ref, *refs):
    table_refs, out_ref = refs[:-1], refs[-1]
    targets, block = plan.targets, plan.block
    meta = [got_ref[s, block:, :block].astype(F32) for s in range(targets)]
    columns = [jnp.transpose(m[:8]) for m in meta]
    total = jnp.zeros(out_ref.shape, F32)
    for part, table_ref in enumerate(table_refs):
        low, high = part * plan.capacity, (part + 1) * plan.capacity
        src = got_ref[:, low:high, :].reshape(targets * plan.capacity, got_ref.shape[2])
        den = jnp.concatenate([c[low:high, 0:1] for c in columns], axis=0)
        ray = jnp.concatenate(
            [m[1:2, low:high] * RAY_BASE + m[2:3, low:high] for m in meta], axis=1
        ).astype(I32)
        wide = src.astype(F32)
        table = table_ref[...]
        first = (den * jnp.dot(src, table, preferred_element_type=F32) + wide).astype(BF16)
        pops = (den * jnp.dot(first, table, preferred_element_type=F32) + wide).astype(BF16)
        pick = (iota((rays, src.shape[0]), 0) == ray).astype(F32).astype(BF16)
        total = total + jnp.dot(pick, pops, preferred_element_type=F32)
    out_ref[...] = total.astype(BF16)


def line_kernel(mine_ref, theirs_ref, line_ref, out_ref):
    sums = mine_ref[...] + theirs_ref[...]
    rows = sums.shape[0]
    high = sums.astype(BF16)
    low = (sums - high.astype(F32)).astype(BF16)
    both = jnp.concatenate([high, low], axis=0)
    got = jnp.dot(both, line_ref[...], preferred_element_type=F32)
    out_ref[...] = got[:rows] + got[rows:]


class Plan:
    def __init__(self, bin_total, cells):
        self.bins = bin_total
        self.targets = bin_total // 2
        self.capacity = max(2, 2 * cells // bin_total)
        self.block = 2 * self.capacity

    def table_moves(self, wave_total):
        moves = []
        for b in range(self.bins):
            for w in range(wave_total):
                to = (b + self.targets) % self.bins if w % 2 else b ^ 1
                moves.append((b * wave_total + w, to * wave_total + w))
        return moves

    def halves(self):
        return [list(range(self.targets)), list(range(self.targets, self.bins))]


def per_device(sources, density, temp_bins, ray_index, rate_tables, line_table):
    cells, levels = sources.shape
    bin_total = lax.axis_size("bin")
    wave_total = lax.axis_size("wave")
    plan = Plan(bin_total, cells)
    rows = plan.block + META_ROWS
    params = pltpu.CompilerParams(vmem_limit_bytes=VMEM_LIMIT)
    vmem = pl.BlockSpec(memory_space=pltpu.VMEM)
    smem = pl.BlockSpec(memory_space=pltpu.SMEM)
    hbm = pl.BlockSpec(memory_space=pltpu.HBM)

    def in_hbm(x):
        return pltpu.with_memory_space_constraint(x, pltpu.HBM)

    arrived = lax.ppermute(rate_tables[0], ("bin", "wave"), plan.table_moves(wave_total))
    passed = lax.ppermute(arrived, "wave", [(i, i ^ 1) for i in range(wave_total)])
    me = lax.axis_index("bin").astype(I32).reshape(1)
    den_rows = cells // min(cells, LANES)
    outgoing, own, held_line = pl.pallas_call(
        functools.partial(pack_kernel, plan),
        out_shape=[
            jax.ShapeDtypeStruct(a, BF16)
            for a in ((plan.targets, rows, levels), rate_tables.shape[1:], line_table.shape)
        ],
        in_specs=[smem] + [hbm] * 6,
        out_specs=[vmem] * 3,
        scratch_shapes=[
            pltpu.VMEM((cells, levels), BF16),
            pltpu.VMEM((den_rows, cells // den_rows), BF16),
            pltpu.VMEM((1, cells), I32),
            pltpu.VMEM((1, cells), I32),
            pltpu.SemaphoreType.DMA((6,)),
        ],
        compiler_params=params,
    )(
        me,
        in_hbm(sources),
        in_hbm(density.reshape(den_rows, cells // den_rows)),
        in_hbm(temp_bins.reshape(1, cells)),
        in_hbm(ray_index.reshape(1, cells)),
        in_hbm(rate_tables[0]),
        in_hbm(line_table),
    )
    got = lax.all_to_all(
        outgoing, "bin", split_axis=0, concat_axis=0, tiled=True, axis_index_groups=plan.halves()
    )
    other = pl.pallas_call(
        keep_kernel,
        out_shape=jax.ShapeDtypeStruct(arrived.shape, BF16),
        in_specs=[smem, vmem, vmem],
        out_specs=vmem,
        compiler_params=params,
        cost_estimate=pl.CostEstimate(
            flops=OVERLAP_FLOPS, bytes_accessed=4 * arrived.size, transcendentals=0
        ),
    )(lax.axis_index("wave").astype(I32).reshape(1), arrived, passed)
    ray_rows = RAY_DEV
    rays = ray_rows * bin_total
    partial_sums = pl.pallas_call(
        functools.partial(level_kernel, plan, rays),
        out_shape=jax.ShapeDtypeStruct((rays, levels), BF16),
        in_specs=[vmem] * 3,
        out_specs=vmem,
        compiler_params=params,
    )(got, own, other)
    held = lax.all_to_all(
        partial_sums.reshape(bin_total, ray_rows, levels),
        "bin",
        split_axis=0,
        concat_axis=0,
        tiled=True,
    )
    total = jnp.sum(held.astype(F32), axis=0)
    theirs = jnp.zeros_like(total)
    step = 1
    while step < wave_total:
        total = total + theirs if step > 1 else total
        theirs = lax.ppermute(total, "wave", [(i, i ^ step) for i in range(wave_total)])
        step *= 2
    return pl.pallas_call(
        line_kernel,
        out_shape=jax.ShapeDtypeStruct((ray_rows, line_table.shape[1]), F32),
        in_specs=[vmem, vmem, vmem],
        out_specs=vmem,
        compiler_params=params,
    )(total, theirs, held_line)


def solution(mesh):
    in_specs = (
        P(("bin", "wave"), None),
        P(("bin", "wave")),
        P(("bin", "wave"), None),
        P(("bin", "wave")),
        P("bin", None, None),
        P(None, "wave"),
    )
    return jax.shard_map(
        per_device, mesh=mesh, in_specs=in_specs, out_specs=P("bin", "wave"), check_vma=False
    )
```

```python
import functools

import jax
import jax.numpy as jnp
from jax import lax
from jax.experimental import pallas as pl
from jax.experimental.pallas import tpu as pltpu
from jax.sharding import PartitionSpec as P

RAY_DEV = 16
META_ROWS = 16
RAY_BASE = 32
LANES = 128
VMEM_LIMIT = 32 * 1024 * 1024
F32 = jnp.float32
BF16 = jnp.bfloat16
I32 = jnp.int32


def nt_dot(a, b):
    return lax.dot_general(a, b, (((1,), (1,)), ((), ())), preferred_element_type=F32)


def iota(shape, dim):
    return lax.broadcasted_iota(I32, shape, dim)


def pack_kernel(plan, me_ref, src_hbm, den_hbm, bin_hbm, ray_hbm, table_hbm, line_hbm, *rest):
    targets, block = plan.targets, plan.block
    out, table_out, line_out, share_out, src_ref, den_ref, bin_ref, ray_ref, sems = rest
    share = share_out.shape[0]
    share_rows = pl.ds(pl.multiple_of(me_ref[0] % 2 * share, share), share)
    copies = [
        pltpu.make_async_copy(a, b, sems.at[i])
        for i, (a, b) in enumerate(
            (
                (bin_hbm, bin_ref),
                (ray_hbm, ray_ref),
                (den_hbm, den_ref),
                (src_hbm, src_ref),
                (table_hbm, table_out),
                (line_hbm, line_out),
                (table_hbm.at[share_rows], share_out),
            )
        )
    ]
    for copy in copies:
        copy.start()
    cells, levels = src_ref.shape
    earlier = (iota((cells, cells), 0) < iota((cells, cells), 1)).astype(F32).astype(BF16)
    my_half = me_ref[0] // (targets * plan.wave)
    for copy in copies[:3]:
        copy.wait()
    bins = bin_ref[...]
    hot = (iota((plan.bins, cells), 0) == bins).astype(F32)
    before = jnp.dot(hot.astype(BF16), earlier, preferred_element_type=F32)
    position = jnp.sum(hot * before, axis=0, keepdims=True).astype(I32)
    half = bins // targets
    slot = (bins - half * targets) * block + (half ^ my_half) * plan.capacity + position
    rays = ray_ref[...]
    ray_high = rays // RAY_BASE
    ray_low = rays - ray_high * RAY_BASE
    den = den_ref[...].astype(F32)
    den_row = jnp.concatenate([den[i : i + 1] for i in range(den.shape[0])], axis=1)
    meta = jnp.concatenate(
        [den_row, ray_high.astype(F32), ray_low.astype(F32), jnp.zeros((META_ROWS - 3, cells), F32)],
        axis=0,
    ).astype(BF16)
    place = (iota((targets * block, cells), 0) == slot).astype(F32).astype(BF16)
    moved = nt_dot(meta, place).astype(BF16)
    copies[3].wait()
    rows = jnp.dot(place, src_ref[...], preferred_element_type=F32).astype(BF16)
    out[:, :block, :] = rows.reshape(targets, block, levels)
    out[:, block:, :] = jnp.zeros((targets, META_ROWS, levels), BF16)
    for t in range(targets):
        out[t, block:, :block] = moved[:, t * block : (t + 1) * block]
    for copy in copies[4:]:
        copy.wait()


def level_kernel(plan, rays, me_ref, got_ref, own_ref, arrived_ref, passed_ref, out_ref):
    upper = me_ref[0] % 2 == 1
    arrived, passed = arrived_ref[...], passed_ref[...]
    other = jnp.concatenate(
        [jnp.where(upper, passed, arrived), jnp.where(upper, arrived, passed)], axis=0
    )
    targets, block = plan.targets, plan.block
    meta = [got_ref[s, block:, :block].astype(F32) for s in range(targets)]
    columns = [jnp.transpose(m[:8]) for m in meta]
    total = jnp.zeros(out_ref.shape, F32)
    for part, table in enumerate((own_ref[...], other)):
        low, high = part * plan.capacity, (part + 1) * plan.capacity
        src = got_ref[:, low:high, :].reshape(targets * plan.capacity, got_ref.shape[2])
        den = jnp.concatenate([c[low:high, 0:1] for c in columns], axis=0)
        ray = jnp.concatenate(
            [m[1:2, low:high] * RAY_BASE + m[2:3, low:high] for m in meta], axis=1
        ).astype(I32)
        wide = src.astype(F32)
        first = (den * jnp.dot(src, table, preferred_element_type=F32) + wide).astype(BF16)
        pops = (den * jnp.dot(first, table, preferred_element_type=F32) + wide).astype(BF16)
        pick = (iota((rays, src.shape[0]), 0) == ray).astype(F32).astype(BF16)
        total = total + jnp.dot(pick, pops, preferred_element_type=F32)
    out_ref[...] = total.astype(BF16)


def line_kernel(mine_ref, theirs_ref, line_ref, out_ref):
    sums = mine_ref[...] + theirs_ref[...]
    rows = sums.shape[0]
    high = sums.astype(BF16)
    low = (sums - high.astype(F32)).astype(BF16)
    both = jnp.concatenate([high, low], axis=0)
    got = jnp.dot(both, line_ref[...], preferred_element_type=F32)
    out_ref[...] = got[:rows] + got[rows:]


class Plan:
    def __init__(self, bin_total, wave_total, cells):
        self.bins = bin_total
        self.wave = wave_total
        self.targets = bin_total // 2
        self.capacity = max(2, 2 * cells // bin_total)
        self.block = 2 * self.capacity

    def table_moves(self):
        return [(i, (i + self.targets) % self.bins) for i in range(self.bins)]

    def halves(self):
        return [list(range(self.targets)), list(range(self.targets, self.bins))]


def per_device(sources, density, temp_bins, ray_index, rate_tables, line_table):
    cells, levels = sources.shape
    bin_total = lax.axis_size("bin")
    wave_total = lax.axis_size("wave")
    plan = Plan(bin_total, wave_total, cells)
    rows = plan.block + META_ROWS
    params = pltpu.CompilerParams(vmem_limit_bytes=VMEM_LIMIT)
    vmem = pl.BlockSpec(memory_space=pltpu.VMEM)
    smem = pl.BlockSpec(memory_space=pltpu.SMEM)
    hbm = pl.BlockSpec(memory_space=pltpu.HBM)

    def in_hbm(x):
        return pltpu.with_memory_space_constraint(x, pltpu.HBM)

    me = lax.axis_index(("bin", "wave")).astype(I32).reshape(1)
    share = (levels // 2, levels)
    den_rows = cells // min(cells, LANES)
    outgoing, own, held_line, own_share = pl.pallas_call(
        functools.partial(pack_kernel, plan),
        out_shape=[
            jax.ShapeDtypeStruct(a, BF16)
            for a in ((plan.targets, rows, levels), (levels, levels), line_table.shape, share)
        ],
        in_specs=[smem] + [hbm] * 6,
        out_specs=[vmem] * 4,
        scratch_shapes=[
            pltpu.VMEM((cells, levels), BF16),
            pltpu.VMEM((den_rows, cells // den_rows), BF16),
            pltpu.VMEM((1, cells), I32),
            pltpu.VMEM((1, cells), I32),
            pltpu.SemaphoreType.DMA((7,)),
        ],
        compiler_params=params,
    )(
        me,
        in_hbm(sources),
        in_hbm(density.reshape(den_rows, cells // den_rows)),
        in_hbm(temp_bins.reshape(1, cells)),
        in_hbm(ray_index.reshape(1, cells)),
        in_hbm(rate_tables[0]),
        in_hbm(line_table),
    )
    got = lax.all_to_all(
        outgoing, "bin", split_axis=0, concat_axis=0, tiled=True, axis_index_groups=plan.halves()
    )
    arrived = lax.ppermute(own_share, "bin", plan.table_moves())
    passed = lax.ppermute(arrived, "wave", [(i, i ^ 1) for i in range(wave_total)])
    ray_rows = RAY_DEV
    rays = ray_rows * bin_total
    partial_sums = pl.pallas_call(
        functools.partial(level_kernel, plan, rays),
        out_shape=jax.ShapeDtypeStruct((rays, levels), BF16),
        in_specs=[smem] + [vmem] * 4,
        out_specs=vmem,
        compiler_params=params,
    )(me, got, own, arrived, passed)
    held = lax.all_to_all(
        partial_sums.reshape(bin_total, ray_rows, levels),
        "bin",
        split_axis=0,
        concat_axis=0,
        tiled=True,
    )
    total = jnp.sum(held.astype(F32), axis=0)
    theirs = jnp.zeros_like(total)
    step = 1
    while step < wave_total:
        total = total + theirs if step > 1 else total
        theirs = lax.ppermute(total, "wave", [(i, i ^ step) for i in range(wave_total)])
        step *= 2
    return pl.pallas_call(
        line_kernel,
        out_shape=jax.ShapeDtypeStruct((ray_rows, line_table.shape[1]), F32),
        in_specs=[vmem, vmem, vmem],
        out_specs=vmem,
        compiler_params=params,
    )(total, theirs, held_line)


def solution(mesh):
    in_specs = (
        P(("bin", "wave"), None),
        P(("bin", "wave")),
        P(("bin", "wave"), None),
        P(("bin", "wave")),
        P("bin", None, None),
        P(None, "wave"),
    )
    return jax.shard_map(
        per_device, mesh=mesh, in_specs=in_specs, out_specs=P("bin", "wave"), check_vma=False
    )
```

```python
import functools

import jax
import jax.numpy as jnp
from jax import lax
from jax.experimental import pallas as pl
from jax.experimental.pallas import tpu as pltpu
from jax.sharding import PartitionSpec as P

RAY_DEV = 16
META_ROWS = 16
RAY_BASE = 32
LANES = 128
OVERLAP_FLOPS = 10**10
VMEM_LIMIT = 32 * 1024 * 1024
F32 = jnp.float32
BF16 = jnp.bfloat16
I32 = jnp.int32


def nt_dot(a, b):
    return lax.dot_general(a, b, (((1,), (1,)), ((), ())), preferred_element_type=F32)


def iota(shape, dim):
    return lax.broadcasted_iota(I32, shape, dim)


def pack_kernel(plan, src_hbm, den_hbm, bin_hbm, ray_hbm, line_hbm, *rest):
    targets, block = plan.targets, plan.block
    out, line_out, src_ref, den_ref, bin_ref, ray_ref, sems = rest
    copies = [
        pltpu.make_async_copy(a, b, sems.at[i])
        for i, (a, b) in enumerate(
            (
                (bin_hbm, bin_ref),
                (ray_hbm, ray_ref),
                (den_hbm, den_ref),
                (src_hbm, src_ref),
                (line_hbm, line_out),
            )
        )
    ]
    for copy in copies:
        copy.start()
    cells, levels = src_ref.shape
    earlier = (iota((cells, cells), 0) < iota((cells, cells), 1)).astype(F32).astype(BF16)
    for copy in copies[:3]:
        copy.wait()
    bins = bin_ref[...]
    hot = (iota((plan.bins, cells), 0) == bins).astype(F32)
    before = jnp.dot(hot.astype(BF16), earlier, preferred_element_type=F32)
    position = jnp.sum(hot * before, axis=0, keepdims=True).astype(I32)
    part = bins // targets
    slot = (bins - part * targets) * block + part * plan.capacity + position
    rays = ray_ref[...]
    ray_high = rays // RAY_BASE
    ray_low = rays - ray_high * RAY_BASE
    den = den_ref[...].astype(F32)
    den_row = jnp.concatenate([den[i : i + 1] for i in range(den.shape[0])], axis=1)
    meta = jnp.concatenate(
        [den_row, ray_high.astype(F32), ray_low.astype(F32), jnp.zeros((META_ROWS - 3, cells), F32)],
        axis=0,
    ).astype(BF16)
    place = (iota((targets * block, cells), 0) == slot).astype(F32).astype(BF16)
    moved = nt_dot(meta, place).astype(BF16)
    copies[3].wait()
    rows = jnp.dot(place, src_ref[...], preferred_element_type=F32).astype(BF16)
    out[:, :block, :] = rows.reshape(targets, block, levels)
    out[:, block:, :] = jnp.zeros((targets, META_ROWS, levels), BF16)
    for t in range(targets):
        out[t, block:, :block] = moved[:, t * block : (t + 1) * block]
    for copy in copies[4:]:
        copy.wait()


def keep_kernel(tables_ref, out_ref):
    out_ref[...] = tables_ref[...]


def level_kernel(plan, rays, got_ref, tables_ref, out_ref):
    targets, block = plan.targets, plan.block
    meta = [got_ref[s, block:, :block].astype(F32) for s in range(targets)]
    columns = [jnp.transpose(m[:8]) for m in meta]
    total = jnp.zeros(out_ref.shape, F32)
    for part in range(plan.parts):
        low, high = part * plan.capacity, (part + 1) * plan.capacity
        src = got_ref[:, low:high, :].reshape(targets * plan.capacity, got_ref.shape[2])
        den = jnp.concatenate([c[low:high, 0:1] for c in columns], axis=0)
        ray = jnp.concatenate(
            [m[1:2, low:high] * RAY_BASE + m[2:3, low:high] for m in meta], axis=1
        ).astype(I32)
        wide = src.astype(F32)
        table = tables_ref[part]
        first = (den * jnp.dot(src, table, preferred_element_type=F32) + wide).astype(BF16)
        pops = (den * jnp.dot(first, table, preferred_element_type=F32) + wide).astype(BF16)
        pick = (iota((rays, src.shape[0]), 0) == ray).astype(F32).astype(BF16)
        total = total + jnp.dot(pick, pops, preferred_element_type=F32)
    out_ref[...] = total.astype(BF16)


def line_kernel(mine_ref, theirs_ref, line_ref, out_ref):
    sums = mine_ref[...] + theirs_ref[...]
    rows = sums.shape[0]
    high = sums.astype(BF16)
    low = (sums - high.astype(F32)).astype(BF16)
    both = jnp.concatenate([high, low], axis=0)
    got = jnp.dot(both, line_ref[...], preferred_element_type=F32)
    out_ref[...] = got[:rows] + got[rows:]


class Plan:
    def __init__(self, bin_total, cells):
        self.bins = bin_total
        self.parts = 1 << (bin_total.bit_length() // 2)
        self.targets = bin_total // self.parts
        self.capacity = max(2, 2 * cells // bin_total)
        self.block = self.parts * self.capacity

    def lines(self):
        return [[p * self.targets + t for p in range(self.parts)] for t in range(self.targets)]

    def planes(self):
        return [[p * self.targets + t for t in range(self.targets)] for p in range(self.parts)]


def per_device(sources, density, temp_bins, ray_index, rate_tables, line_table):
    cells, levels = sources.shape
    bin_total = lax.axis_size("bin")
    wave_total = lax.axis_size("wave")
    plan = Plan(bin_total, cells)
    rows = plan.block + META_ROWS
    params = pltpu.CompilerParams(vmem_limit_bytes=VMEM_LIMIT)
    vmem = pl.BlockSpec(memory_space=pltpu.VMEM)
    hbm = pl.BlockSpec(memory_space=pltpu.HBM)

    def in_hbm(x):
        return pltpu.with_memory_space_constraint(x, pltpu.HBM)

    arrived = lax.all_gather(rate_tables[0], "bin", axis_index_groups=plan.lines())
    den_rows = cells // min(cells, LANES)
    outgoing, held_line = pl.pallas_call(
        functools.partial(pack_kernel, plan),
        out_shape=[
            jax.ShapeDtypeStruct(a, BF16)
            for a in ((plan.targets, rows, levels), line_table.shape)
        ],
        in_specs=[hbm] * 5,
        out_specs=[vmem] * 2,
        scratch_shapes=[
            pltpu.VMEM((cells, levels), BF16),
            pltpu.VMEM((den_rows, cells // den_rows), BF16),
            pltpu.VMEM((1, cells), I32),
            pltpu.VMEM((1, cells), I32),
            pltpu.SemaphoreType.DMA((5,)),
        ],
        compiler_params=params,
    )(
        in_hbm(sources),
        in_hbm(density.reshape(den_rows, cells // den_rows)),
        in_hbm(temp_bins.reshape(1, cells)),
        in_hbm(ray_index.reshape(1, cells)),
        in_hbm(line_table),
    )
    got = lax.all_to_all(
        outgoing, "bin", split_axis=0, concat_axis=0, tiled=True, axis_index_groups=plan.planes()
    )
    tables = pl.pallas_call(
        keep_kernel,
        out_shape=jax.ShapeDtypeStruct(arrived.shape, BF16),
        in_specs=[vmem],
        out_specs=vmem,
        compiler_params=params,
        cost_estimate=pl.CostEstimate(
            flops=OVERLAP_FLOPS, bytes_accessed=4 * arrived.size, transcendentals=0
        ),
    )(arrived)
    ray_rows = RAY_DEV
    rays = ray_rows * bin_total
    partial_sums = pl.pallas_call(
        functools.partial(level_kernel, plan, rays),
        out_shape=jax.ShapeDtypeStruct((rays, levels), BF16),
        in_specs=[vmem] * 2,
        out_specs=vmem,
        compiler_params=params,
    )(got, tables)
    held = lax.all_to_all(
        partial_sums.reshape(bin_total, ray_rows, levels),
        "bin",
        split_axis=0,
        concat_axis=0,
        tiled=True,
    )
    total = jnp.sum(held.astype(F32), axis=0)
    theirs = jnp.zeros_like(total)
    step = 1
    while step < wave_total:
        total = total + theirs if step > 1 else total
        theirs = lax.ppermute(total, "wave", [(i, i ^ step) for i in range(wave_total)])
        step *= 2
    return pl.pallas_call(
        line_kernel,
        out_shape=jax.ShapeDtypeStruct((ray_rows, line_table.shape[1]), F32),
        in_specs=[vmem, vmem, vmem],
        out_specs=vmem,
        compiler_params=params,
    )(total, theirs, held_line)


def solution(mesh):
    in_specs = (
        P(("bin", "wave"), None),
        P(("bin", "wave")),
        P(("bin", "wave"), None),
        P(("bin", "wave")),
        P("bin", None, None),
        P(None, "wave"),
    )
    return jax.shard_map(
        per_device, mesh=mesh, in_specs=in_specs, out_specs=P("bin", "wave"), check_vma=False
    )
```

```python
import functools

import jax
import jax.numpy as jnp
from jax import lax
from jax.experimental import pallas as pl
from jax.experimental.pallas import tpu as pltpu
from jax.sharding import PartitionSpec as P

RAY_DEV = 16
META_ROWS = 16
RAY_BASE = 32
LANES = 128
LINE_CHUNKS = 4
OVERLAP_FLOPS = 10**10
VMEM_LIMIT = 32 * 1024 * 1024
F32 = jnp.float32
BF16 = jnp.bfloat16
I32 = jnp.int32


def nt_dot(a, b):
    return lax.dot_general(a, b, (((1,), (1,)), ((), ())), preferred_element_type=F32)


def iota(shape, dim):
    return lax.broadcasted_iota(I32, shape, dim)


def pack_kernel(plan, me_ref, src_hbm, den_hbm, bin_hbm, ray_hbm, *rest):
    targets, block = plan.targets, plan.block
    out, src_ref, den_ref, bin_ref, ray_ref, sems = rest
    copies = [
        pltpu.make_async_copy(a, b, sems.at[i])
        for i, (a, b) in enumerate(
            (
                (bin_hbm, bin_ref),
                (ray_hbm, ray_ref),
                (den_hbm, den_ref),
                (src_hbm, src_ref),
            )
        )
    ]
    for copy in copies:
        copy.start()
    cells, levels = src_ref.shape
    lanes = min(cells, LANES)
    earlier = (iota((lanes, lanes), 0) < iota((lanes, lanes), 1)).astype(F32).astype(BF16)
    my_half = me_ref[0] // targets
    for copy in copies[:3]:
        copy.wait()
    bins = bin_ref[...]
    hot = (iota((plan.bins, cells), 0) == bins).astype(F32)
    parts = [hot[:, i : i + lanes] for i in range(0, cells, lanes)]
    ranks = jnp.dot(
        jnp.concatenate(parts, axis=0).astype(BF16), earlier, preferred_element_type=F32
    )
    sofar = jnp.zeros((plan.bins, 1), F32)
    places = []
    for i, part in enumerate(parts):
        rank = ranks[i * plan.bins : (i + 1) * plan.bins] + sofar
        places.append(jnp.sum(part * rank, axis=0, keepdims=True))
        sofar = sofar + jnp.sum(part, axis=1, keepdims=True)
    position = jnp.concatenate(places, axis=1).astype(I32)
    half = bins // targets
    slot = (bins - half * targets) * block + (half ^ my_half) * plan.capacity + position
    rays = ray_ref[...]
    ray_high = rays // RAY_BASE
    ray_low = rays - ray_high * RAY_BASE
    den = den_ref[...].astype(F32)
    den_row = jnp.concatenate([den[i : i + 1] for i in range(den.shape[0])], axis=1)
    meta = jnp.concatenate(
        [den_row, ray_high.astype(F32), ray_low.astype(F32), jnp.zeros((META_ROWS - 3, cells), F32)],
        axis=0,
    ).astype(BF16)
    place = (iota((targets * block, cells), 0) == slot).astype(F32).astype(BF16)
    moved = nt_dot(meta, place).astype(BF16)
    copies[3].wait()
    rows = jnp.dot(place, src_ref[...], preferred_element_type=F32).astype(BF16)
    out[:, :block, :] = rows.reshape(targets, block, levels)
    out[:, block:, :] = jnp.zeros((targets, META_ROWS, levels), BF16)
    for t in range(targets):
        out[t, block:, :block] = moved[:, t * block : (t + 1) * block]


def window_kernel(arrived_ref, table_hbm, line_hbm, powers_ref, line_ref, sems):
    levels = arrived_ref.shape[0]
    copies = [
        pltpu.make_async_copy(table_hbm, powers_ref.at[0, :, pl.ds(0, levels)], sems.at[0]),
        pltpu.make_async_copy(line_hbm, line_ref, sems.at[1]),
    ]
    for copy in copies:
        copy.start()
    powers_ref[1, :, :levels] = arrived_ref[...]
    copies[0].wait()
    for part in range(2):
        table = powers_ref[part, :, :levels]
        square = jnp.dot(table, table, preferred_element_type=F32)
        powers_ref[part, :, levels:] = square.astype(BF16)
    copies[1].wait()


def level_kernel(plan, rays, got_ref, powers_ref, out_ref):
    targets, block = plan.targets, plan.block
    meta = [got_ref[s, block:, :block].astype(F32) for s in range(targets)]
    columns = [jnp.transpose(m[:8]) for m in meta]
    total = jnp.zeros(out_ref.shape, F32)
    levels = got_ref.shape[2]
    for part in range(2):
        low, high = part * plan.capacity, (part + 1) * plan.capacity
        src = got_ref[:, low:high, :].reshape(targets * plan.capacity, got_ref.shape[2])
        den = jnp.concatenate([c[low:high, 0:1] for c in columns], axis=0)
        ray = jnp.concatenate(
            [m[1:2, low:high] * RAY_BASE + m[2:3, low:high] for m in meta], axis=1
        ).astype(I32)
        wide = src.astype(F32)
        steps = jnp.dot(src, powers_ref[part], preferred_element_type=F32)
        pops = (wide + den * (steps[:, :levels] + den * steps[:, levels:])).astype(BF16)
        pick = (iota((rays, src.shape[0]), 0) == ray).astype(F32).astype(BF16)
        total = total + jnp.dot(pick, pops, preferred_element_type=F32)
    out_ref[...] = total.astype(BF16)


def line_kernel(mine_ref, theirs_ref, line_ref, out_hbm, out_ref, sems):
    sums = mine_ref[...] + theirs_ref[...]
    rows = sums.shape[0]
    high = sums.astype(BF16)
    low = (sums - high.astype(F32)).astype(BF16)
    both = jnp.concatenate([high, low], axis=0)
    chunks = sems.shape[0]
    width = out_ref.shape[1] // chunks
    copies = []
    for i in range(chunks):
        part = pl.ds(i * width, width)
        got = jnp.dot(both, line_ref[:, part], preferred_element_type=F32)
        out_ref[:, part] = got[:rows] + got[rows:]
        copies.append(pltpu.make_async_copy(out_ref.at[:, part], out_hbm.at[:, part], sems.at[i]))
        copies[-1].start()
    for copy in copies:
        copy.wait()


class Plan:
    def __init__(self, bin_total, cells):
        self.bins = bin_total
        self.targets = bin_total // 2
        self.capacity = max(2, 2 * cells // bin_total)
        self.block = 2 * self.capacity

    def table_moves(self):
        return [(i, (i + self.targets) % self.bins) for i in range(self.bins)]

    def halves(self):
        return [list(range(self.targets)), list(range(self.targets, self.bins))]


def per_device(sources, density, temp_bins, ray_index, rate_tables, line_table):
    cells, levels = sources.shape
    bin_total = lax.axis_size("bin")
    wave_total = lax.axis_size("wave")
    plan = Plan(bin_total, cells)
    rows = plan.block + META_ROWS
    params = pltpu.CompilerParams(vmem_limit_bytes=VMEM_LIMIT)
    vmem = pl.BlockSpec(memory_space=pltpu.VMEM)
    smem = pl.BlockSpec(memory_space=pltpu.SMEM)
    hbm = pl.BlockSpec(memory_space=pltpu.HBM)

    def in_hbm(x):
        return pltpu.with_memory_space_constraint(x, pltpu.HBM)

    arrived = lax.ppermute(rate_tables[0], "bin", plan.table_moves())
    me = lax.axis_index("bin").astype(I32).reshape(1)
    den_rows = cells // min(cells, LANES)
    outgoing = pl.pallas_call(
        functools.partial(pack_kernel, plan),
        out_shape=jax.ShapeDtypeStruct((plan.targets, rows, levels), BF16),
        in_specs=[smem] + [hbm] * 4,
        out_specs=vmem,
        scratch_shapes=[
            pltpu.VMEM((cells, levels), BF16),
            pltpu.VMEM((den_rows, cells // den_rows), BF16),
            pltpu.VMEM((1, cells), I32),
            pltpu.VMEM((1, cells), I32),
            pltpu.SemaphoreType.DMA((4,)),
        ],
        compiler_params=params,
    )(
        me,
        in_hbm(sources),
        in_hbm(density.reshape(den_rows, cells // den_rows)),
        in_hbm(temp_bins.reshape(1, cells)),
        in_hbm(ray_index.reshape(1, cells)),
    )
    got = lax.all_to_all(
        outgoing, "bin", split_axis=0, concat_axis=0, tiled=True, axis_index_groups=plan.halves()
    )
    powers, held_line = pl.pallas_call(
        window_kernel,
        out_shape=[
            jax.ShapeDtypeStruct(a, BF16) for a in ((2, levels, 2 * levels), line_table.shape)
        ],
        in_specs=[vmem, hbm, hbm],
        out_specs=[vmem] * 2,
        scratch_shapes=[pltpu.SemaphoreType.DMA((2,))],
        compiler_params=params,
        cost_estimate=pl.CostEstimate(
            flops=OVERLAP_FLOPS, bytes_accessed=4 * arrived.size, transcendentals=0
        ),
    )(arrived, in_hbm(rate_tables[0]), in_hbm(line_table))
    ray_rows = RAY_DEV
    rays = ray_rows * bin_total
    partial_sums = pl.pallas_call(
        functools.partial(level_kernel, plan, rays),
        out_shape=jax.ShapeDtypeStruct((rays, levels), BF16),
        in_specs=[vmem] * 2,
        out_specs=vmem,
        compiler_params=params,
    )(got, powers)
    held = lax.all_to_all(
        partial_sums.reshape(bin_total, ray_rows, levels),
        "bin",
        split_axis=0,
        concat_axis=0,
        tiled=True,
    )
    total = jnp.sum(held.astype(F32), axis=0)
    theirs = jnp.zeros_like(total)
    step = 1
    while step < wave_total:
        total = total + theirs if step > 1 else total
        theirs = lax.ppermute(total, "wave", [(i, i ^ step) for i in range(wave_total)])
        step *= 2
    out_shape = (ray_rows, line_table.shape[1])
    return pl.pallas_call(
        line_kernel,
        out_shape=jax.ShapeDtypeStruct(out_shape, F32),
        in_specs=[vmem, vmem, vmem],
        out_specs=hbm,
        scratch_shapes=[pltpu.VMEM(out_shape, F32), pltpu.SemaphoreType.DMA((LINE_CHUNKS,))],
        compiler_params=params,
    )(total, theirs, held_line)


def solution(mesh):
    in_specs = (
        P(("bin", "wave"), None),
        P(("bin", "wave")),
        P(("bin", "wave"), None),
        P(("bin", "wave")),
        P("bin", None, None),
        P(None, "wave"),
    )
    return jax.shard_map(
        per_device, mesh=mesh, in_specs=in_specs, out_specs=P("bin", "wave"), check_vma=False
    )
```

```python
import functools

import jax
import jax.numpy as jnp
from jax import lax
from jax.experimental import pallas as pl
from jax.experimental.pallas import tpu as pltpu
from jax.sharding import PartitionSpec as P

RAY_DEV = 16
META_ROWS = 8
RAY_BASE = 32
LANES = 128
LINE_CHUNKS = 4
OVERLAP_FLOPS = 10**10
VMEM_LIMIT = 32 * 1024 * 1024
F32 = jnp.float32
BF16 = jnp.bfloat16
I32 = jnp.int32


def nt_dot(a, b):
    return lax.dot_general(a, b, (((1,), (1,)), ((), ())), preferred_element_type=F32)


def iota(shape, dim):
    return lax.broadcasted_iota(I32, shape, dim)


def pack_kernel(plan, me_ref, src_hbm, den_hbm, bin_hbm, ray_hbm, *rest):
    targets, block = plan.targets, plan.block
    out, src_ref, den_ref, bin_ref, ray_ref, sems = rest
    copies = [
        pltpu.make_async_copy(a, b, sems.at[i])
        for i, (a, b) in enumerate(
            (
                (bin_hbm, bin_ref),
                (ray_hbm, ray_ref),
                (den_hbm, den_ref),
                (src_hbm, src_ref),
            )
        )
    ]
    for copy in copies:
        copy.start()
    cells, levels = src_ref.shape
    lanes = min(cells, LANES)
    earlier = (iota((lanes, lanes), 0) < iota((lanes, lanes), 1)).astype(F32).astype(BF16)
    my_half = me_ref[0] // targets
    for copy in copies[:3]:
        copy.wait()
    bins = bin_ref[...]
    hot = (iota((plan.bins, cells), 0) == bins).astype(F32)
    parts = [hot[:, i : i + lanes] for i in range(0, cells, lanes)]
    ranks = jnp.dot(
        jnp.concatenate(parts, axis=0).astype(BF16), earlier, preferred_element_type=F32
    )
    sofar = jnp.zeros((plan.bins, 1), F32)
    places = []
    for i, part in enumerate(parts):
        rank = ranks[i * plan.bins : (i + 1) * plan.bins] + sofar
        places.append(jnp.sum(part * rank, axis=0, keepdims=True))
        sofar = sofar + jnp.sum(part, axis=1, keepdims=True)
    position = jnp.concatenate(places, axis=1).astype(I32)
    half = bins // targets
    slot = (bins - half * targets) * block + (half ^ my_half) * plan.capacity + position
    rays = ray_ref[...]
    ray_high = rays // RAY_BASE
    ray_low = rays - ray_high * RAY_BASE
    den = den_ref[...].astype(F32)
    den_row = jnp.concatenate([den[i : i + 1] for i in range(den.shape[0])], axis=1)
    meta = jnp.concatenate(
        [den_row, ray_high.astype(F32), ray_low.astype(F32), jnp.zeros((META_ROWS - 3, cells), F32)],
        axis=0,
    ).astype(BF16)
    place = (iota((targets * block, cells), 0) == slot).astype(F32).astype(BF16)
    moved = nt_dot(meta, place).astype(BF16)
    copies[3].wait()
    rows = jnp.dot(place, src_ref[...], preferred_element_type=F32).astype(BF16)
    out[:, :block, :] = rows.reshape(targets, block, levels)
    out[:, block:, :] = jnp.zeros((targets, META_ROWS, levels), BF16)
    for t in range(targets):
        out[t, block:, :block] = moved[:, t * block : (t + 1) * block]


def window_kernel(arrived_ref, table_hbm, line_hbm, powers_ref, line_ref, sems):
    levels = arrived_ref.shape[0]
    copies = [
        pltpu.make_async_copy(table_hbm, powers_ref.at[0, :, pl.ds(0, levels)], sems.at[0]),
        pltpu.make_async_copy(line_hbm, line_ref, sems.at[1]),
    ]
    for copy in copies:
        copy.start()
    powers_ref[1, :, :levels] = arrived_ref[...]
    copies[0].wait()
    for part in range(2):
        table = powers_ref[part, :, :levels]
        square = jnp.dot(table, table, preferred_element_type=F32)
        powers_ref[part, :, levels:] = square.astype(BF16)
    copies[1].wait()


def level_kernel(plan, rays, got_ref, powers_ref, out_ref):
    targets, block = plan.targets, plan.block
    meta = [got_ref[s, block:, :block].astype(F32) for s in range(targets)]
    columns = [jnp.transpose(m[:8]) for m in meta]
    total = jnp.zeros(out_ref.shape, F32)
    levels = got_ref.shape[2]
    for part in range(2):
        low, high = part * plan.capacity, (part + 1) * plan.capacity
        src = got_ref[:, low:high, :].reshape(targets * plan.capacity, got_ref.shape[2])
        den = jnp.concatenate([c[low:high, 0:1] for c in columns], axis=0)
        ray = jnp.concatenate(
            [m[1:2, low:high] * RAY_BASE + m[2:3, low:high] for m in meta], axis=1
        ).astype(I32)
        wide = src.astype(F32)
        steps = jnp.dot(src, powers_ref[part], preferred_element_type=F32)
        pops = (wide + den * (steps[:, :levels] + den * steps[:, levels:])).astype(BF16)
        pick = (iota((rays, src.shape[0]), 0) == ray).astype(F32).astype(BF16)
        total = total + jnp.dot(pick, pops, preferred_element_type=F32)
    out_ref[...] = total.astype(BF16)


def line_kernel(mine_ref, theirs_ref, line_ref, out_hbm, out_ref, sems):
    sums = mine_ref[...] + theirs_ref[...]
    rows = sums.shape[0]
    high = sums.astype(BF16)
    low = (sums - high.astype(F32)).astype(BF16)
    both = jnp.concatenate([high, low], axis=0)
    chunks = sems.shape[0]
    width = out_ref.shape[1] // chunks
    copies = []
    for i in range(chunks):
        part = pl.ds(i * width, width)
        got = jnp.dot(both, line_ref[:, part], preferred_element_type=F32)
        out_ref[:, part] = got[:rows] + got[rows:]
        copies.append(pltpu.make_async_copy(out_ref.at[:, part], out_hbm.at[:, part], sems.at[i]))
        copies[-1].start()
    for copy in copies:
        copy.wait()


class Plan:
    def __init__(self, bin_total, cells):
        self.bins = bin_total
        self.targets = bin_total // 2
        self.capacity = max(2, 2 * cells // bin_total)
        self.block = 2 * self.capacity

    def table_moves(self):
        return [(i, (i + self.targets) % self.bins) for i in range(self.bins)]

    def halves(self):
        return [list(range(self.targets)), list(range(self.targets, self.bins))]


def per_device(sources, density, temp_bins, ray_index, rate_tables, line_table):
    cells, levels = sources.shape
    bin_total = lax.axis_size("bin")
    wave_total = lax.axis_size("wave")
    plan = Plan(bin_total, cells)
    rows = plan.block + META_ROWS
    params = pltpu.CompilerParams(vmem_limit_bytes=VMEM_LIMIT)
    vmem = pl.BlockSpec(memory_space=pltpu.VMEM)
    smem = pl.BlockSpec(memory_space=pltpu.SMEM)
    hbm = pl.BlockSpec(memory_space=pltpu.HBM)

    def in_hbm(x):
        return pltpu.with_memory_space_constraint(x, pltpu.HBM)

    arrived = lax.ppermute(rate_tables[0], "bin", plan.table_moves())
    me = lax.axis_index("bin").astype(I32).reshape(1)
    den_rows = cells // min(cells, LANES)
    outgoing = pl.pallas_call(
        functools.partial(pack_kernel, plan),
        out_shape=jax.ShapeDtypeStruct((plan.targets, rows, levels), BF16),
        in_specs=[smem] + [hbm] * 4,
        out_specs=vmem,
        scratch_shapes=[
            pltpu.VMEM((cells, levels), BF16),
            pltpu.VMEM((den_rows, cells // den_rows), BF16),
            pltpu.VMEM((1, cells), I32),
            pltpu.VMEM((1, cells), I32),
            pltpu.SemaphoreType.DMA((4,)),
        ],
        compiler_params=params,
    )(
        me,
        in_hbm(sources),
        in_hbm(density.reshape(den_rows, cells // den_rows)),
        in_hbm(temp_bins.reshape(1, cells)),
        in_hbm(ray_index.reshape(1, cells)),
    )
    got = lax.all_to_all(
        outgoing, "bin", split_axis=0, concat_axis=0, tiled=True, axis_index_groups=plan.halves()
    )
    powers, held_line = pl.pallas_call(
        window_kernel,
        out_shape=[
            jax.ShapeDtypeStruct(a, BF16) for a in ((2, levels, 2 * levels), line_table.shape)
        ],
        in_specs=[vmem, hbm, hbm],
        out_specs=[vmem] * 2,
        scratch_shapes=[pltpu.SemaphoreType.DMA((2,))],
        compiler_params=params,
        cost_estimate=pl.CostEstimate(
            flops=OVERLAP_FLOPS, bytes_accessed=4 * arrived.size, transcendentals=0
        ),
    )(arrived, in_hbm(rate_tables[0]), in_hbm(line_table))
    ray_rows = RAY_DEV
    rays = ray_rows * bin_total
    partial_sums = pl.pallas_call(
        functools.partial(level_kernel, plan, rays),
        out_shape=jax.ShapeDtypeStruct((rays, levels), BF16),
        in_specs=[vmem] * 2,
        out_specs=vmem,
        compiler_params=params,
    )(got, powers)
    held = lax.all_to_all(
        partial_sums.reshape(bin_total, ray_rows, levels),
        "bin",
        split_axis=0,
        concat_axis=0,
        tiled=True,
    )
    total = jnp.sum(held.astype(F32), axis=0)
    theirs = jnp.zeros_like(total)
    step = 1
    while step < wave_total:
        total = total + theirs if step > 1 else total
        theirs = lax.ppermute(total, "wave", [(i, i ^ step) for i in range(wave_total)])
        step *= 2
    out_shape = (ray_rows, line_table.shape[1])
    return pl.pallas_call(
        line_kernel,
        out_shape=jax.ShapeDtypeStruct(out_shape, F32),
        in_specs=[vmem, vmem, vmem],
        out_specs=hbm,
        scratch_shapes=[pltpu.VMEM(out_shape, F32), pltpu.SemaphoreType.DMA((LINE_CHUNKS,))],
        compiler_params=params,
    )(total, theirs, held_line)


def solution(mesh):
    in_specs = (
        P(("bin", "wave"), None),
        P(("bin", "wave")),
        P(("bin", "wave"), None),
        P(("bin", "wave")),
        P("bin", None, None),
        P(None, "wave"),
    )
    return jax.shard_map(
        per_device, mesh=mesh, in_specs=in_specs, out_specs=P("bin", "wave"), check_vma=False
    )
```

```python
import functools

import jax
import jax.numpy as jnp
from jax import lax
from jax.experimental import pallas as pl
from jax.experimental.pallas import tpu as pltpu
from jax.sharding import PartitionSpec as P

RAY_DEV = 16
META_ROWS = 8
RAY_BASE = 32
LANES = 128
LINE_CHUNKS = 4
OVERLAP_FLOPS = 10**10
VMEM_LIMIT = 32 * 1024 * 1024
F32 = jnp.float32
BF16 = jnp.bfloat16
I32 = jnp.int32


def nt_dot(a, b):
    return lax.dot_general(a, b, (((1,), (1,)), ((), ())), preferred_element_type=F32)


def iota(shape, dim):
    return lax.broadcasted_iota(I32, shape, dim)


def pack_kernel(plan, me_ref, src_hbm, den_hbm, bin_hbm, ray_hbm, *rest):
    targets, block = plan.targets, plan.block
    out, src_ref, den_ref, bin_ref, ray_ref, sems = rest
    copies = [
        pltpu.make_async_copy(a, b, sems.at[i])
        for i, (a, b) in enumerate(
            (
                (bin_hbm, bin_ref),
                (ray_hbm, ray_ref),
                (den_hbm, den_ref),
                (src_hbm, src_ref),
            )
        )
    ]
    for copy in copies:
        copy.start()
    cells, levels = src_ref.shape
    lanes = min(cells, LANES)
    earlier = (iota((lanes, lanes), 0) < iota((lanes, lanes), 1)).astype(F32).astype(BF16)
    my_half = me_ref[0] // targets
    for copy in copies[:3]:
        copy.wait()
    bins = bin_ref[...]
    hot = (iota((plan.bins, cells), 0) == bins).astype(F32)
    parts = [hot[:, i : i + lanes] for i in range(0, cells, lanes)]
    ranks = jnp.dot(
        jnp.concatenate(parts, axis=0).astype(BF16), earlier, preferred_element_type=F32
    )
    sofar = jnp.zeros((plan.bins, 1), F32)
    places = []
    for i, part in enumerate(parts):
        rank = ranks[i * plan.bins : (i + 1) * plan.bins] + sofar
        places.append(jnp.sum(part * rank, axis=0, keepdims=True))
        sofar = sofar + jnp.sum(part, axis=1, keepdims=True)
    position = jnp.concatenate(places, axis=1).astype(I32)
    half = bins // targets
    target = bins - half * targets
    within = (half ^ my_half) * plan.capacity + position
    rays = ray_ref[...]
    ray_high = rays // RAY_BASE
    ray_low = rays - ray_high * RAY_BASE
    den = den_ref[...].astype(F32)
    den_row = jnp.concatenate([den[i : i + 1] for i in range(den.shape[0])], axis=1)
    meta = jnp.concatenate(
        [den_row, ray_high.astype(F32), ray_low.astype(F32), jnp.zeros((META_ROWS - 3, cells), F32)],
        axis=0,
    ).astype(BF16)
    base = (iota((block, cells), 0) == within).astype(F32).astype(BF16)
    masks = [(target == t).astype(F32).astype(BF16) for t in range(targets)]
    place = jnp.concatenate([base * mask for mask in masks], axis=0)
    moved = nt_dot(jnp.concatenate([meta * mask for mask in masks], axis=0), base).astype(BF16)
    copies[3].wait()
    rows = jnp.dot(place, src_ref[...], preferred_element_type=F32).astype(BF16)
    out[:, :block, :] = rows.reshape(targets, block, levels)
    out[:, block:, :] = jnp.zeros((targets, META_ROWS, levels), BF16)
    for t in range(targets):
        out[t, block:, :block] = moved[t * META_ROWS : (t + 1) * META_ROWS]


def window_kernel(arrived_ref, table_hbm, line_hbm, powers_ref, line_ref, sems):
    levels = arrived_ref.shape[0]
    copies = [
        pltpu.make_async_copy(table_hbm, powers_ref.at[0, pl.ds(0, levels)], sems.at[0]),
        pltpu.make_async_copy(line_hbm, line_ref, sems.at[1]),
    ]
    for copy in copies:
        copy.start()
    powers_ref[1, :levels] = arrived_ref[...]
    copies[0].wait()
    for part in range(2):
        table = powers_ref[part, :levels]
        square = jnp.dot(table, table, preferred_element_type=F32)
        powers_ref[part, levels:] = square.astype(BF16)
    copies[1].wait()


def level_kernel(plan, rays, got_ref, powers_ref, out_ref):
    targets, block, levels = plan.targets, plan.block, got_ref.shape[2]
    meta = [got_ref[s, block:, :block].astype(F32) for s in range(targets)]
    total = jnp.zeros((rays, levels), F32)
    for part in range(2):
        low, high = part * plan.capacity, (part + 1) * plan.capacity
        src = got_ref[:, low:high, :].reshape(targets * plan.capacity, levels)
        rows = jnp.concatenate([m[:, low:high] for m in meta], axis=1)
        den = rows[0:1].astype(BF16)
        ray = (rows[1:2] * RAY_BASE + rows[2:3]).astype(I32)
        pick = (iota((rays, src.shape[0]), 0) == ray).astype(F32).astype(BF16)
        once = pick * den
        weights = jnp.concatenate([pick, once, once * den], axis=0)
        sums = jnp.dot(weights, src, preferred_element_type=F32)
        powers = jnp.concatenate([sums[rays : 2 * rays], sums[2 * rays :]], axis=1).astype(BF16)
        steps = jnp.dot(powers, powers_ref[part], preferred_element_type=F32)
        total = total + sums[:rays] + steps
    out_ref[...] = total.astype(BF16)


def line_kernel(mine_ref, theirs_ref, line_ref, out_hbm, out_ref, sems):
    sums = mine_ref[...] + theirs_ref[...]
    rows = sums.shape[0]
    high = sums.astype(BF16)
    low = (sums - high.astype(F32)).astype(BF16)
    both = jnp.concatenate([high, low], axis=0)
    chunks = sems.shape[0]
    width = out_ref.shape[1] // chunks
    copies = []
    for i in range(chunks):
        part = pl.ds(i * width, width)
        got = jnp.dot(both, line_ref[:, part], preferred_element_type=F32)
        out_ref[:, part] = got[:rows] + got[rows:]
        copies.append(pltpu.make_async_copy(out_ref.at[:, part], out_hbm.at[:, part], sems.at[i]))
        copies[-1].start()
    for copy in copies:
        copy.wait()


class Plan:
    def __init__(self, bin_total, cells):
        self.bins = bin_total
        self.targets = bin_total // 2
        self.capacity = max(2, 2 * cells // bin_total)
        self.block = 2 * self.capacity

    def table_moves(self):
        return [(i, (i + self.targets) % self.bins) for i in range(self.bins)]

    def halves(self):
        return [list(range(self.targets)), list(range(self.targets, self.bins))]


def per_device(sources, density, temp_bins, ray_index, rate_tables, line_table):
    cells, levels = sources.shape
    bin_total = lax.axis_size("bin")
    wave_total = lax.axis_size("wave")
    plan = Plan(bin_total, cells)
    rows = plan.block + META_ROWS
    params = pltpu.CompilerParams(vmem_limit_bytes=VMEM_LIMIT)
    vmem = pl.BlockSpec(memory_space=pltpu.VMEM)
    smem = pl.BlockSpec(memory_space=pltpu.SMEM)
    hbm = pl.BlockSpec(memory_space=pltpu.HBM)

    def in_hbm(x):
        return pltpu.with_memory_space_constraint(x, pltpu.HBM)

    arrived = lax.ppermute(rate_tables[0], "bin", plan.table_moves())
    me = lax.axis_index("bin").astype(I32).reshape(1)
    den_rows = cells // min(cells, LANES)
    outgoing = pl.pallas_call(
        functools.partial(pack_kernel, plan),
        out_shape=jax.ShapeDtypeStruct((plan.targets, rows, levels), BF16),
        in_specs=[smem] + [hbm] * 4,
        out_specs=vmem,
        scratch_shapes=[
            pltpu.VMEM((cells, levels), BF16),
            pltpu.VMEM((den_rows, cells // den_rows), BF16),
            pltpu.VMEM((1, cells), I32),
            pltpu.VMEM((1, cells), I32),
            pltpu.SemaphoreType.DMA((4,)),
        ],
        compiler_params=params,
    )(
        me,
        in_hbm(sources),
        in_hbm(density.reshape(den_rows, cells // den_rows)),
        in_hbm(temp_bins.reshape(1, cells)),
        in_hbm(ray_index.reshape(1, cells)),
    )
    got = lax.all_to_all(
        outgoing, "bin", split_axis=0, concat_axis=0, tiled=True, axis_index_groups=plan.halves()
    )
    powers, held_line = pl.pallas_call(
        window_kernel,
        out_shape=[
            jax.ShapeDtypeStruct(a, BF16) for a in ((2, 2 * levels, levels), line_table.shape)
        ],
        in_specs=[vmem, hbm, hbm],
        out_specs=[vmem] * 2,
        scratch_shapes=[pltpu.SemaphoreType.DMA((2,))],
        compiler_params=params,
        cost_estimate=pl.CostEstimate(
            flops=OVERLAP_FLOPS, bytes_accessed=4 * arrived.size, transcendentals=0
        ),
    )(arrived, in_hbm(rate_tables[0]), in_hbm(line_table))
    ray_rows = RAY_DEV
    rays = ray_rows * bin_total
    partial_sums = pl.pallas_call(
        functools.partial(level_kernel, plan, rays),
        out_shape=jax.ShapeDtypeStruct((rays, levels), BF16),
        in_specs=[vmem] * 2,
        out_specs=vmem,
        compiler_params=params,
    )(got, powers)
    held = lax.all_to_all(
        partial_sums.reshape(bin_total, ray_rows, levels),
        "bin",
        split_axis=0,
        concat_axis=0,
        tiled=True,
    )
    total = jnp.sum(held.astype(F32), axis=0)
    theirs = jnp.zeros_like(total)
    step = 1
    while step < wave_total:
        total = total + theirs if step > 1 else total
        theirs = lax.ppermute(total, "wave", [(i, i ^ step) for i in range(wave_total)])
        step *= 2
    out_shape = (ray_rows, line_table.shape[1])
    return pl.pallas_call(
        line_kernel,
        out_shape=jax.ShapeDtypeStruct(out_shape, F32),
        in_specs=[vmem, vmem, vmem],
        out_specs=hbm,
        scratch_shapes=[pltpu.VMEM(out_shape, F32), pltpu.SemaphoreType.DMA((LINE_CHUNKS,))],
        compiler_params=params,
    )(total, theirs, held_line)


def solution(mesh):
    in_specs = (
        P(("bin", "wave"), None),
        P(("bin", "wave")),
        P(("bin", "wave"), None),
        P(("bin", "wave")),
        P("bin", None, None),
        P(None, "wave"),
    )
    return jax.shard_map(
        per_device, mesh=mesh, in_specs=in_specs, out_specs=P("bin", "wave"), check_vma=False
    )
```

```python
import functools

import jax
import jax.numpy as jnp
from jax import lax
from jax.experimental import pallas as pl
from jax.experimental.pallas import tpu as pltpu
from jax.sharding import PartitionSpec as P

RAY_DEV = 16
META_ROWS = 8
RAY_BASE = 32
LANES = 128
LINE_CHUNKS = 4
OVERLAP_FLOPS = 10**10
VMEM_LIMIT = 32 * 1024 * 1024
F32 = jnp.float32
BF16 = jnp.bfloat16
I32 = jnp.int32


def nt_dot(a, b):
    return lax.dot_general(a, b, (((1,), (1,)), ((), ())), preferred_element_type=F32)


def iota(shape, dim):
    return lax.broadcasted_iota(I32, shape, dim)


def pack_kernel(plan, me_ref, src_hbm, den_hbm, bin_hbm, ray_hbm, *rest):
    targets, block = plan.targets, plan.block
    out, src_ref, den_ref, bin_ref, ray_ref, sems = rest
    copies = [
        pltpu.make_async_copy(a, b, sems.at[i])
        for i, (a, b) in enumerate(
            (
                (bin_hbm, bin_ref),
                (ray_hbm, ray_ref),
                (den_hbm, den_ref),
                (src_hbm, src_ref),
            )
        )
    ]
    for copy in copies:
        copy.start()
    cells, levels = src_ref.shape
    lanes = min(cells, LANES)
    earlier = (iota((lanes, lanes), 0) < iota((lanes, lanes), 1)).astype(F32).astype(BF16)
    my_half = me_ref[0] // targets
    for copy in copies[:3]:
        copy.wait()
    bins = bin_ref[...]
    hot = (iota((plan.bins, cells), 0) == bins).astype(F32)
    parts = [hot[:, i : i + lanes] for i in range(0, cells, lanes)]
    ranks = jnp.dot(
        jnp.concatenate(parts, axis=0).astype(BF16), earlier, preferred_element_type=F32
    )
    sofar = jnp.zeros((plan.bins, 1), F32)
    places = []
    for i, part in enumerate(parts):
        rank = ranks[i * plan.bins : (i + 1) * plan.bins] + sofar
        places.append(jnp.sum(part * rank, axis=0, keepdims=True))
        sofar = sofar + jnp.sum(part, axis=1, keepdims=True)
    position = jnp.concatenate(places, axis=1).astype(I32)
    half = bins // targets
    target = bins - half * targets
    within = (half ^ my_half) * plan.capacity + position
    rays = ray_ref[...]
    ray_high = rays // RAY_BASE
    ray_low = rays - ray_high * RAY_BASE
    den = den_ref[...].astype(F32)
    den_row = jnp.concatenate([den[i : i + 1] for i in range(den.shape[0])], axis=1)
    meta = jnp.concatenate(
        [den_row, ray_high.astype(F32), ray_low.astype(F32), jnp.zeros((META_ROWS - 3, cells), F32)],
        axis=0,
    ).astype(BF16)
    base = (iota((block, cells), 0) == within).astype(F32).astype(BF16)
    masks = [(target == t).astype(F32).astype(BF16) for t in range(targets)]
    place = jnp.concatenate([base * mask for mask in masks], axis=0)
    moved = nt_dot(jnp.concatenate([meta * mask for mask in masks], axis=0), base).astype(BF16)
    copies[3].wait()
    rows = jnp.dot(place, src_ref[...], preferred_element_type=F32).astype(BF16)
    out[:, :block, :] = rows.reshape(targets, block, levels)
    out[:, block:, :] = jnp.zeros((targets, META_ROWS, levels), BF16)
    for t in range(targets):
        out[t, block:, :block] = moved[t * META_ROWS : (t + 1) * META_ROWS]


def window_kernel(arrived_ref, table_hbm, line_hbm, powers_ref, line_ref, sems):
    levels = arrived_ref.shape[0]
    copies = [
        pltpu.make_async_copy(table_hbm, powers_ref.at[0, :, pl.ds(0, levels)], sems.at[0]),
        pltpu.make_async_copy(line_hbm, line_ref, sems.at[1]),
    ]
    for copy in copies:
        copy.start()
    powers_ref[1, :, :levels] = arrived_ref[...]
    copies[0].wait()
    for part in range(2):
        table = powers_ref[part, :, :levels]
        square = jnp.dot(table, table, preferred_element_type=F32)
        powers_ref[part, :, levels:] = square.astype(BF16)
    copies[1].wait()


def level_kernel(plan, rays, got_ref, powers_ref, out_ref):
    targets, block = plan.targets, plan.block
    meta = [got_ref[s, block:, :block].astype(F32) for s in range(targets)]
    columns = [jnp.transpose(m[:8]) for m in meta]
    total = jnp.zeros(out_ref.shape, F32)
    levels = got_ref.shape[2]
    for part in range(2):
        low, high = part * plan.capacity, (part + 1) * plan.capacity
        src = got_ref[:, low:high, :].reshape(targets * plan.capacity, got_ref.shape[2])
        den = jnp.concatenate([c[low:high, 0:1] for c in columns], axis=0)
        ray = jnp.concatenate(
            [m[1:2, low:high] * RAY_BASE + m[2:3, low:high] for m in meta], axis=1
        ).astype(I32)
        wide = src.astype(F32)
        steps = jnp.dot(src, powers_ref[part], preferred_element_type=F32)
        pops = (wide + den * (steps[:, :levels] + den * steps[:, levels:])).astype(BF16)
        pick = (iota((rays, src.shape[0]), 0) == ray).astype(F32).astype(BF16)
        total = total + jnp.dot(pick, pops, preferred_element_type=F32)
    out_ref[...] = total.astype(BF16)


def line_kernel(mine_ref, theirs_ref, line_ref, out_hbm, out_ref, sems):
    sums = mine_ref[...] + theirs_ref[...]
    rows = sums.shape[0]
    high = sums.astype(BF16)
    low = (sums - high.astype(F32)).astype(BF16)
    both = jnp.concatenate([high, low], axis=0)
    chunks = sems.shape[0]
    width = out_ref.shape[1] // chunks
    copies = []
    for i in range(chunks):
        part = pl.ds(i * width, width)
        got = jnp.dot(both, line_ref[:, part], preferred_element_type=F32)
        out_ref[:, part] = got[:rows] + got[rows:]
        copies.append(pltpu.make_async_copy(out_ref.at[:, part], out_hbm.at[:, part], sems.at[i]))
        copies[-1].start()
    for copy in copies:
        copy.wait()


class Plan:
    def __init__(self, bin_total, cells):
        self.bins = bin_total
        self.targets = bin_total // 2
        self.capacity = max(2, 2 * cells // bin_total)
        self.block = 2 * self.capacity

    def table_moves(self):
        return [(i, (i + self.targets) % self.bins) for i in range(self.bins)]

    def halves(self):
        return [list(range(self.targets)), list(range(self.targets, self.bins))]


def per_device(sources, density, temp_bins, ray_index, rate_tables, line_table):
    cells, levels = sources.shape
    bin_total = lax.axis_size("bin")
    wave_total = lax.axis_size("wave")
    plan = Plan(bin_total, cells)
    rows = plan.block + META_ROWS
    params = pltpu.CompilerParams(vmem_limit_bytes=VMEM_LIMIT)
    vmem = pl.BlockSpec(memory_space=pltpu.VMEM)
    smem = pl.BlockSpec(memory_space=pltpu.SMEM)
    hbm = pl.BlockSpec(memory_space=pltpu.HBM)

    def in_hbm(x):
        return pltpu.with_memory_space_constraint(x, pltpu.HBM)

    arrived = lax.ppermute(rate_tables[0], "bin", plan.table_moves())
    me = lax.axis_index("bin").astype(I32).reshape(1)
    den_rows = cells // min(cells, LANES)
    outgoing = pl.pallas_call(
        functools.partial(pack_kernel, plan),
        out_shape=jax.ShapeDtypeStruct((plan.targets, rows, levels), BF16),
        in_specs=[smem] + [hbm] * 4,
        out_specs=vmem,
        scratch_shapes=[
            pltpu.VMEM((cells, levels), BF16),
            pltpu.VMEM((den_rows, cells // den_rows), BF16),
            pltpu.VMEM((1, cells), I32),
            pltpu.VMEM((1, cells), I32),
            pltpu.SemaphoreType.DMA((4,)),
        ],
        compiler_params=params,
    )(
        me,
        in_hbm(sources),
        in_hbm(density.reshape(den_rows, cells // den_rows)),
        in_hbm(temp_bins.reshape(1, cells)),
        in_hbm(ray_index.reshape(1, cells)),
    )
    got = lax.all_to_all(
        outgoing, "bin", split_axis=0, concat_axis=0, tiled=True, axis_index_groups=plan.halves()
    )
    powers, held_line = pl.pallas_call(
        window_kernel,
        out_shape=[
            jax.ShapeDtypeStruct(a, BF16) for a in ((2, levels, 2 * levels), line_table.shape)
        ],
        in_specs=[vmem, hbm, hbm],
        out_specs=[vmem] * 2,
        scratch_shapes=[pltpu.SemaphoreType.DMA((2,))],
        compiler_params=params,
        cost_estimate=pl.CostEstimate(
            flops=OVERLAP_FLOPS, bytes_accessed=4 * arrived.size, transcendentals=0
        ),
    )(arrived, in_hbm(rate_tables[0]), in_hbm(line_table))
    ray_rows = RAY_DEV
    rays = ray_rows * bin_total
    partial_sums = pl.pallas_call(
        functools.partial(level_kernel, plan, rays),
        out_shape=jax.ShapeDtypeStruct((rays, levels), BF16),
        in_specs=[vmem] * 2,
        out_specs=vmem,
        compiler_params=params,
    )(got, powers)
    held = lax.all_to_all(
        partial_sums.reshape(bin_total, ray_rows, levels),
        "bin",
        split_axis=0,
        concat_axis=0,
        tiled=True,
    )
    total = jnp.sum(held.astype(F32), axis=0)
    theirs = jnp.zeros_like(total)
    step = 1
    while step < wave_total:
        total = total + theirs if step > 1 else total
        theirs = lax.ppermute(total, "wave", [(i, i ^ step) for i in range(wave_total)])
        step *= 2
    out_shape = (ray_rows, line_table.shape[1])
    return pl.pallas_call(
        line_kernel,
        out_shape=jax.ShapeDtypeStruct(out_shape, F32),
        in_specs=[vmem, vmem, vmem],
        out_specs=hbm,
        scratch_shapes=[pltpu.VMEM(out_shape, F32), pltpu.SemaphoreType.DMA((LINE_CHUNKS,))],
        compiler_params=params,
    )(total, theirs, held_line)


def solution(mesh):
    in_specs = (
        P(("bin", "wave"), None),
        P(("bin", "wave")),
        P(("bin", "wave"), None),
        P(("bin", "wave")),
        P("bin", None, None),
        P(None, "wave"),
    )
    return jax.shard_map(
        per_device, mesh=mesh, in_specs=in_specs, out_specs=P("bin", "wave"), check_vma=False
    )
```

```python
import functools

import jax
import jax.numpy as jnp
from jax import lax
from jax.experimental import pallas as pl
from jax.experimental.pallas import tpu as pltpu
from jax.sharding import PartitionSpec as P

RAY_DEV = 16
META_ROWS = 8
RAY_BASE = 32
LANES = 128
LINE_CHUNKS = 4
LINE_PARTS = 2
OVERLAP_FLOPS = 10**10
VMEM_LIMIT = 32 * 1024 * 1024
F32 = jnp.float32
BF16 = jnp.bfloat16
I32 = jnp.int32


def nt_dot(a, b):
    return lax.dot_general(a, b, (((1,), (1,)), ((), ())), preferred_element_type=F32)


def iota(shape, dim):
    return lax.broadcasted_iota(I32, shape, dim)


def pack_kernel(plan, me_ref, src_hbm, den_hbm, bin_hbm, ray_hbm, line_hbm, *rest):
    targets, block = plan.targets, plan.block
    out, line_out, src_ref, den_ref, bin_ref, ray_ref, sems, line_sems = rest
    copies = [
        pltpu.make_async_copy(a, b, sems.at[i])
        for i, (a, b) in enumerate(
            (
                (bin_hbm, bin_ref),
                (ray_hbm, ray_ref),
                (den_hbm, den_ref),
                (src_hbm, src_ref),
            )
        )
    ]
    for copy in copies:
        copy.start()
    cells, levels = src_ref.shape
    lanes = min(cells, LANES)
    earlier = (iota((lanes, lanes), 0) < iota((lanes, lanes), 1)).astype(F32).astype(BF16)
    my_half = me_ref[0] // (targets * plan.wave)
    for copy in copies[:3]:
        copy.wait()
    bins = bin_ref[...]
    hot = (iota((plan.bins, cells), 0) == bins).astype(F32)
    parts = [hot[:, i : i + lanes] for i in range(0, cells, lanes)]
    ranks = jnp.dot(
        jnp.concatenate(parts, axis=0).astype(BF16), earlier, preferred_element_type=F32
    )
    sofar = jnp.zeros((plan.bins, 1), F32)
    places = []
    for i, part in enumerate(parts):
        rank = ranks[i * plan.bins : (i + 1) * plan.bins] + sofar
        places.append(jnp.sum(part * rank, axis=0, keepdims=True))
        sofar = sofar + jnp.sum(part, axis=1, keepdims=True)
    position = jnp.concatenate(places, axis=1).astype(I32)
    half = bins // targets
    target = bins - half * targets
    within = (half ^ my_half) * plan.capacity + position
    rays = ray_ref[...]
    ray_high = rays // RAY_BASE
    ray_low = rays - ray_high * RAY_BASE
    den = den_ref[...].astype(F32)
    den_row = jnp.concatenate([den[i : i + 1] for i in range(den.shape[0])], axis=1)
    meta = jnp.concatenate(
        [den_row, ray_high.astype(F32), ray_low.astype(F32), jnp.zeros((META_ROWS - 3, cells), F32)],
        axis=0,
    ).astype(BF16)
    base = (iota((block, cells), 0) == within).astype(F32).astype(BF16)
    masks = [(target == t).astype(F32).astype(BF16) for t in range(targets)]
    place = jnp.concatenate([base * mask for mask in masks], axis=0)
    moved = nt_dot(jnp.concatenate([meta * mask for mask in masks], axis=0), base).astype(BF16)
    copies[3].wait()
    rows = jnp.dot(place, src_ref[...], preferred_element_type=F32).astype(BF16)
    out[:, :block, :] = rows.reshape(targets, block, levels)
    out[:, block:, :] = jnp.zeros((targets, META_ROWS, levels), BF16)
    for t in range(targets):
        out[t, block:, :block] = moved[t * META_ROWS : (t + 1) * META_ROWS]

    @pl.when(me_ref[0] % 2 == 1)
    def _():
        width = line_out.shape[1] // LINE_PARTS
        for i in range(LINE_PARTS):
            part = pl.ds(i * width, width)
            copy = pltpu.make_async_copy(
                line_hbm.at[:, part], line_out.at[:, part], line_sems.at[i]
            )
            copy.start()
            copy.wait()


def window_kernel(me_ref, arrived_ref, loaded_ref, table_hbm, line_hbm, powers_ref, line_ref, sems):
    levels = arrived_ref.shape[0]
    even = me_ref[0] % 2 == 0
    table_copy = pltpu.make_async_copy(table_hbm, powers_ref.at[0, :, pl.ds(0, levels)], sems.at[0])
    line_copy = pltpu.make_async_copy(line_hbm, line_ref, sems.at[1])
    table_copy.start()

    @pl.when(even)
    def _():
        line_copy.start()

    @pl.when(jnp.logical_not(even))
    def _():
        line_ref[...] = loaded_ref[...]

    powers_ref[1, :, :levels] = arrived_ref[...]
    table_copy.wait()
    for part in range(2):
        table = powers_ref[part, :, :levels]
        square = jnp.dot(table, table, preferred_element_type=F32)
        powers_ref[part, :, levels:] = square.astype(BF16)

    @pl.when(even)
    def _():
        line_copy.wait()


def level_kernel(plan, rays, got_ref, powers_ref, out_ref):
    targets, block = plan.targets, plan.block
    meta = [got_ref[s, block:, :block].astype(F32) for s in range(targets)]
    columns = [jnp.transpose(m[:8]) for m in meta]
    total = jnp.zeros(out_ref.shape, F32)
    levels = got_ref.shape[2]
    for part in range(2):
        low, high = part * plan.capacity, (part + 1) * plan.capacity
        src = got_ref[:, low:high, :].reshape(targets * plan.capacity, got_ref.shape[2])
        den = jnp.concatenate([c[low:high, 0:1] for c in columns], axis=0)
        ray = jnp.concatenate(
            [m[1:2, low:high] * RAY_BASE + m[2:3, low:high] for m in meta], axis=1
        ).astype(I32)
        wide = src.astype(F32)
        steps = jnp.dot(src, powers_ref[part], preferred_element_type=F32)
        pops = (wide + den * (steps[:, :levels] + den * steps[:, levels:])).astype(BF16)
        pick = (iota((rays, src.shape[0]), 0) == ray).astype(F32).astype(BF16)
        total = total + jnp.dot(pick, pops, preferred_element_type=F32)
    out_ref[...] = total.astype(BF16)


def line_kernel(mine_ref, theirs_ref, line_ref, out_hbm, out_ref, sems):
    sums = mine_ref[...] + theirs_ref[...]
    rows = sums.shape[0]
    high = sums.astype(BF16)
    low = (sums - high.astype(F32)).astype(BF16)
    both = jnp.concatenate([high, low], axis=0)
    chunks = sems.shape[0]
    width = out_ref.shape[1] // chunks
    copies = []
    for i in range(chunks):
        part = pl.ds(i * width, width)
        got = jnp.dot(both, line_ref[:, part], preferred_element_type=F32)
        out_ref[:, part] = got[:rows] + got[rows:]
        copies.append(pltpu.make_async_copy(out_ref.at[:, part], out_hbm.at[:, part], sems.at[i]))
        copies[-1].start()
    for copy in copies:
        copy.wait()


class Plan:
    def __init__(self, bin_total, wave_total, cells):
        self.bins = bin_total
        self.wave = wave_total
        self.targets = bin_total // 2
        self.capacity = max(2, 2 * cells // bin_total)
        self.block = 2 * self.capacity

    def table_moves(self):
        return [(i, (i + self.targets) % self.bins) for i in range(self.bins)]

    def halves(self):
        return [list(range(self.targets)), list(range(self.targets, self.bins))]


def per_device(sources, density, temp_bins, ray_index, rate_tables, line_table):
    cells, levels = sources.shape
    bin_total = lax.axis_size("bin")
    wave_total = lax.axis_size("wave")
    plan = Plan(bin_total, wave_total, cells)
    rows = plan.block + META_ROWS
    params = pltpu.CompilerParams(vmem_limit_bytes=VMEM_LIMIT)
    vmem = pl.BlockSpec(memory_space=pltpu.VMEM)
    smem = pl.BlockSpec(memory_space=pltpu.SMEM)
    hbm = pl.BlockSpec(memory_space=pltpu.HBM)

    def in_hbm(x):
        return pltpu.with_memory_space_constraint(x, pltpu.HBM)

    arrived = lax.ppermute(rate_tables[0], "bin", plan.table_moves())
    me = lax.axis_index(("bin", "wave")).astype(I32).reshape(1)
    den_rows = cells // min(cells, LANES)
    outgoing, loaded = pl.pallas_call(
        functools.partial(pack_kernel, plan),
        out_shape=[
            jax.ShapeDtypeStruct(a, BF16) for a in ((plan.targets, rows, levels), line_table.shape)
        ],
        in_specs=[smem] + [hbm] * 5,
        out_specs=[vmem] * 2,
        scratch_shapes=[
            pltpu.VMEM((cells, levels), BF16),
            pltpu.VMEM((den_rows, cells // den_rows), BF16),
            pltpu.VMEM((1, cells), I32),
            pltpu.VMEM((1, cells), I32),
            pltpu.SemaphoreType.DMA((4,)),
            pltpu.SemaphoreType.DMA((LINE_PARTS,)),
        ],
        compiler_params=params,
    )(
        me,
        in_hbm(sources),
        in_hbm(density.reshape(den_rows, cells // den_rows)),
        in_hbm(temp_bins.reshape(1, cells)),
        in_hbm(ray_index.reshape(1, cells)),
        in_hbm(line_table),
    )
    got = lax.all_to_all(
        outgoing, "bin", split_axis=0, concat_axis=0, tiled=True, axis_index_groups=plan.halves()
    )
    powers, held_line = pl.pallas_call(
        window_kernel,
        out_shape=[
            jax.ShapeDtypeStruct(a, BF16) for a in ((2, levels, 2 * levels), line_table.shape)
        ],
        in_specs=[smem, vmem, vmem, hbm, hbm],
        out_specs=[vmem] * 2,
        scratch_shapes=[pltpu.SemaphoreType.DMA((2,))],
        compiler_params=params,
        cost_estimate=pl.CostEstimate(
            flops=OVERLAP_FLOPS, bytes_accessed=4 * arrived.size, transcendentals=0
        ),
    )(me, arrived, loaded, in_hbm(rate_tables[0]), in_hbm(line_table))
    ray_rows = RAY_DEV
    rays = ray_rows * bin_total
    partial_sums = pl.pallas_call(
        functools.partial(level_kernel, plan, rays),
        out_shape=jax.ShapeDtypeStruct((rays, levels), BF16),
        in_specs=[vmem] * 2,
        out_specs=vmem,
        compiler_params=params,
    )(got, powers)
    held = lax.all_to_all(
        partial_sums.reshape(bin_total, ray_rows, levels),
        "bin",
        split_axis=0,
        concat_axis=0,
        tiled=True,
    )
    total = jnp.sum(held.astype(F32), axis=0)
    theirs = jnp.zeros_like(total)
    step = 1
    while step < wave_total:
        total = total + theirs if step > 1 else total
        theirs = lax.ppermute(total, "wave", [(i, i ^ step) for i in range(wave_total)])
        step *= 2
    out_shape = (ray_rows, line_table.shape[1])
    return pl.pallas_call(
        line_kernel,
        out_shape=jax.ShapeDtypeStruct(out_shape, F32),
        in_specs=[vmem, vmem, vmem],
        out_specs=hbm,
        scratch_shapes=[pltpu.VMEM(out_shape, F32), pltpu.SemaphoreType.DMA((LINE_CHUNKS,))],
        compiler_params=params,
    )(total, theirs, held_line)


def solution(mesh):
    in_specs = (
        P(("bin", "wave"), None),
        P(("bin", "wave")),
        P(("bin", "wave"), None),
        P(("bin", "wave")),
        P("bin", None, None),
        P(None, "wave"),
    )
    return jax.shard_map(
        per_device, mesh=mesh, in_specs=in_specs, out_specs=P("bin", "wave"), check_vma=False
    )
```

```python
import functools

import jax
import jax.numpy as jnp
from jax import lax
from jax.experimental import pallas as pl
from jax.experimental.pallas import tpu as pltpu
from jax.sharding import PartitionSpec as P

RAY_DEV = 16
META_ROWS = 8
RAY_BASE = 32
LANES = 128
LINE_CHUNKS = 4
OVERLAP_FLOPS = 10**10
VMEM_LIMIT = 32 * 1024 * 1024
F32 = jnp.float32
BF16 = jnp.bfloat16
I32 = jnp.int32


def nt_dot(a, b):
    return lax.dot_general(a, b, (((1,), (1,)), ((), ())), preferred_element_type=F32)


def iota(shape, dim):
    return lax.broadcasted_iota(I32, shape, dim)


def pack_kernel(plan, me_ref, src_hbm, den_hbm, bin_hbm, ray_hbm, *rest):
    targets, block = plan.targets, plan.block
    out, src_ref, den_ref, bin_ref, ray_ref, sems = rest
    copies = [
        pltpu.make_async_copy(a, b, sems.at[i])
        for i, (a, b) in enumerate(
            (
                (bin_hbm, bin_ref),
                (ray_hbm, ray_ref),
                (den_hbm, den_ref),
                (src_hbm, src_ref),
            )
        )
    ]
    for copy in copies:
        copy.start()
    cells, levels = src_ref.shape
    lanes = min(cells, LANES)
    earlier = (iota((lanes, lanes), 0) < iota((lanes, lanes), 1)).astype(F32).astype(BF16)
    my_half = me_ref[0] // targets
    for copy in copies[:3]:
        copy.wait()
    bins = bin_ref[...]
    hot = (iota((plan.bins, cells), 0) == bins).astype(F32)
    parts = [hot[:, i : i + lanes] for i in range(0, cells, lanes)]
    ranks = jnp.dot(
        jnp.concatenate(parts, axis=0).astype(BF16), earlier, preferred_element_type=F32
    )
    sofar = jnp.zeros((plan.bins, 1), F32)
    places = []
    for i, part in enumerate(parts):
        rank = ranks[i * plan.bins : (i + 1) * plan.bins] + sofar
        places.append(jnp.sum(part * rank, axis=0, keepdims=True))
        sofar = sofar + jnp.sum(part, axis=1, keepdims=True)
    position = jnp.concatenate(places, axis=1).astype(I32)
    half = bins // targets
    target = bins - half * targets
    within = (half ^ my_half) * plan.capacity + position
    rays = ray_ref[...]
    ray_high = rays // RAY_BASE
    ray_low = rays - ray_high * RAY_BASE
    den = den_ref[...].astype(F32)
    den_row = jnp.concatenate([den[i : i + 1] for i in range(den.shape[0])], axis=1)
    meta = jnp.concatenate(
        [den_row, ray_high.astype(F32), ray_low.astype(F32), jnp.zeros((META_ROWS - 3, cells), F32)],
        axis=0,
    ).astype(BF16)
    base = (iota((block, cells), 0) == within).astype(F32).astype(BF16)
    masks = [(target == t).astype(F32).astype(BF16) for t in range(targets)]
    place = jnp.concatenate([base * mask for mask in masks], axis=0)
    moved = nt_dot(jnp.concatenate([meta * mask for mask in masks], axis=0), base).astype(BF16)
    copies[3].wait()
    rows = jnp.dot(place, src_ref[...], preferred_element_type=F32).astype(BF16)
    out[:, :block, :] = rows.reshape(targets, block, levels)
    out[:, block:, :] = jnp.zeros((targets, META_ROWS, levels), BF16)
    for t in range(targets):
        out[t, block:, :block] = moved[t * META_ROWS : (t + 1) * META_ROWS]


def window_kernel(arrived_ref, table_hbm, line_hbm, powers_ref, line_ref, sems):
    levels = arrived_ref.shape[0]
    copies = [
        pltpu.make_async_copy(table_hbm, powers_ref.at[0, :, pl.ds(0, levels)], sems.at[0]),
        pltpu.make_async_copy(line_hbm, line_ref, sems.at[1]),
    ]
    for copy in copies:
        copy.start()
    powers_ref[1, :, :levels] = arrived_ref[...]
    copies[0].wait()
    for part in range(2):
        table = powers_ref[part, :, :levels]
        square = jnp.dot(table, table, preferred_element_type=F32)
        powers_ref[part, :, levels:] = square.astype(BF16)
    copies[1].wait()


def level_kernel(plan, rays, got_ref, powers_ref, out_ref):
    targets, block = plan.targets, plan.block
    meta = [got_ref[s, block:, :block].astype(F32) for s in range(targets)]
    columns = [jnp.transpose(m[:8]) for m in meta]
    total = jnp.zeros(out_ref.shape, F32)
    levels = got_ref.shape[2]
    for part in range(2):
        low, high = part * plan.capacity, (part + 1) * plan.capacity
        src = got_ref[:, low:high, :].reshape(targets * plan.capacity, got_ref.shape[2])
        den = jnp.concatenate([c[low:high, 0:1] for c in columns], axis=0)
        ray = jnp.concatenate(
            [m[1:2, low:high] * RAY_BASE + m[2:3, low:high] for m in meta], axis=1
        ).astype(I32)
        wide = src.astype(F32)
        steps = jnp.dot(src, powers_ref[part], preferred_element_type=F32)
        pops = (wide + den * (steps[:, :levels] + den * steps[:, levels:])).astype(BF16)
        pick = (iota((rays, src.shape[0]), 0) == ray).astype(F32).astype(BF16)
        total = total + jnp.dot(pick, pops, preferred_element_type=F32)
    out_ref[...] = total.astype(BF16)


def line_kernel(mine_ref, theirs_ref, line_ref, out_hbm, out_ref, sems):
    sums = mine_ref[...] + theirs_ref[...]
    rows = sums.shape[0]
    high = sums.astype(BF16)
    low = (sums - high.astype(F32)).astype(BF16)
    both = jnp.concatenate([high, low], axis=0)
    chunks = sems.shape[0]
    width = out_ref.shape[1] // chunks
    copies = []
    for i in range(chunks):
        part = pl.ds(i * width, width)
        got = jnp.dot(both, line_ref[:, part], preferred_element_type=F32)
        out_ref[:, part] = got[:rows] + got[rows:]
        copies.append(pltpu.make_async_copy(out_ref.at[:, part], out_hbm.at[:, part], sems.at[i]))
        copies[-1].start()
    for copy in copies:
        copy.wait()


class Plan:
    def __init__(self, bin_total, wave_total, cells):
        self.bins = bin_total
        self.wave = wave_total
        self.targets = bin_total // 2
        self.capacity = max(2, 2 * cells // bin_total)
        self.block = 2 * self.capacity

    def table_moves(self):
        return [(i, (i + self.targets) % self.bins) for i in range(self.bins)]

    def groups(self, size):
        return [
            [b * self.wave + (w ^ (bin(b).count("1") % 2)) for b in range(first, first + size)]
            for first in range(0, self.bins, size)
            for w in range(self.wave)
        ]


def per_device(sources, density, temp_bins, ray_index, rate_tables, line_table):
    cells, levels = sources.shape
    bin_total = lax.axis_size("bin")
    wave_total = lax.axis_size("wave")
    plan = Plan(bin_total, wave_total, cells)
    rows = plan.block + META_ROWS
    params = pltpu.CompilerParams(vmem_limit_bytes=VMEM_LIMIT)
    vmem = pl.BlockSpec(memory_space=pltpu.VMEM)
    smem = pl.BlockSpec(memory_space=pltpu.SMEM)
    hbm = pl.BlockSpec(memory_space=pltpu.HBM)
    both = ("bin", "wave")

    def in_hbm(x):
        return pltpu.with_memory_space_constraint(x, pltpu.HBM)

    arrived = lax.ppermute(rate_tables[0], "bin", plan.table_moves())
    me = lax.axis_index("bin").astype(I32).reshape(1)
    den_rows = cells // min(cells, LANES)
    outgoing = pl.pallas_call(
        functools.partial(pack_kernel, plan),
        out_shape=jax.ShapeDtypeStruct((plan.targets, rows, levels), BF16),
        in_specs=[smem] + [hbm] * 4,
        out_specs=vmem,
        scratch_shapes=[
            pltpu.VMEM((cells, levels), BF16),
            pltpu.VMEM((den_rows, cells // den_rows), BF16),
            pltpu.VMEM((1, cells), I32),
            pltpu.VMEM((1, cells), I32),
            pltpu.SemaphoreType.DMA((4,)),
        ],
        compiler_params=params,
    )(
        me,
        in_hbm(sources),
        in_hbm(density.reshape(den_rows, cells // den_rows)),
        in_hbm(temp_bins.reshape(1, cells)),
        in_hbm(ray_index.reshape(1, cells)),
    )
    got = lax.all_to_all(
        outgoing,
        both,
        split_axis=0,
        concat_axis=0,
        tiled=True,
        axis_index_groups=plan.groups(plan.targets),
    )
    powers, held_line = pl.pallas_call(
        window_kernel,
        out_shape=[
            jax.ShapeDtypeStruct(a, BF16) for a in ((2, levels, 2 * levels), line_table.shape)
        ],
        in_specs=[vmem, hbm, hbm],
        out_specs=[vmem] * 2,
        scratch_shapes=[pltpu.SemaphoreType.DMA((2,))],
        compiler_params=params,
        cost_estimate=pl.CostEstimate(
            flops=OVERLAP_FLOPS, bytes_accessed=4 * arrived.size, transcendentals=0
        ),
    )(arrived, in_hbm(rate_tables[0]), in_hbm(line_table))
    ray_rows = RAY_DEV
    rays = ray_rows * bin_total
    partial_sums = pl.pallas_call(
        functools.partial(level_kernel, plan, rays),
        out_shape=jax.ShapeDtypeStruct((rays, levels), BF16),
        in_specs=[vmem] * 2,
        out_specs=vmem,
        compiler_params=params,
    )(got, powers)
    held = lax.all_to_all(
        partial_sums.reshape(bin_total, ray_rows, levels),
        both,
        split_axis=0,
        concat_axis=0,
        tiled=True,
        axis_index_groups=plan.groups(bin_total),
    )
    total = jnp.sum(held.astype(F32), axis=0)
    theirs = jnp.zeros_like(total)
    step = 1
    while step < wave_total:
        total = total + theirs if step > 1 else total
        theirs = lax.ppermute(total, "wave", [(i, i ^ step) for i in range(wave_total)])
        step *= 2
    out_shape = (ray_rows, line_table.shape[1])
    return pl.pallas_call(
        line_kernel,
        out_shape=jax.ShapeDtypeStruct(out_shape, F32),
        in_specs=[vmem, vmem, vmem],
        out_specs=hbm,
        scratch_shapes=[pltpu.VMEM(out_shape, F32), pltpu.SemaphoreType.DMA((LINE_CHUNKS,))],
        compiler_params=params,
    )(total, theirs, held_line)


def solution(mesh):
    in_specs = (
        P(("bin", "wave"), None),
        P(("bin", "wave")),
        P(("bin", "wave"), None),
        P(("bin", "wave")),
        P("bin", None, None),
        P(None, "wave"),
    )
    return jax.shard_map(
        per_device, mesh=mesh, in_specs=in_specs, out_specs=P("bin", "wave"), check_vma=False
    )
```

```python
import functools

import jax
import jax.numpy as jnp
from jax import lax
from jax.experimental import pallas as pl
from jax.experimental.pallas import tpu as pltpu
from jax.sharding import PartitionSpec as P

RAY_DEV = 16
META_ROWS = 8
RAY_BASE = 32
LANES = 128
LINE_CHUNKS = 4
PACK_GROUPS = 2
OVERLAP_FLOPS = 10**10
VMEM_LIMIT = 32 * 1024 * 1024
F32 = jnp.float32
BF16 = jnp.bfloat16
I32 = jnp.int32


def nt_dot(a, b):
    return lax.dot_general(a, b, (((1,), (1,)), ((), ())), preferred_element_type=F32)


def iota(shape, dim):
    return lax.broadcasted_iota(I32, shape, dim)


def pack_kernel(plan, me_ref, src_hbm, den_hbm, bin_hbm, ray_hbm, *rest):
    targets, block = plan.targets, plan.block
    out_hbm, src_ref, den_ref, bin_ref, ray_ref, held, sems, out_sems = rest
    copies = [
        pltpu.make_async_copy(a, b, sems.at[i])
        for i, (a, b) in enumerate(
            (
                (bin_hbm, bin_ref),
                (ray_hbm, ray_ref),
                (den_hbm, den_ref),
                (src_hbm, src_ref),
            )
        )
    ]
    for copy in copies:
        copy.start()
    cells, levels = src_ref.shape
    lanes = min(cells, LANES)
    earlier = (iota((lanes, lanes), 0) < iota((lanes, lanes), 1)).astype(F32).astype(BF16)
    my_half = me_ref[0] // targets
    for copy in copies[:3]:
        copy.wait()
    bins = bin_ref[...]
    hot = (iota((plan.bins, cells), 0) == bins).astype(F32)
    parts = [hot[:, i : i + lanes] for i in range(0, cells, lanes)]
    ranks = jnp.dot(
        jnp.concatenate(parts, axis=0).astype(BF16), earlier, preferred_element_type=F32
    )
    sofar = jnp.zeros((plan.bins, 1), F32)
    places = []
    for i, part in enumerate(parts):
        rank = ranks[i * plan.bins : (i + 1) * plan.bins] + sofar
        places.append(jnp.sum(part * rank, axis=0, keepdims=True))
        sofar = sofar + jnp.sum(part, axis=1, keepdims=True)
    position = jnp.concatenate(places, axis=1).astype(I32)
    half = bins // targets
    target = bins - half * targets
    within = (half ^ my_half) * plan.capacity + position
    rays = ray_ref[...]
    ray_high = rays // RAY_BASE
    ray_low = rays - ray_high * RAY_BASE
    den = den_ref[...].astype(F32)
    den_row = jnp.concatenate([den[i : i + 1] for i in range(den.shape[0])], axis=1)
    meta = jnp.concatenate(
        [den_row, ray_high.astype(F32), ray_low.astype(F32), jnp.zeros((META_ROWS - 3, cells), F32)],
        axis=0,
    ).astype(BF16)
    base = (iota((block, cells), 0) == within).astype(F32).astype(BF16)
    masks = [(target == t).astype(F32).astype(BF16) for t in range(targets)]
    moved = nt_dot(jnp.concatenate([meta * mask for mask in masks], axis=0), base).astype(BF16)
    held[:, block:, :] = jnp.zeros((targets, META_ROWS, levels), BF16)
    for t in range(targets):
        held[t, block:, :block] = moved[t * META_ROWS : (t + 1) * META_ROWS]
    copies[3].wait()
    src = src_ref[...]
    size = max(1, targets // PACK_GROUPS)
    leaving = []
    for first in range(0, targets, size):
        place = jnp.concatenate([base * mask for mask in masks[first : first + size]], axis=0)
        rows = jnp.dot(place, src, preferred_element_type=F32).astype(BF16)
        part = pl.ds(first, size)
        held[part, :block, :] = rows.reshape(size, block, levels)
        copy = pltpu.make_async_copy(held.at[part], out_hbm.at[part], out_sems.at[len(leaving)])
        copy.start()
        leaving.append(copy)
    for copy in leaving:
        copy.wait()


def window_kernel(arrived_ref, table_hbm, line_hbm, powers_ref, line_ref, sems):
    levels = arrived_ref.shape[0]
    copies = [
        pltpu.make_async_copy(table_hbm, powers_ref.at[0, :, pl.ds(0, levels)], sems.at[0]),
        pltpu.make_async_copy(line_hbm, line_ref, sems.at[1]),
    ]
    for copy in copies:
        copy.start()
    powers_ref[1, :, :levels] = arrived_ref[...]
    copies[0].wait()
    for part in range(2):
        table = powers_ref[part, :, :levels]
        square = jnp.dot(table, table, preferred_element_type=F32)
        powers_ref[part, :, levels:] = square.astype(BF16)
    copies[1].wait()


def level_kernel(plan, rays, got_ref, powers_ref, out_ref):
    targets, block = plan.targets, plan.block
    meta = [got_ref[s, block:, :block].astype(F32) for s in range(targets)]
    columns = [jnp.transpose(m[:8]) for m in meta]
    total = jnp.zeros(out_ref.shape, F32)
    levels = got_ref.shape[2]
    for part in range(2):
        low, high = part * plan.capacity, (part + 1) * plan.capacity
        src = got_ref[:, low:high, :].reshape(targets * plan.capacity, got_ref.shape[2])
        den = jnp.concatenate([c[low:high, 0:1] for c in columns], axis=0)
        ray = jnp.concatenate(
            [m[1:2, low:high] * RAY_BASE + m[2:3, low:high] for m in meta], axis=1
        ).astype(I32)
        wide = src.astype(F32)
        steps = jnp.dot(src, powers_ref[part], preferred_element_type=F32)
        pops = (wide + den * (steps[:, :levels] + den * steps[:, levels:])).astype(BF16)
        pick = (iota((rays, src.shape[0]), 0) == ray).astype(F32).astype(BF16)
        total = total + jnp.dot(pick, pops, preferred_element_type=F32)
    out_ref[...] = total.astype(BF16)


def line_kernel(mine_ref, theirs_ref, line_ref, out_hbm, out_ref, sems):
    sums = mine_ref[...] + theirs_ref[...]
    rows = sums.shape[0]
    high = sums.astype(BF16)
    low = (sums - high.astype(F32)).astype(BF16)
    both = jnp.concatenate([high, low], axis=0)
    chunks = sems.shape[0]
    width = out_ref.shape[1] // chunks
    copies = []
    for i in range(chunks):
        part = pl.ds(i * width, width)
        got = jnp.dot(both, line_ref[:, part], preferred_element_type=F32)
        out_ref[:, part] = got[:rows] + got[rows:]
        copies.append(pltpu.make_async_copy(out_ref.at[:, part], out_hbm.at[:, part], sems.at[i]))
        copies[-1].start()
    for copy in copies:
        copy.wait()


class Plan:
    def __init__(self, bin_total, cells):
        self.bins = bin_total
        self.targets = bin_total // 2
        self.capacity = max(2, 2 * cells // bin_total)
        self.block = 2 * self.capacity

    def table_moves(self):
        return [(i, (i + self.targets) % self.bins) for i in range(self.bins)]

    def halves(self):
        return [list(range(self.targets)), list(range(self.targets, self.bins))]


def per_device(sources, density, temp_bins, ray_index, rate_tables, line_table):
    cells, levels = sources.shape
    bin_total = lax.axis_size("bin")
    wave_total = lax.axis_size("wave")
    plan = Plan(bin_total, cells)
    rows = plan.block + META_ROWS
    params = pltpu.CompilerParams(vmem_limit_bytes=VMEM_LIMIT)
    vmem = pl.BlockSpec(memory_space=pltpu.VMEM)
    smem = pl.BlockSpec(memory_space=pltpu.SMEM)
    hbm = pl.BlockSpec(memory_space=pltpu.HBM)

    def in_hbm(x):
        return pltpu.with_memory_space_constraint(x, pltpu.HBM)

    arrived = lax.ppermute(rate_tables[0], "bin", plan.table_moves())
    me = lax.axis_index("bin").astype(I32).reshape(1)
    den_rows = cells // min(cells, LANES)
    outgoing = pl.pallas_call(
        functools.partial(pack_kernel, plan),
        out_shape=jax.ShapeDtypeStruct((plan.targets, rows, levels), BF16),
        in_specs=[smem] + [hbm] * 4,
        out_specs=hbm,
        scratch_shapes=[
            pltpu.VMEM((cells, levels), BF16),
            pltpu.VMEM((den_rows, cells // den_rows), BF16),
            pltpu.VMEM((1, cells), I32),
            pltpu.VMEM((1, cells), I32),
            pltpu.VMEM((plan.targets, rows, levels), BF16),
            pltpu.SemaphoreType.DMA((4,)),
            pltpu.SemaphoreType.DMA((PACK_GROUPS,)),
        ],
        compiler_params=params,
    )(
        me,
        in_hbm(sources),
        in_hbm(density.reshape(den_rows, cells // den_rows)),
        in_hbm(temp_bins.reshape(1, cells)),
        in_hbm(ray_index.reshape(1, cells)),
    )
    got = lax.all_to_all(
        outgoing, "bin", split_axis=0, concat_axis=0, tiled=True, axis_index_groups=plan.halves()
    )
    powers, held_line = pl.pallas_call(
        window_kernel,
        out_shape=[
            jax.ShapeDtypeStruct(a, BF16) for a in ((2, levels, 2 * levels), line_table.shape)
        ],
        in_specs=[vmem, hbm, hbm],
        out_specs=[vmem] * 2,
        scratch_shapes=[pltpu.SemaphoreType.DMA((2,))],
        compiler_params=params,
        cost_estimate=pl.CostEstimate(
            flops=OVERLAP_FLOPS, bytes_accessed=4 * arrived.size, transcendentals=0
        ),
    )(arrived, in_hbm(rate_tables[0]), in_hbm(line_table))
    ray_rows = RAY_DEV
    rays = ray_rows * bin_total
    partial_sums = pl.pallas_call(
        functools.partial(level_kernel, plan, rays),
        out_shape=jax.ShapeDtypeStruct((rays, levels), BF16),
        in_specs=[vmem] * 2,
        out_specs=vmem,
        compiler_params=params,
    )(got, powers)
    held = lax.all_to_all(
        partial_sums.reshape(bin_total, ray_rows, levels),
        "bin",
        split_axis=0,
        concat_axis=0,
        tiled=True,
    )
    total = jnp.sum(held.astype(F32), axis=0)
    theirs = jnp.zeros_like(total)
    step = 1
    while step < wave_total:
        total = total + theirs if step > 1 else total
        theirs = lax.ppermute(total, "wave", [(i, i ^ step) for i in range(wave_total)])
        step *= 2
    out_shape = (ray_rows, line_table.shape[1])
    return pl.pallas_call(
        line_kernel,
        out_shape=jax.ShapeDtypeStruct(out_shape, F32),
        in_specs=[vmem, vmem, vmem],
        out_specs=hbm,
        scratch_shapes=[pltpu.VMEM(out_shape, F32), pltpu.SemaphoreType.DMA((LINE_CHUNKS,))],
        compiler_params=params,
    )(total, theirs, held_line)


def solution(mesh):
    in_specs = (
        P(("bin", "wave"), None),
        P(("bin", "wave")),
        P(("bin", "wave"), None),
        P(("bin", "wave")),
        P("bin", None, None),
        P(None, "wave"),
    )
    return jax.shard_map(
        per_device, mesh=mesh, in_specs=in_specs, out_specs=P("bin", "wave"), check_vma=False
    )
```

```python
import functools

import jax
import jax.numpy as jnp
from jax import lax
from jax.experimental import pallas as pl
from jax.experimental.pallas import tpu as pltpu
from jax.sharding import PartitionSpec as P

RAY_DEV = 16
META_ROWS = 8
RAY_BASE = 32
LANES = 128
LINE_CHUNKS = 4
OVERLAP_FLOPS = 10**10
VMEM_LIMIT = 32 * 1024 * 1024
F32 = jnp.float32
BF16 = jnp.bfloat16
I32 = jnp.int32


def nt_dot(a, b):
    return lax.dot_general(a, b, (((1,), (1,)), ((), ())), preferred_element_type=F32)


def iota(shape, dim):
    return lax.broadcasted_iota(I32, shape, dim)


def gray_place(index, size):
    place, shift = index, 1
    while 1 << shift < size:
        place = place ^ (index >> shift)
        shift += 1
    return place


def pack_kernel(plan, me_ref, src_hbm, den_hbm, bin_hbm, ray_hbm, *rest):
    targets, block = plan.targets, plan.block
    out, src_ref, den_ref, bin_ref, ray_ref, sems = rest
    copies = [
        pltpu.make_async_copy(a, b, sems.at[i])
        for i, (a, b) in enumerate(
            (
                (bin_hbm, bin_ref),
                (ray_hbm, ray_ref),
                (den_hbm, den_ref),
                (src_hbm, src_ref),
            )
        )
    ]
    for copy in copies:
        copy.start()
    cells, levels = src_ref.shape
    lanes = min(cells, LANES)
    earlier = (iota((lanes, lanes), 0) < iota((lanes, lanes), 1)).astype(F32).astype(BF16)
    my_half = me_ref[0] // targets
    for copy in copies[:3]:
        copy.wait()
    bins = bin_ref[...]
    hot = (iota((plan.bins, cells), 0) == bins).astype(F32)
    parts = [hot[:, i : i + lanes] for i in range(0, cells, lanes)]
    ranks = jnp.dot(
        jnp.concatenate(parts, axis=0).astype(BF16), earlier, preferred_element_type=F32
    )
    sofar = jnp.zeros((plan.bins, 1), F32)
    places = []
    for i, part in enumerate(parts):
        rank = ranks[i * plan.bins : (i + 1) * plan.bins] + sofar
        places.append(jnp.sum(part * rank, axis=0, keepdims=True))
        sofar = sofar + jnp.sum(part, axis=1, keepdims=True)
    position = jnp.concatenate(places, axis=1).astype(I32)
    half = bins // targets
    target = gray_place(bins - half * targets, targets)
    within = (half ^ my_half) * plan.capacity + position
    rays = ray_ref[...]
    ray_high = rays // RAY_BASE
    ray_low = rays - ray_high * RAY_BASE
    den = den_ref[...].astype(F32)
    den_row = jnp.concatenate([den[i : i + 1] for i in range(den.shape[0])], axis=1)
    meta = jnp.concatenate(
        [den_row, ray_high.astype(F32), ray_low.astype(F32), jnp.zeros((META_ROWS - 3, cells), F32)],
        axis=0,
    ).astype(BF16)
    base = (iota((block, cells), 0) == within).astype(F32).astype(BF16)
    masks = [(target == t).astype(F32).astype(BF16) for t in range(targets)]
    place = jnp.concatenate([base * mask for mask in masks], axis=0)
    moved = nt_dot(jnp.concatenate([meta * mask for mask in masks], axis=0), base).astype(BF16)
    copies[3].wait()
    rows = jnp.dot(place, src_ref[...], preferred_element_type=F32).astype(BF16)
    out[:, :block, :] = rows.reshape(targets, block, levels)
    out[:, block:, :] = jnp.zeros((targets, META_ROWS, levels), BF16)
    for t in range(targets):
        out[t, block:, :block] = moved[t * META_ROWS : (t + 1) * META_ROWS]


def window_kernel(arrived_ref, table_hbm, line_hbm, powers_ref, line_ref, sems):
    levels = arrived_ref.shape[0]
    copies = [
        pltpu.make_async_copy(table_hbm, powers_ref.at[0, :, pl.ds(0, levels)], sems.at[0]),
        pltpu.make_async_copy(line_hbm, line_ref, sems.at[1]),
    ]
    for copy in copies:
        copy.start()
    powers_ref[1, :, :levels] = arrived_ref[...]
    copies[0].wait()
    for part in range(2):
        table = powers_ref[part, :, :levels]
        square = jnp.dot(table, table, preferred_element_type=F32)
        powers_ref[part, :, levels:] = square.astype(BF16)
    copies[1].wait()


def level_kernel(plan, ray_rows, got_ref, powers_ref, out_ref):
    targets, block = plan.targets, plan.block
    rays = plan.bins * ray_rows
    meta = [got_ref[s, block:, :block].astype(F32) for s in range(targets)]
    columns = [jnp.transpose(m[:8]) for m in meta]
    total = jnp.zeros(out_ref.shape, F32)
    levels = got_ref.shape[2]
    for part in range(2):
        low, high = part * plan.capacity, (part + 1) * plan.capacity
        src = got_ref[:, low:high, :].reshape(targets * plan.capacity, got_ref.shape[2])
        den = jnp.concatenate([c[low:high, 0:1] for c in columns], axis=0)
        ray = jnp.concatenate(
            [m[1:2, low:high] * RAY_BASE + m[2:3, low:high] for m in meta], axis=1
        ).astype(I32)
        owner = ray // ray_rows
        row = gray_place(owner, plan.bins) * ray_rows + (ray - owner * ray_rows)
        wide = src.astype(F32)
        steps = jnp.dot(src, powers_ref[part], preferred_element_type=F32)
        pops = (wide + den * (steps[:, :levels] + den * steps[:, levels:])).astype(BF16)
        pick = (iota((rays, src.shape[0]), 0) == row).astype(F32).astype(BF16)
        total = total + jnp.dot(pick, pops, preferred_element_type=F32)
    out_ref[...] = total.astype(BF16)


def line_kernel(mine_ref, theirs_ref, line_ref, out_hbm, out_ref, sems):
    sums = mine_ref[...] + theirs_ref[...]
    rows = sums.shape[0]
    high = sums.astype(BF16)
    low = (sums - high.astype(F32)).astype(BF16)
    both = jnp.concatenate([high, low], axis=0)
    chunks = sems.shape[0]
    width = out_ref.shape[1] // chunks
    copies = []
    for i in range(chunks):
        part = pl.ds(i * width, width)
        got = jnp.dot(both, line_ref[:, part], preferred_element_type=F32)
        out_ref[:, part] = got[:rows] + got[rows:]
        copies.append(pltpu.make_async_copy(out_ref.at[:, part], out_hbm.at[:, part], sems.at[i]))
        copies[-1].start()
    for copy in copies:
        copy.wait()


class Plan:
    def __init__(self, bin_total, cells):
        self.bins = bin_total
        self.targets = bin_total // 2
        self.capacity = max(2, 2 * cells // bin_total)
        self.block = 2 * self.capacity

    def table_moves(self):
        return [(i, (i + self.targets) % self.bins) for i in range(self.bins)]

    def halves(self):
        order = [i ^ (i >> 1) for i in range(self.targets)]
        return [order, [self.targets + i for i in order]]

    def everyone(self):
        return [[i ^ (i >> 1) for i in range(self.bins)]]


def per_device(sources, density, temp_bins, ray_index, rate_tables, line_table):
    cells, levels = sources.shape
    bin_total = lax.axis_size("bin")
    wave_total = lax.axis_size("wave")
    plan = Plan(bin_total, cells)
    rows = plan.block + META_ROWS
    params = pltpu.CompilerParams(vmem_limit_bytes=VMEM_LIMIT)
    vmem = pl.BlockSpec(memory_space=pltpu.VMEM)
    smem = pl.BlockSpec(memory_space=pltpu.SMEM)
    hbm = pl.BlockSpec(memory_space=pltpu.HBM)

    def in_hbm(x):
        return pltpu.with_memory_space_constraint(x, pltpu.HBM)

    arrived = lax.ppermute(rate_tables[0], "bin", plan.table_moves())
    me = lax.axis_index("bin").astype(I32).reshape(1)
    den_rows = cells // min(cells, LANES)
    outgoing = pl.pallas_call(
        functools.partial(pack_kernel, plan),
        out_shape=jax.ShapeDtypeStruct((plan.targets, rows, levels), BF16),
        in_specs=[smem] + [hbm] * 4,
        out_specs=vmem,
        scratch_shapes=[
            pltpu.VMEM((cells, levels), BF16),
            pltpu.VMEM((den_rows, cells // den_rows), BF16),
            pltpu.VMEM((1, cells), I32),
            pltpu.VMEM((1, cells), I32),
            pltpu.SemaphoreType.DMA((4,)),
        ],
        compiler_params=params,
    )(
        me,
        in_hbm(sources),
        in_hbm(density.reshape(den_rows, cells // den_rows)),
        in_hbm(temp_bins.reshape(1, cells)),
        in_hbm(ray_index.reshape(1, cells)),
    )
    got = lax.all_to_all(
        outgoing, "bin", split_axis=0, concat_axis=0, tiled=True, axis_index_groups=plan.halves()
    )
    powers, held_line = pl.pallas_call(
        window_kernel,
        out_shape=[
            jax.ShapeDtypeStruct(a, BF16) for a in ((2, levels, 2 * levels), line_table.shape)
        ],
        in_specs=[vmem, hbm, hbm],
        out_specs=[vmem] * 2,
        scratch_shapes=[pltpu.SemaphoreType.DMA((2,))],
        compiler_params=params,
        cost_estimate=pl.CostEstimate(
            flops=OVERLAP_FLOPS, bytes_accessed=4 * arrived.size, transcendentals=0
        ),
    )(arrived, in_hbm(rate_tables[0]), in_hbm(line_table))
    ray_rows = RAY_DEV
    rays = ray_rows * bin_total
    partial_sums = pl.pallas_call(
        functools.partial(level_kernel, plan, ray_rows),
        out_shape=jax.ShapeDtypeStruct((rays, levels), BF16),
        in_specs=[vmem] * 2,
        out_specs=vmem,
        compiler_params=params,
    )(got, powers)
    held = lax.all_to_all(
        partial_sums.reshape(bin_total, ray_rows, levels),
        "bin",
        split_axis=0,
        concat_axis=0,
        tiled=True,
        axis_index_groups=plan.everyone(),
    )
    total = jnp.sum(held.astype(F32), axis=0)
    theirs = jnp.zeros_like(total)
    step = 1
    while step < wave_total:
        total = total + theirs if step > 1 else total
        theirs = lax.ppermute(total, "wave", [(i, i ^ step) for i in range(wave_total)])
        step *= 2
    out_shape = (ray_rows, line_table.shape[1])
    return pl.pallas_call(
        line_kernel,
        out_shape=jax.ShapeDtypeStruct(out_shape, F32),
        in_specs=[vmem, vmem, vmem],
        out_specs=hbm,
        scratch_shapes=[pltpu.VMEM(out_shape, F32), pltpu.SemaphoreType.DMA((LINE_CHUNKS,))],
        compiler_params=params,
    )(total, theirs, held_line)


def solution(mesh):
    in_specs = (
        P(("bin", "wave"), None),
        P(("bin", "wave")),
        P(("bin", "wave"), None),
        P(("bin", "wave")),
        P("bin", None, None),
        P(None, "wave"),
    )
    return jax.shard_map(
        per_device, mesh=mesh, in_specs=in_specs, out_specs=P("bin", "wave"), check_vma=False
    )
```

```python
import functools

import jax
import jax.numpy as jnp
from jax import lax
from jax.experimental import pallas as pl
from jax.experimental.pallas import tpu as pltpu
from jax.sharding import PartitionSpec as P

RAY_DEV = 16
META_ROWS = 8
RAY_BASE = 32
LANES = 128
LINE_CHUNKS = 4
OVERLAP_FLOPS = 10**10
VMEM_LIMIT = 32 * 1024 * 1024
F32 = jnp.float32
BF16 = jnp.bfloat16
I32 = jnp.int32


def nt_dot(a, b):
    return lax.dot_general(a, b, (((1,), (1,)), ((), ())), preferred_element_type=F32)


def iota(shape, dim):
    return lax.broadcasted_iota(I32, shape, dim)


def far_place(index, size):
    return jnp.where(index < size // 2, 2 * index, 2 * (size - 1 - index) + 1)


def far_order(size):
    return [i // 2 if i % 2 == 0 else size - 1 - i // 2 for i in range(size)]


def pack_kernel(plan, me_ref, src_hbm, den_hbm, bin_hbm, ray_hbm, *rest):
    targets, block = plan.targets, plan.block
    out, src_ref, den_ref, bin_ref, ray_ref, sems = rest
    copies = [
        pltpu.make_async_copy(a, b, sems.at[i])
        for i, (a, b) in enumerate(
            (
                (bin_hbm, bin_ref),
                (ray_hbm, ray_ref),
                (den_hbm, den_ref),
                (src_hbm, src_ref),
            )
        )
    ]
    for copy in copies:
        copy.start()
    cells, levels = src_ref.shape
    lanes = min(cells, LANES)
    earlier = (iota((lanes, lanes), 0) < iota((lanes, lanes), 1)).astype(F32).astype(BF16)
    my_half = me_ref[0] // targets
    for copy in copies[:3]:
        copy.wait()
    bins = bin_ref[...]
    hot = (iota((plan.bins, cells), 0) == bins).astype(F32)
    parts = [hot[:, i : i + lanes] for i in range(0, cells, lanes)]
    ranks = jnp.dot(
        jnp.concatenate(parts, axis=0).astype(BF16), earlier, preferred_element_type=F32
    )
    sofar = jnp.zeros((plan.bins, 1), F32)
    places = []
    for i, part in enumerate(parts):
        rank = ranks[i * plan.bins : (i + 1) * plan.bins] + sofar
        places.append(jnp.sum(part * rank, axis=0, keepdims=True))
        sofar = sofar + jnp.sum(part, axis=1, keepdims=True)
    position = jnp.concatenate(places, axis=1).astype(I32)
    half = bins // targets
    target = far_place(bins - half * targets, targets)
    within = (half ^ my_half) * plan.capacity + position
    rays = ray_ref[...]
    ray_high = rays // RAY_BASE
    ray_low = rays - ray_high * RAY_BASE
    den = den_ref[...].astype(F32)
    den_row = jnp.concatenate([den[i : i + 1] for i in range(den.shape[0])], axis=1)
    meta = jnp.concatenate(
        [den_row, ray_high.astype(F32), ray_low.astype(F32), jnp.zeros((META_ROWS - 3, cells), F32)],
        axis=0,
    ).astype(BF16)
    base = (iota((block, cells), 0) == within).astype(F32).astype(BF16)
    masks = [(target == t).astype(F32).astype(BF16) for t in range(targets)]
    place = jnp.concatenate([base * mask for mask in masks], axis=0)
    moved = nt_dot(jnp.concatenate([meta * mask for mask in masks], axis=0), base).astype(BF16)
    copies[3].wait()
    rows = jnp.dot(place, src_ref[...], preferred_element_type=F32).astype(BF16)
    out[:, :block, :] = rows.reshape(targets, block, levels)
    out[:, block:, :] = jnp.zeros((targets, META_ROWS, levels), BF16)
    for t in range(targets):
        out[t, block:, :block] = moved[t * META_ROWS : (t + 1) * META_ROWS]


def window_kernel(arrived_ref, table_hbm, line_hbm, powers_ref, line_ref, sems):
    levels = arrived_ref.shape[0]
    copies = [
        pltpu.make_async_copy(table_hbm, powers_ref.at[0, :, pl.ds(0, levels)], sems.at[0]),
        pltpu.make_async_copy(line_hbm, line_ref, sems.at[1]),
    ]
    for copy in copies:
        copy.start()
    powers_ref[1, :, :levels] = arrived_ref[...]
    copies[0].wait()
    for part in range(2):
        table = powers_ref[part, :, :levels]
        square = jnp.dot(table, table, preferred_element_type=F32)
        powers_ref[part, :, levels:] = square.astype(BF16)
    copies[1].wait()


def level_kernel(plan, ray_rows, got_ref, powers_ref, out_ref):
    targets, block = plan.targets, plan.block
    rays = plan.bins * ray_rows
    meta = [got_ref[s, block:, :block].astype(F32) for s in range(targets)]
    columns = [jnp.transpose(m[:8]) for m in meta]
    total = jnp.zeros(out_ref.shape, F32)
    levels = got_ref.shape[2]
    for part in range(2):
        low, high = part * plan.capacity, (part + 1) * plan.capacity
        src = got_ref[:, low:high, :].reshape(targets * plan.capacity, got_ref.shape[2])
        den = jnp.concatenate([c[low:high, 0:1] for c in columns], axis=0)
        ray = jnp.concatenate(
            [m[1:2, low:high] * RAY_BASE + m[2:3, low:high] for m in meta], axis=1
        ).astype(I32)
        owner = ray // ray_rows
        row = far_place(owner, plan.bins) * ray_rows + (ray - owner * ray_rows)
        wide = src.astype(F32)
        steps = jnp.dot(src, powers_ref[part], preferred_element_type=F32)
        pops = (wide + den * (steps[:, :levels] + den * steps[:, levels:])).astype(BF16)
        pick = (iota((rays, src.shape[0]), 0) == row).astype(F32).astype(BF16)
        total = total + jnp.dot(pick, pops, preferred_element_type=F32)
    out_ref[...] = total.astype(BF16)


def line_kernel(mine_ref, theirs_ref, line_ref, out_hbm, out_ref, sems):
    sums = mine_ref[...] + theirs_ref[...]
    rows = sums.shape[0]
    high = sums.astype(BF16)
    low = (sums - high.astype(F32)).astype(BF16)
    both = jnp.concatenate([high, low], axis=0)
    chunks = sems.shape[0]
    width = out_ref.shape[1] // chunks
    copies = []
    for i in range(chunks):
        part = pl.ds(i * width, width)
        got = jnp.dot(both, line_ref[:, part], preferred_element_type=F32)
        out_ref[:, part] = got[:rows] + got[rows:]
        copies.append(pltpu.make_async_copy(out_ref.at[:, part], out_hbm.at[:, part], sems.at[i]))
        copies[-1].start()
    for copy in copies:
        copy.wait()


class Plan:
    def __init__(self, bin_total, cells):
        self.bins = bin_total
        self.targets = bin_total // 2
        self.capacity = max(2, 2 * cells // bin_total)
        self.block = 2 * self.capacity

    def table_moves(self):
        return [(i, (i + self.targets) % self.bins) for i in range(self.bins)]

    def halves(self):
        order = far_order(self.targets)
        return [order, [self.targets + i for i in order]]

    def everyone(self):
        return [far_order(self.bins)]


def per_device(sources, density, temp_bins, ray_index, rate_tables, line_table):
    cells, levels = sources.shape
    bin_total = lax.axis_size("bin")
    wave_total = lax.axis_size("wave")
    plan = Plan(bin_total, cells)
    rows = plan.block + META_ROWS
    params = pltpu.CompilerParams(vmem_limit_bytes=VMEM_LIMIT)
    vmem = pl.BlockSpec(memory_space=pltpu.VMEM)
    smem = pl.BlockSpec(memory_space=pltpu.SMEM)
    hbm = pl.BlockSpec(memory_space=pltpu.HBM)

    def in_hbm(x):
        return pltpu.with_memory_space_constraint(x, pltpu.HBM)

    arrived = lax.ppermute(rate_tables[0], "bin", plan.table_moves())
    me = lax.axis_index("bin").astype(I32).reshape(1)
    den_rows = cells // min(cells, LANES)
    outgoing = pl.pallas_call(
        functools.partial(pack_kernel, plan),
        out_shape=jax.ShapeDtypeStruct((plan.targets, rows, levels), BF16),
        in_specs=[smem] + [hbm] * 4,
        out_specs=vmem,
        scratch_shapes=[
            pltpu.VMEM((cells, levels), BF16),
            pltpu.VMEM((den_rows, cells // den_rows), BF16),
            pltpu.VMEM((1, cells), I32),
            pltpu.VMEM((1, cells), I32),
            pltpu.SemaphoreType.DMA((4,)),
        ],
        compiler_params=params,
    )(
        me,
        in_hbm(sources),
        in_hbm(density.reshape(den_rows, cells // den_rows)),
        in_hbm(temp_bins.reshape(1, cells)),
        in_hbm(ray_index.reshape(1, cells)),
    )
    got = lax.all_to_all(
        outgoing, "bin", split_axis=0, concat_axis=0, tiled=True, axis_index_groups=plan.halves()
    )
    powers, held_line = pl.pallas_call(
        window_kernel,
        out_shape=[
            jax.ShapeDtypeStruct(a, BF16) for a in ((2, levels, 2 * levels), line_table.shape)
        ],
        in_specs=[vmem, hbm, hbm],
        out_specs=[vmem] * 2,
        scratch_shapes=[pltpu.SemaphoreType.DMA((2,))],
        compiler_params=params,
        cost_estimate=pl.CostEstimate(
            flops=OVERLAP_FLOPS, bytes_accessed=4 * arrived.size, transcendentals=0
        ),
    )(arrived, in_hbm(rate_tables[0]), in_hbm(line_table))
    ray_rows = RAY_DEV
    rays = ray_rows * bin_total
    partial_sums = pl.pallas_call(
        functools.partial(level_kernel, plan, ray_rows),
        out_shape=jax.ShapeDtypeStruct((rays, levels), BF16),
        in_specs=[vmem] * 2,
        out_specs=vmem,
        compiler_params=params,
    )(got, powers)
    held = lax.all_to_all(
        partial_sums.reshape(bin_total, ray_rows, levels),
        "bin",
        split_axis=0,
        concat_axis=0,
        tiled=True,
        axis_index_groups=plan.everyone(),
    )
    total = jnp.sum(held.astype(F32), axis=0)
    theirs = jnp.zeros_like(total)
    step = 1
    while step < wave_total:
        total = total + theirs if step > 1 else total
        theirs = lax.ppermute(total, "wave", [(i, i ^ step) for i in range(wave_total)])
        step *= 2
    out_shape = (ray_rows, line_table.shape[1])
    return pl.pallas_call(
        line_kernel,
        out_shape=jax.ShapeDtypeStruct(out_shape, F32),
        in_specs=[vmem, vmem, vmem],
        out_specs=hbm,
        scratch_shapes=[pltpu.VMEM(out_shape, F32), pltpu.SemaphoreType.DMA((LINE_CHUNKS,))],
        compiler_params=params,
    )(total, theirs, held_line)


def solution(mesh):
    in_specs = (
        P(("bin", "wave"), None),
        P(("bin", "wave")),
        P(("bin", "wave"), None),
        P(("bin", "wave")),
        P("bin", None, None),
        P(None, "wave"),
    )
    return jax.shard_map(
        per_device, mesh=mesh, in_specs=in_specs, out_specs=P("bin", "wave"), check_vma=False
    )
```

```python
import functools

import jax
import jax.numpy as jnp
from jax import lax
from jax.experimental import pallas as pl
from jax.experimental.pallas import tpu as pltpu
from jax.sharding import PartitionSpec as P

RAY_DEV = 16
META_ROWS = 8
RAY_BASE = 32
LANES = 128
LINE_CHUNKS = 4
OVERLAP_FLOPS = 10**10
VMEM_LIMIT = 32 * 1024 * 1024
F32 = jnp.float32
BF16 = jnp.bfloat16
I32 = jnp.int32


def nt_dot(a, b):
    return lax.dot_general(a, b, (((1,), (1,)), ((), ())), preferred_element_type=F32)


def iota(shape, dim):
    return lax.broadcasted_iota(I32, shape, dim)


def pack_kernel(plan, me_ref, src_hbm, den_hbm, bin_hbm, ray_hbm, *rest):
    targets, block = plan.targets, plan.block
    out, src_ref, den_ref, bin_ref, ray_ref, sems = rest
    copies = [
        pltpu.make_async_copy(a, b, sems.at[i])
        for i, (a, b) in enumerate(
            (
                (bin_hbm, bin_ref),
                (ray_hbm, ray_ref),
                (den_hbm, den_ref),
                (src_hbm, src_ref),
            )
        )
    ]
    for copy in copies:
        copy.start()
    cells, levels = src_ref.shape
    lanes = min(cells, LANES)
    earlier = (iota((lanes, lanes), 0) < iota((lanes, lanes), 1)).astype(F32).astype(BF16)
    my_half = me_ref[0] // targets
    for copy in copies[:3]:
        copy.wait()
    bins = bin_ref[...]
    hot = (iota((plan.bins, cells), 0) == bins).astype(F32)
    parts = [hot[:, i : i + lanes] for i in range(0, cells, lanes)]
    ranks = jnp.dot(
        jnp.concatenate(parts, axis=0).astype(BF16), earlier, preferred_element_type=F32
    )
    sofar = jnp.zeros((plan.bins, 1), F32)
    places = []
    for i, part in enumerate(parts):
        rank = ranks[i * plan.bins : (i + 1) * plan.bins] + sofar
        places.append(jnp.sum(part * rank, axis=0, keepdims=True))
        sofar = sofar + jnp.sum(part, axis=1, keepdims=True)
    position = jnp.concatenate(places, axis=1).astype(I32)
    half = bins // targets
    target = bins - half * targets
    within = (half ^ my_half) * plan.capacity + position
    rays = ray_ref[...]
    ray_high = rays // RAY_BASE
    ray_low = rays - ray_high * RAY_BASE
    den = den_ref[...].astype(F32)
    den_row = jnp.concatenate([den[i : i + 1] for i in range(den.shape[0])], axis=1)
    meta = jnp.concatenate(
        [den_row, ray_high.astype(F32), ray_low.astype(F32), jnp.zeros((META_ROWS - 3, cells), F32)],
        axis=0,
    ).astype(BF16)
    base = (iota((block, cells), 0) == within).astype(F32).astype(BF16)
    masks = [(target == t).astype(F32).astype(BF16) for t in range(targets)]
    place = jnp.concatenate([base * mask for mask in masks], axis=0)
    moved = nt_dot(jnp.concatenate([meta * mask for mask in masks], axis=0), base).astype(BF16)
    copies[3].wait()
    rows = jnp.dot(place, src_ref[...], preferred_element_type=F32).astype(BF16)
    out[:, :block, :] = rows.reshape(targets, block, levels)
    out[:, block:, :] = jnp.zeros((targets, META_ROWS, levels), BF16)
    for t in range(targets):
        out[t, block:, :block] = moved[t * META_ROWS : (t + 1) * META_ROWS]


def window_kernel(arrived_ref, table_hbm, line_hbm, powers_ref, line_ref, sems):
    levels = arrived_ref.shape[0]
    copies = [
        pltpu.make_async_copy(table_hbm, powers_ref.at[0, :, pl.ds(0, levels)], sems.at[0]),
        pltpu.make_async_copy(line_hbm, line_ref, sems.at[1]),
    ]
    for copy in copies:
        copy.start()
    powers_ref[1, :, :levels] = arrived_ref[...]
    copies[0].wait()
    for part in range(2):
        table = powers_ref[part, :, :levels]
        square = jnp.dot(table, table, preferred_element_type=F32)
        powers_ref[part, :, levels:] = square.astype(BF16)
    copies[1].wait()


def level_kernel(plan, rays, got_ref, powers_ref, out_ref):
    targets, block = plan.targets, plan.block
    meta = [got_ref[s, block:, :block].astype(F32) for s in range(targets)]
    columns = [jnp.transpose(m[:8]) for m in meta]
    total = jnp.zeros(out_ref.shape, F32)
    levels = got_ref.shape[2]
    for part in range(2):
        low, high = part * plan.capacity, (part + 1) * plan.capacity
        src = got_ref[:, low:high, :].reshape(targets * plan.capacity, got_ref.shape[2])
        den = jnp.concatenate([c[low:high, 0:1] for c in columns], axis=0)
        ray = jnp.concatenate(
            [m[1:2, low:high] * RAY_BASE + m[2:3, low:high] for m in meta], axis=1
        ).astype(I32)
        wide = src.astype(F32)
        steps = jnp.dot(src, powers_ref[part], preferred_element_type=F32)
        pops = (wide + den * (steps[:, :levels] + den * steps[:, levels:])).astype(BF16)
        pick = (iota((rays, src.shape[0]), 0) == ray).astype(F32).astype(BF16)
        total = total + jnp.dot(pick, pops, preferred_element_type=F32)
    out_ref[...] = total.astype(BF16)


def line_kernel(mine_ref, theirs_ref, line_ref, out_hbm, out_ref, sems):
    sums = mine_ref[...] + theirs_ref[...]
    rows = sums.shape[0]
    high = sums.astype(BF16)
    low = (sums - high.astype(F32)).astype(BF16)
    both = jnp.concatenate([high, low], axis=0)
    chunks = sems.shape[0]
    width = out_ref.shape[1] // chunks
    copies = []
    for i in range(chunks):
        part = pl.ds(i * width, width)
        got = jnp.dot(both, line_ref[:, part], preferred_element_type=F32)
        out_ref[:, part] = got[:rows] + got[rows:]
        copies.append(pltpu.make_async_copy(out_ref.at[:, part], out_hbm.at[:, part], sems.at[i]))
        copies[-1].start()
    for copy in copies:
        copy.wait()


class Plan:
    def __init__(self, bin_total, cells):
        self.bins = bin_total
        self.targets = bin_total // 2
        self.capacity = max(2, 2 * cells // bin_total)
        self.block = 2 * self.capacity

    def table_moves(self, wave_total):
        return [
            (b * wave_total + w, (b + self.targets) % self.bins * wave_total + (w ^ 1))
            for b in range(self.bins)
            for w in range(wave_total)
        ]

    def halves(self):
        return [list(range(self.targets)), list(range(self.targets, self.bins))]


def per_device(sources, density, temp_bins, ray_index, rate_tables, line_table):
    cells, levels = sources.shape
    bin_total = lax.axis_size("bin")
    wave_total = lax.axis_size("wave")
    plan = Plan(bin_total, cells)
    rows = plan.block + META_ROWS
    params = pltpu.CompilerParams(vmem_limit_bytes=VMEM_LIMIT)
    vmem = pl.BlockSpec(memory_space=pltpu.VMEM)
    smem = pl.BlockSpec(memory_space=pltpu.SMEM)
    hbm = pl.BlockSpec(memory_space=pltpu.HBM)

    def in_hbm(x):
        return pltpu.with_memory_space_constraint(x, pltpu.HBM)

    arrived = lax.ppermute(rate_tables[0], ("bin", "wave"), plan.table_moves(wave_total))
    me = lax.axis_index("bin").astype(I32).reshape(1)
    den_rows = cells // min(cells, LANES)
    outgoing = pl.pallas_call(
        functools.partial(pack_kernel, plan),
        out_shape=jax.ShapeDtypeStruct((plan.targets, rows, levels), BF16),
        in_specs=[smem] + [hbm] * 4,
        out_specs=vmem,
        scratch_shapes=[
            pltpu.VMEM((cells, levels), BF16),
            pltpu.VMEM((den_rows, cells // den_rows), BF16),
            pltpu.VMEM((1, cells), I32),
            pltpu.VMEM((1, cells), I32),
            pltpu.SemaphoreType.DMA((4,)),
        ],
        compiler_params=params,
    )(
        me,
        in_hbm(sources),
        in_hbm(density.reshape(den_rows, cells // den_rows)),
        in_hbm(temp_bins.reshape(1, cells)),
        in_hbm(ray_index.reshape(1, cells)),
    )
    got = lax.all_to_all(
        outgoing, "bin", split_axis=0, concat_axis=0, tiled=True, axis_index_groups=plan.halves()
    )
    powers, held_line = pl.pallas_call(
        window_kernel,
        out_shape=[
            jax.ShapeDtypeStruct(a, BF16) for a in ((2, levels, 2 * levels), line_table.shape)
        ],
        in_specs=[vmem, hbm, hbm],
        out_specs=[vmem] * 2,
        scratch_shapes=[pltpu.SemaphoreType.DMA((2,))],
        compiler_params=params,
        cost_estimate=pl.CostEstimate(
            flops=OVERLAP_FLOPS, bytes_accessed=4 * arrived.size, transcendentals=0
        ),
    )(arrived, in_hbm(rate_tables[0]), in_hbm(line_table))
    ray_rows = RAY_DEV
    rays = ray_rows * bin_total
    partial_sums = pl.pallas_call(
        functools.partial(level_kernel, plan, rays),
        out_shape=jax.ShapeDtypeStruct((rays, levels), BF16),
        in_specs=[vmem] * 2,
        out_specs=vmem,
        compiler_params=params,
    )(got, powers)
    held = lax.all_to_all(
        partial_sums.reshape(bin_total, ray_rows, levels),
        "bin",
        split_axis=0,
        concat_axis=0,
        tiled=True,
    )
    total = jnp.sum(held.astype(F32), axis=0)
    theirs = jnp.zeros_like(total)
    step = 1
    while step < wave_total:
        total = total + theirs if step > 1 else total
        theirs = lax.ppermute(total, "wave", [(i, i ^ step) for i in range(wave_total)])
        step *= 2
    out_shape = (ray_rows, line_table.shape[1])
    return pl.pallas_call(
        line_kernel,
        out_shape=jax.ShapeDtypeStruct(out_shape, F32),
        in_specs=[vmem, vmem, vmem],
        out_specs=hbm,
        scratch_shapes=[pltpu.VMEM(out_shape, F32), pltpu.SemaphoreType.DMA((LINE_CHUNKS,))],
        compiler_params=params,
    )(total, theirs, held_line)


def solution(mesh):
    in_specs = (
        P(("bin", "wave"), None),
        P(("bin", "wave")),
        P(("bin", "wave"), None),
        P(("bin", "wave")),
        P("bin", None, None),
        P(None, "wave"),
    )
    return jax.shard_map(
        per_device, mesh=mesh, in_specs=in_specs, out_specs=P("bin", "wave"), check_vma=False
    )
```

```python
import functools

import jax
import jax.numpy as jnp
from jax import lax
from jax.experimental import pallas as pl
from jax.experimental.pallas import tpu as pltpu
from jax.sharding import PartitionSpec as P

RAY_DEV = 16
META_ROWS = 8
RAY_BASE = 32
LANES = 128
LINE_CHUNKS = 4
OVERLAP_FLOPS = 10**10
VMEM_LIMIT = 32 * 1024 * 1024
F32 = jnp.float32
BF16 = jnp.bfloat16
I32 = jnp.int32


def nt_dot(a, b):
    return lax.dot_general(a, b, (((1,), (1,)), ((), ())), preferred_element_type=F32)


def iota(shape, dim):
    return lax.broadcasted_iota(I32, shape, dim)


def pack_kernel(plan, me_ref, src_hbm, den_hbm, bin_hbm, ray_hbm, *rest):
    targets, block = plan.targets, plan.block
    outs, near_out = rest[: len(plan.far)], rest[len(plan.far)]
    src_ref, den_ref, bin_ref, ray_ref, sems = rest[len(plan.far) + 1 :]
    copies = [
        pltpu.make_async_copy(a, b, sems.at[i])
        for i, (a, b) in enumerate(
            (
                (bin_hbm, bin_ref),
                (ray_hbm, ray_ref),
                (den_hbm, den_ref),
                (src_hbm, src_ref),
            )
        )
    ]
    for copy in copies:
        copy.start()
    cells, levels = src_ref.shape
    lanes = min(cells, LANES)
    earlier = (iota((lanes, lanes), 0) < iota((lanes, lanes), 1)).astype(F32).astype(BF16)
    my_half = me_ref[0] // targets
    my_place = me_ref[0] - my_half * targets
    for copy in copies[:3]:
        copy.wait()
    bins = bin_ref[...]
    hot = (iota((plan.bins, cells), 0) == bins).astype(F32)
    parts = [hot[:, i : i + lanes] for i in range(0, cells, lanes)]
    ranks = jnp.dot(
        jnp.concatenate(parts, axis=0).astype(BF16), earlier, preferred_element_type=F32
    )
    sofar = jnp.zeros((plan.bins, 1), F32)
    places = []
    for i, part in enumerate(parts):
        rank = ranks[i * plan.bins : (i + 1) * plan.bins] + sofar
        places.append(jnp.sum(part * rank, axis=0, keepdims=True))
        sofar = sofar + jnp.sum(part, axis=1, keepdims=True)
    position = jnp.concatenate(places, axis=1).astype(I32)
    half = bins // targets
    target = bins - half * targets
    within = (half ^ my_half) * plan.capacity + position
    rays = ray_ref[...]
    ray_high = rays // RAY_BASE
    ray_low = rays - ray_high * RAY_BASE
    den = den_ref[...].astype(F32)
    den_row = jnp.concatenate([den[i : i + 1] for i in range(den.shape[0])], axis=1)
    meta = jnp.concatenate(
        [den_row, ray_high.astype(F32), ray_low.astype(F32), jnp.zeros((META_ROWS - 3, cells), F32)],
        axis=0,
    ).astype(BF16)
    base = (iota((block, cells), 0) == within).astype(F32).astype(BF16)
    turn = target ^ my_place
    flips = turn
    for shift in range(1, targets.bit_length() - 1):
        flips = flips ^ (turn >> shift)
    pairs = jnp.where(flips % 2 == 0, target // 2, -1)
    masks = [(pairs == p).astype(F32).astype(BF16) for p in range(targets // 2)]
    masks = [(turn == k).astype(F32).astype(BF16) for k in plan.far] + masks
    place = jnp.concatenate([base * mask for mask in masks], axis=0)
    moved = nt_dot(jnp.concatenate([meta * mask for mask in masks], axis=0), base).astype(BF16)
    copies[3].wait()
    rows = jnp.dot(place, src_ref[...], preferred_element_type=F32).astype(BF16)
    for t in range(targets):
        out = outs[t] if t < len(outs) else near_out.at[t - len(outs)]
        out[:block, :] = rows[t * block : (t + 1) * block]
        out[block:, :] = jnp.zeros((META_ROWS, levels), BF16)
        out[block:, :block] = moved[t * META_ROWS : (t + 1) * META_ROWS]


def stage_kernel(near_ref, out_hbm, sem):
    copy = pltpu.make_async_copy(near_ref, out_hbm, sem)
    copy.start()
    copy.wait()


def window_kernel(arrived_ref, table_hbm, line_hbm, powers_ref, line_ref, sems):
    levels = arrived_ref.shape[0]
    copies = [
        pltpu.make_async_copy(table_hbm, powers_ref.at[0, :, pl.ds(0, levels)], sems.at[0]),
        pltpu.make_async_copy(line_hbm, line_ref, sems.at[1]),
    ]
    for copy in copies:
        copy.start()
    powers_ref[1, :, :levels] = arrived_ref[...]
    copies[0].wait()
    for part in range(2):
        table = powers_ref[part, :, :levels]
        square = jnp.dot(table, table, preferred_element_type=F32)
        powers_ref[part, :, levels:] = square.astype(BF16)
    copies[1].wait()


def level_kernel(plan, rays, powers_ref, near_ref, *refs):
    out_ref, block, levels = refs[-1], plan.block, near_ref.shape[2]
    got = list(refs[:-1]) + [near_ref.at[i] for i in range(near_ref.shape[0])]
    meta = [g[block:, :block].astype(F32) for g in got]
    columns = [jnp.transpose(m[:8]) for m in meta]
    total = jnp.zeros(out_ref.shape, F32)
    for part in range(2):
        low, high = part * plan.capacity, (part + 1) * plan.capacity
        src = jnp.concatenate([g[low:high, :] for g in got], axis=0)
        den = jnp.concatenate([c[low:high, 0:1] for c in columns], axis=0)
        ray = jnp.concatenate(
            [m[1:2, low:high] * RAY_BASE + m[2:3, low:high] for m in meta], axis=1
        ).astype(I32)
        wide = src.astype(F32)
        steps = jnp.dot(src, powers_ref[part], preferred_element_type=F32)
        pops = (wide + den * (steps[:, :levels] + den * steps[:, levels:])).astype(BF16)
        pick = (iota((rays, src.shape[0]), 0) == ray).astype(F32).astype(BF16)
        total = total + jnp.dot(pick, pops, preferred_element_type=F32)
    out_ref[...] = total.astype(BF16)


def line_kernel(mine_ref, theirs_ref, line_ref, out_hbm, out_ref, sems):
    sums = mine_ref[...] + theirs_ref[...]
    rows = sums.shape[0]
    high = sums.astype(BF16)
    low = (sums - high.astype(F32)).astype(BF16)
    both = jnp.concatenate([high, low], axis=0)
    chunks = sems.shape[0]
    width = out_ref.shape[1] // chunks
    copies = []
    for i in range(chunks):
        part = pl.ds(i * width, width)
        got = jnp.dot(both, line_ref[:, part], preferred_element_type=F32)
        out_ref[:, part] = got[:rows] + got[rows:]
        copies.append(pltpu.make_async_copy(out_ref.at[:, part], out_hbm.at[:, part], sems.at[i]))
        copies[-1].start()
    for copy in copies:
        copy.wait()


class Plan:
    def __init__(self, bin_total, cells):
        self.bins = bin_total
        self.targets = bin_total // 2
        self.capacity = max(2, 2 * cells // bin_total)
        self.block = 2 * self.capacity
        even = [k for k in range(self.targets) if bin(k).count("1") % 2 == 0]
        odd = [k for k in range(self.targets) if bin(k).count("1") % 2]
        self.far = sorted(odd, key=lambda k: (-bin(k).count("1"), k))
        self.quads = [[h + k for k in ks] for h in (0, self.targets) for ks in (even, odd)]

    def table_moves(self):
        return [(i, (i + self.targets) % self.bins) for i in range(self.bins)]

    def moves(self, k):
        return [(i, i ^ k) for i in range(self.bins)]


def per_device(sources, density, temp_bins, ray_index, rate_tables, line_table):
    cells, levels = sources.shape
    bin_total = lax.axis_size("bin")
    wave_total = lax.axis_size("wave")
    plan = Plan(bin_total, cells)
    rows = plan.block + META_ROWS
    params = pltpu.CompilerParams(vmem_limit_bytes=VMEM_LIMIT)
    vmem = pl.BlockSpec(memory_space=pltpu.VMEM)
    smem = pl.BlockSpec(memory_space=pltpu.SMEM)
    hbm = pl.BlockSpec(memory_space=pltpu.HBM)

    def in_hbm(x):
        return pltpu.with_memory_space_constraint(x, pltpu.HBM)

    arrived = lax.ppermute(rate_tables[0], "bin", plan.table_moves())
    me = lax.axis_index("bin").astype(I32).reshape(1)
    den_rows = cells // min(cells, LANES)
    near_shape = jax.ShapeDtypeStruct((plan.targets // 2, rows, levels), BF16)
    *outgoing, near = pl.pallas_call(
        functools.partial(pack_kernel, plan),
        out_shape=[jax.ShapeDtypeStruct((rows, levels), BF16)] * len(plan.far) + [near_shape],
        in_specs=[smem] + [hbm] * 4,
        out_specs=[vmem] * (len(plan.far) + 1),
        scratch_shapes=[
            pltpu.VMEM((cells, levels), BF16),
            pltpu.VMEM((den_rows, cells // den_rows), BF16),
            pltpu.VMEM((1, cells), I32),
            pltpu.VMEM((1, cells), I32),
            pltpu.SemaphoreType.DMA((4,)),
        ],
        compiler_params=params,
    )(
        me,
        in_hbm(sources),
        in_hbm(density.reshape(den_rows, cells // den_rows)),
        in_hbm(temp_bins.reshape(1, cells)),
        in_hbm(ray_index.reshape(1, cells)),
    )
    far = [lax.ppermute(x, "bin", plan.moves(k)) for x, k in zip(outgoing, plan.far)]
    staged = pl.pallas_call(
        stage_kernel,
        out_shape=near_shape,
        in_specs=[vmem],
        out_specs=hbm,
        scratch_shapes=[pltpu.SemaphoreType.DMA],
        compiler_params=params,
    )(near)
    got = lax.all_to_all(
        staged, "bin", split_axis=0, concat_axis=0, tiled=True, axis_index_groups=plan.quads
    )
    powers, held_line = pl.pallas_call(
        window_kernel,
        out_shape=[
            jax.ShapeDtypeStruct(a, BF16) for a in ((2, levels, 2 * levels), line_table.shape)
        ],
        in_specs=[vmem, hbm, hbm],
        out_specs=[vmem] * 2,
        scratch_shapes=[pltpu.SemaphoreType.DMA((2,))],
        compiler_params=params,
        cost_estimate=pl.CostEstimate(
            flops=OVERLAP_FLOPS, bytes_accessed=4 * arrived.size, transcendentals=0
        ),
    )(arrived, in_hbm(rate_tables[0]), in_hbm(line_table))
    ray_rows = RAY_DEV
    rays = ray_rows * bin_total
    partial_sums = pl.pallas_call(
        functools.partial(level_kernel, plan, rays),
        out_shape=jax.ShapeDtypeStruct((rays, levels), BF16),
        in_specs=[vmem] * (2 + len(far)),
        out_specs=vmem,
        compiler_params=params,
    )(powers, got, *far)
    held = lax.all_to_all(
        partial_sums.reshape(bin_total, ray_rows, levels),
        "bin",
        split_axis=0,
        concat_axis=0,
        tiled=True,
    )
    total = jnp.sum(held.astype(F32), axis=0)
    theirs = jnp.zeros_like(total)
    step = 1
    while step < wave_total:
        total = total + theirs if step > 1 else total
        theirs = lax.ppermute(total, "wave", [(i, i ^ step) for i in range(wave_total)])
        step *= 2
    out_shape = (ray_rows, line_table.shape[1])
    return pl.pallas_call(
        line_kernel,
        out_shape=jax.ShapeDtypeStruct(out_shape, F32),
        in_specs=[vmem, vmem, vmem],
        out_specs=hbm,
        scratch_shapes=[pltpu.VMEM(out_shape, F32), pltpu.SemaphoreType.DMA((LINE_CHUNKS,))],
        compiler_params=params,
    )(total, theirs, held_line)


def solution(mesh):
    in_specs = (
        P(("bin", "wave"), None),
        P(("bin", "wave")),
        P(("bin", "wave"), None),
        P(("bin", "wave")),
        P("bin", None, None),
        P(None, "wave"),
    )
    return jax.shard_map(
        per_device, mesh=mesh, in_specs=in_specs, out_specs=P("bin", "wave"), check_vma=False
    )
```

```python
import functools

import jax
import jax.numpy as jnp
from jax import lax
from jax.experimental import pallas as pl
from jax.experimental.pallas import tpu as pltpu
from jax.sharding import PartitionSpec as P

RAY_DEV = 16
META_ROWS = 8
RAY_BASE = 32
LANES = 128
LINE_CHUNKS = 4
OVERLAP_FLOPS = 10**10
VMEM_LIMIT = 32 * 1024 * 1024
F32 = jnp.float32
BF16 = jnp.bfloat16
I32 = jnp.int32


def nt_dot(a, b):
    return lax.dot_general(a, b, (((1,), (1,)), ((), ())), preferred_element_type=F32)


def iota(shape, dim):
    return lax.broadcasted_iota(I32, shape, dim)


def pack_kernel(plan, me_ref, src_hbm, den_hbm, bin_hbm, ray_hbm, *rest):
    targets, block = plan.targets, plan.block
    outs, near_out = rest[: len(plan.far)], rest[len(plan.far)]
    src_ref, den_ref, bin_ref, ray_ref, sems = rest[len(plan.far) + 1 :]
    copies = [
        pltpu.make_async_copy(a, b, sems.at[i])
        for i, (a, b) in enumerate(
            (
                (bin_hbm, bin_ref),
                (ray_hbm, ray_ref),
                (den_hbm, den_ref),
                (src_hbm, src_ref),
            )
        )
    ]
    for copy in copies:
        copy.start()
    cells, levels = src_ref.shape
    lanes = min(cells, LANES)
    earlier = (iota((lanes, lanes), 0) < iota((lanes, lanes), 1)).astype(F32).astype(BF16)
    my_half = me_ref[0] // targets
    my_place = me_ref[0] - my_half * targets
    for copy in copies[:3]:
        copy.wait()
    bins = bin_ref[...]
    hot = (iota((plan.bins, cells), 0) == bins).astype(F32)
    parts = [hot[:, i : i + lanes] for i in range(0, cells, lanes)]
    ranks = jnp.dot(
        jnp.concatenate(parts, axis=0).astype(BF16), earlier, preferred_element_type=F32
    )
    sofar = jnp.zeros((plan.bins, 1), F32)
    places = []
    for i, part in enumerate(parts):
        rank = ranks[i * plan.bins : (i + 1) * plan.bins] + sofar
        places.append(jnp.sum(part * rank, axis=0, keepdims=True))
        sofar = sofar + jnp.sum(part, axis=1, keepdims=True)
    position = jnp.concatenate(places, axis=1).astype(I32)
    half = bins // targets
    target = bins - half * targets
    within = (half ^ my_half) * plan.capacity + position
    rays = ray_ref[...]
    ray_high = rays // RAY_BASE
    ray_low = rays - ray_high * RAY_BASE
    den = den_ref[...].astype(F32)
    den_row = jnp.concatenate([den[i : i + 1] for i in range(den.shape[0])], axis=1)
    meta = jnp.concatenate(
        [den_row, ray_high.astype(F32), ray_low.astype(F32), jnp.zeros((META_ROWS - 3, cells), F32)],
        axis=0,
    ).astype(BF16)
    base = (iota((block, cells), 0) == within).astype(F32).astype(BF16)
    turn = target ^ my_place
    flips = turn
    for shift in range(1, targets.bit_length() - 1):
        flips = flips ^ (turn >> shift)
    pairs = jnp.where(flips % 2 == 0, target // 2, -1)
    masks = [(pairs == p).astype(F32).astype(BF16) for p in range(targets // 2)]
    masks = [(turn == k).astype(F32).astype(BF16) for k in plan.far] + masks
    place = jnp.concatenate([base * mask for mask in masks], axis=0)
    moved = nt_dot(jnp.concatenate([meta * mask for mask in masks], axis=0), base).astype(BF16)
    copies[3].wait()
    rows = jnp.dot(place, src_ref[...], preferred_element_type=F32).astype(BF16)
    for t in range(targets):
        out = outs[t] if t < len(outs) else near_out.at[t - len(outs)]
        out[:block, :] = rows[t * block : (t + 1) * block]
        out[block:, :] = jnp.zeros((META_ROWS, levels), BF16)
        out[block:, :block] = moved[t * META_ROWS : (t + 1) * META_ROWS]


def stage_kernel(near_ref, out_hbm, sem):
    copy = pltpu.make_async_copy(near_ref, out_hbm, sem)
    copy.start()
    copy.wait()


def window_kernel(arrived_ref, table_hbm, line_hbm, powers_ref, line_ref, sems):
    levels = arrived_ref.shape[0]
    copies = [
        pltpu.make_async_copy(table_hbm, powers_ref.at[0, :, pl.ds(0, levels)], sems.at[0]),
        pltpu.make_async_copy(line_hbm, line_ref, sems.at[1]),
    ]
    for copy in copies:
        copy.start()
    powers_ref[1, :, :levels] = arrived_ref[...]
    copies[0].wait()
    for part in range(2):
        table = powers_ref[part, :, :levels]
        square = jnp.dot(table, table, preferred_element_type=F32)
        powers_ref[part, :, levels:] = square.astype(BF16)
    copies[1].wait()


def token_kernel(*refs):
    refs[-1][...] = jnp.zeros_like(refs[-1])


def level_kernel(plan, rays, token_ref, powers_ref, near_ref, *refs):
    out_ref, block, levels = refs[-1], plan.block, near_ref.shape[2]
    got = list(refs[:-1]) + [near_ref.at[i] for i in range(near_ref.shape[0])]
    meta = [g[block:, :block].astype(F32) for g in got]
    columns = [jnp.transpose(m[:8]) for m in meta]
    total = jnp.zeros(out_ref.shape, F32)
    for part in range(2):
        low, high = part * plan.capacity, (part + 1) * plan.capacity
        src = jnp.concatenate([g[low:high, :] for g in got], axis=0)
        den = jnp.concatenate([c[low:high, 0:1] for c in columns], axis=0)
        ray = jnp.concatenate(
            [m[1:2, low:high] * RAY_BASE + m[2:3, low:high] for m in meta], axis=1
        ).astype(I32)
        wide = src.astype(F32)
        steps = jnp.dot(src, powers_ref[part], preferred_element_type=F32)
        pops = (wide + den * (steps[:, :levels] + den * steps[:, levels:])).astype(BF16)
        pick = (iota((rays, src.shape[0]), 0) == ray).astype(F32).astype(BF16)
        total = total + jnp.dot(pick, pops, preferred_element_type=F32)
    out_ref[...] = total.astype(BF16)


def line_kernel(mine_ref, theirs_ref, line_ref, out_hbm, out_ref, sems):
    sums = mine_ref[...] + theirs_ref[...]
    rows = sums.shape[0]
    high = sums.astype(BF16)
    low = (sums - high.astype(F32)).astype(BF16)
    both = jnp.concatenate([high, low], axis=0)
    chunks = sems.shape[0]
    width = out_ref.shape[1] // chunks
    copies = []
    for i in range(chunks):
        part = pl.ds(i * width, width)
        got = jnp.dot(both, line_ref[:, part], preferred_element_type=F32)
        out_ref[:, part] = got[:rows] + got[rows:]
        copies.append(pltpu.make_async_copy(out_ref.at[:, part], out_hbm.at[:, part], sems.at[i]))
        copies[-1].start()
    for copy in copies:
        copy.wait()


class Plan:
    def __init__(self, bin_total, cells):
        self.bins = bin_total
        self.targets = bin_total // 2
        self.capacity = max(2, 2 * cells // bin_total)
        self.block = 2 * self.capacity
        even = [k for k in range(self.targets) if bin(k).count("1") % 2 == 0]
        odd = [k for k in range(self.targets) if bin(k).count("1") % 2]
        self.far = sorted(odd, key=lambda k: (-bin(k).count("1"), k))
        self.quads = [[h + k for k in ks] for h in (0, self.targets) for ks in (even, odd)]

    def table_moves(self):
        return [(i, (i + self.targets) % self.bins) for i in range(self.bins)]

    def moves(self, k):
        return [(i, i ^ k) for i in range(self.bins)]


def per_device(sources, density, temp_bins, ray_index, rate_tables, line_table):
    cells, levels = sources.shape
    bin_total = lax.axis_size("bin")
    wave_total = lax.axis_size("wave")
    plan = Plan(bin_total, cells)
    rows = plan.block + META_ROWS
    params = pltpu.CompilerParams(vmem_limit_bytes=VMEM_LIMIT)
    vmem = pl.BlockSpec(memory_space=pltpu.VMEM)
    smem = pl.BlockSpec(memory_space=pltpu.SMEM)
    hbm = pl.BlockSpec(memory_space=pltpu.HBM)

    def in_hbm(x):
        return pltpu.with_memory_space_constraint(x, pltpu.HBM)

    arrived = lax.ppermute(rate_tables[0], "bin", plan.table_moves())
    me = lax.axis_index("bin").astype(I32).reshape(1)
    den_rows = cells // min(cells, LANES)
    near_shape = jax.ShapeDtypeStruct((plan.targets // 2, rows, levels), BF16)
    *outgoing, near = pl.pallas_call(
        functools.partial(pack_kernel, plan),
        out_shape=[jax.ShapeDtypeStruct((rows, levels), BF16)] * len(plan.far) + [near_shape],
        in_specs=[smem] + [hbm] * 4,
        out_specs=[vmem] * (len(plan.far) + 1),
        scratch_shapes=[
            pltpu.VMEM((cells, levels), BF16),
            pltpu.VMEM((den_rows, cells // den_rows), BF16),
            pltpu.VMEM((1, cells), I32),
            pltpu.VMEM((1, cells), I32),
            pltpu.SemaphoreType.DMA((4,)),
        ],
        compiler_params=params,
    )(
        me,
        in_hbm(sources),
        in_hbm(density.reshape(den_rows, cells // den_rows)),
        in_hbm(temp_bins.reshape(1, cells)),
        in_hbm(ray_index.reshape(1, cells)),
    )
    far = [lax.ppermute(x, "bin", plan.moves(k)) for x, k in zip(outgoing, plan.far)]
    staged = pl.pallas_call(
        stage_kernel,
        out_shape=near_shape,
        in_specs=[vmem],
        out_specs=hbm,
        scratch_shapes=[pltpu.SemaphoreType.DMA],
        compiler_params=params,
    )(near)
    got = lax.all_to_all(
        staged, "bin", split_axis=0, concat_axis=0, tiled=True, axis_index_groups=plan.quads
    )
    powers, held_line = pl.pallas_call(
        window_kernel,
        out_shape=[
            jax.ShapeDtypeStruct(a, BF16) for a in ((2, levels, 2 * levels), line_table.shape)
        ],
        in_specs=[vmem, hbm, hbm],
        out_specs=[vmem] * 2,
        scratch_shapes=[pltpu.SemaphoreType.DMA((2,))],
        compiler_params=params,
        cost_estimate=pl.CostEstimate(
            flops=OVERLAP_FLOPS, bytes_accessed=4 * arrived.size, transcendentals=0
        ),
    )(arrived, in_hbm(rate_tables[0]), in_hbm(line_table))
    token = pl.pallas_call(
        token_kernel,
        out_shape=jax.ShapeDtypeStruct((8, LANES), F32),
        in_specs=[vmem] * len(far),
        out_specs=vmem,
        compiler_params=params,
        cost_estimate=pl.CostEstimate(
            flops=OVERLAP_FLOPS, bytes_accessed=4 * arrived.size, transcendentals=0
        ),
    )(*far)
    ray_rows = RAY_DEV
    rays = ray_rows * bin_total
    partial_sums = pl.pallas_call(
        functools.partial(level_kernel, plan, rays),
        out_shape=jax.ShapeDtypeStruct((rays, levels), BF16),
        in_specs=[vmem] * (3 + len(far)),
        out_specs=vmem,
        compiler_params=params,
    )(token, powers, got, *far)
    held = lax.all_to_all(
        partial_sums.reshape(bin_total, ray_rows, levels),
        "bin",
        split_axis=0,
        concat_axis=0,
        tiled=True,
    )
    total = jnp.sum(held.astype(F32), axis=0)
    theirs = jnp.zeros_like(total)
    step = 1
    while step < wave_total:
        total = total + theirs if step > 1 else total
        theirs = lax.ppermute(total, "wave", [(i, i ^ step) for i in range(wave_total)])
        step *= 2
    out_shape = (ray_rows, line_table.shape[1])
    return pl.pallas_call(
        line_kernel,
        out_shape=jax.ShapeDtypeStruct(out_shape, F32),
        in_specs=[vmem, vmem, vmem],
        out_specs=hbm,
        scratch_shapes=[pltpu.VMEM(out_shape, F32), pltpu.SemaphoreType.DMA((LINE_CHUNKS,))],
        compiler_params=params,
    )(total, theirs, held_line)


def solution(mesh):
    in_specs = (
        P(("bin", "wave"), None),
        P(("bin", "wave")),
        P(("bin", "wave"), None),
        P(("bin", "wave")),
        P("bin", None, None),
        P(None, "wave"),
    )
    return jax.shard_map(
        per_device, mesh=mesh, in_specs=in_specs, out_specs=P("bin", "wave"), check_vma=False
    )
```

```python
import functools

import jax
import jax.numpy as jnp
from jax import lax
from jax.experimental import pallas as pl
from jax.experimental.pallas import tpu as pltpu
from jax.sharding import PartitionSpec as P

RAY_DEV = 16
META_ROWS = 8
RAY_BASE = 32
LANES = 128
LINE_CHUNKS = 4
OVERLAP_FLOPS = 10**10
VMEM_LIMIT = 32 * 1024 * 1024
F32 = jnp.float32
BF16 = jnp.bfloat16
I32 = jnp.int32


def nt_dot(a, b):
    return lax.dot_general(a, b, (((1,), (1,)), ((), ())), preferred_element_type=F32)


def iota(shape, dim):
    return lax.broadcasted_iota(I32, shape, dim)


def pack_kernel(plan, me_ref, src_hbm, den_hbm, bin_hbm, ray_hbm, *rest):
    targets, block = plan.targets, plan.block
    out, src_ref, den_ref, bin_ref, ray_ref, sems = rest
    copies = [
        pltpu.make_async_copy(a, b, sems.at[i])
        for i, (a, b) in enumerate(
            (
                (bin_hbm, bin_ref),
                (ray_hbm, ray_ref),
                (den_hbm, den_ref),
                (src_hbm, src_ref),
            )
        )
    ]
    for copy in copies:
        copy.start()
    cells, levels = src_ref.shape
    lanes = min(cells, LANES)
    earlier = (iota((lanes, lanes), 0) < iota((lanes, lanes), 1)).astype(F32).astype(BF16)
    my_half = me_ref[0] // targets
    for copy in copies[:3]:
        copy.wait()
    bins = bin_ref[...]
    hot = (iota((plan.bins, cells), 0) == bins).astype(F32)
    parts = [hot[:, i : i + lanes] for i in range(0, cells, lanes)]
    ranks = jnp.dot(
        jnp.concatenate(parts, axis=0).astype(BF16), earlier, preferred_element_type=F32
    )
    sofar = jnp.zeros((plan.bins, 1), F32)
    places = []
    for i, part in enumerate(parts):
        rank = ranks[i * plan.bins : (i + 1) * plan.bins] + sofar
        places.append(jnp.sum(part * rank, axis=0, keepdims=True))
        sofar = sofar + jnp.sum(part, axis=1, keepdims=True)
    position = jnp.concatenate(places, axis=1).astype(I32)
    half = bins // targets
    target = bins - half * targets
    within = (half ^ my_half) * plan.capacity + position
    rays = ray_ref[...]
    ray_high = rays // RAY_BASE
    ray_low = rays - ray_high * RAY_BASE
    den = den_ref[...].astype(F32)
    den_row = jnp.concatenate([den[i : i + 1] for i in range(den.shape[0])], axis=1)
    meta = jnp.concatenate(
        [den_row, ray_high.astype(F32), ray_low.astype(F32), jnp.zeros((META_ROWS - 3, cells), F32)],
        axis=0,
    ).astype(BF16)
    base = (iota((block, cells), 0) == within).astype(F32).astype(BF16)
    masks = [(target == t).astype(F32).astype(BF16) for t in range(targets)]
    place = jnp.concatenate([base * mask for mask in masks], axis=0)
    moved = nt_dot(jnp.concatenate([meta * mask for mask in masks], axis=0), base).astype(BF16)
    copies[3].wait()
    rows = jnp.dot(place, src_ref[...], preferred_element_type=F32).astype(BF16)
    out[:, :block, :] = rows.reshape(targets, block, levels)
    out[:, block:, :] = jnp.zeros((targets, META_ROWS, levels), BF16)
    for t in range(targets):
        out[t, block:, :block] = moved[t * META_ROWS : (t + 1) * META_ROWS]


def window_kernel(core_ref, arrived_ref, table_hbm, line_hbm, powers_ref, line_ref, sems):
    levels = arrived_ref.shape[0]
    even = core_ref[0] % 2 == 0
    table_copy = pltpu.make_async_copy(table_hbm, powers_ref.at[0, :, pl.ds(0, levels)], sems.at[0])
    line_copy = pltpu.make_async_copy(line_hbm, line_ref, sems.at[1])
    table_copy.start()

    @pl.when(even)
    def _():
        line_copy.start()

    powers_ref[1, :, :levels] = arrived_ref[...]
    table_copy.wait()
    for part in range(2):
        table = powers_ref[part, :, :levels]
        square = jnp.dot(table, table, preferred_element_type=F32)
        powers_ref[part, :, levels:] = square.astype(BF16)

    @pl.when(even)
    def _():
        line_copy.wait()


def level_kernel(plan, rays, core_ref, got_ref, powers_ref, line_hbm, out_ref, line_ref, sem):
    odd = core_ref[0] % 2 == 1
    line_copy = pltpu.make_async_copy(line_hbm, line_ref, sem)

    @pl.when(odd)
    def _():
        line_copy.start()

    targets, block = plan.targets, plan.block
    meta = [got_ref[s, block:, :block].astype(F32) for s in range(targets)]
    columns = [jnp.transpose(m[:8]) for m in meta]
    total = jnp.zeros(out_ref.shape, F32)
    levels = got_ref.shape[2]
    for part in range(2):
        low, high = part * plan.capacity, (part + 1) * plan.capacity
        src = got_ref[:, low:high, :].reshape(targets * plan.capacity, got_ref.shape[2])
        den = jnp.concatenate([c[low:high, 0:1] for c in columns], axis=0)
        ray = jnp.concatenate(
            [m[1:2, low:high] * RAY_BASE + m[2:3, low:high] for m in meta], axis=1
        ).astype(I32)
        wide = src.astype(F32)
        steps = jnp.dot(src, powers_ref[part], preferred_element_type=F32)
        pops = (wide + den * (steps[:, :levels] + den * steps[:, levels:])).astype(BF16)
        pick = (iota((rays, src.shape[0]), 0) == ray).astype(F32).astype(BF16)
        total = total + jnp.dot(pick, pops, preferred_element_type=F32)
    out_ref[...] = total.astype(BF16)

    @pl.when(odd)
    def _():
        line_copy.wait()


def line_kernel(core_ref, mine_ref, theirs_ref, even_ref, odd_ref, out_hbm, out_ref, sems):
    for parity, line_ref in ((0, even_ref), (1, odd_ref)):

        @pl.when(core_ref[0] % 2 == parity)
        def _(line_ref=line_ref):
            line_product(mine_ref, theirs_ref, line_ref, out_hbm, out_ref, sems)


def line_product(mine_ref, theirs_ref, line_ref, out_hbm, out_ref, sems):
    sums = mine_ref[...] + theirs_ref[...]
    rows = sums.shape[0]
    high = sums.astype(BF16)
    low = (sums - high.astype(F32)).astype(BF16)
    both = jnp.concatenate([high, low], axis=0)
    chunks = sems.shape[0]
    width = out_ref.shape[1] // chunks
    copies = []
    for i in range(chunks):
        part = pl.ds(i * width, width)
        got = jnp.dot(both, line_ref[:, part], preferred_element_type=F32)
        out_ref[:, part] = got[:rows] + got[rows:]
        copies.append(pltpu.make_async_copy(out_ref.at[:, part], out_hbm.at[:, part], sems.at[i]))
        copies[-1].start()
    for copy in copies:
        copy.wait()


class Plan:
    def __init__(self, bin_total, cells):
        self.bins = bin_total
        self.targets = bin_total // 2
        self.capacity = max(2, 2 * cells // bin_total)
        self.block = 2 * self.capacity

    def table_moves(self):
        return [(i, (i + self.targets) % self.bins) for i in range(self.bins)]

    def halves(self):
        return [list(range(self.targets)), list(range(self.targets, self.bins))]


def per_device(sources, density, temp_bins, ray_index, rate_tables, line_table):
    cells, levels = sources.shape
    bin_total = lax.axis_size("bin")
    wave_total = lax.axis_size("wave")
    plan = Plan(bin_total, cells)
    rows = plan.block + META_ROWS
    params = pltpu.CompilerParams(vmem_limit_bytes=VMEM_LIMIT)
    vmem = pl.BlockSpec(memory_space=pltpu.VMEM)
    smem = pl.BlockSpec(memory_space=pltpu.SMEM)
    hbm = pl.BlockSpec(memory_space=pltpu.HBM)

    def in_hbm(x):
        return pltpu.with_memory_space_constraint(x, pltpu.HBM)

    arrived = lax.ppermute(rate_tables[0], "bin", plan.table_moves())
    me = lax.axis_index("bin").astype(I32).reshape(1)
    den_rows = cells // min(cells, LANES)
    outgoing = pl.pallas_call(
        functools.partial(pack_kernel, plan),
        out_shape=jax.ShapeDtypeStruct((plan.targets, rows, levels), BF16),
        in_specs=[smem] + [hbm] * 4,
        out_specs=vmem,
        scratch_shapes=[
            pltpu.VMEM((cells, levels), BF16),
            pltpu.VMEM((den_rows, cells // den_rows), BF16),
            pltpu.VMEM((1, cells), I32),
            pltpu.VMEM((1, cells), I32),
            pltpu.SemaphoreType.DMA((4,)),
        ],
        compiler_params=params,
    )(
        me,
        in_hbm(sources),
        in_hbm(density.reshape(den_rows, cells // den_rows)),
        in_hbm(temp_bins.reshape(1, cells)),
        in_hbm(ray_index.reshape(1, cells)),
    )
    got = lax.all_to_all(
        outgoing, "bin", split_axis=0, concat_axis=0, tiled=True, axis_index_groups=plan.halves()
    )
    core = lax.axis_index("wave").astype(I32).reshape(1)
    powers, even_line = pl.pallas_call(
        window_kernel,
        out_shape=[
            jax.ShapeDtypeStruct(a, BF16) for a in ((2, levels, 2 * levels), line_table.shape)
        ],
        in_specs=[smem, vmem, hbm, hbm],
        out_specs=[vmem] * 2,
        scratch_shapes=[pltpu.SemaphoreType.DMA((2,))],
        compiler_params=params,
        cost_estimate=pl.CostEstimate(
            flops=OVERLAP_FLOPS, bytes_accessed=4 * arrived.size, transcendentals=0
        ),
    )(core, arrived, in_hbm(rate_tables[0]), in_hbm(line_table))
    ray_rows = RAY_DEV
    rays = ray_rows * bin_total
    partial_sums, odd_line = pl.pallas_call(
        functools.partial(level_kernel, plan, rays),
        out_shape=[
            jax.ShapeDtypeStruct(a, BF16) for a in ((rays, levels), line_table.shape)
        ],
        in_specs=[smem, vmem, vmem, hbm],
        out_specs=[vmem] * 2,
        scratch_shapes=[pltpu.SemaphoreType.DMA],
        compiler_params=params,
    )(core, got, powers, in_hbm(line_table))
    held = lax.all_to_all(
        partial_sums.reshape(bin_total, ray_rows, levels),
        "bin",
        split_axis=0,
        concat_axis=0,
        tiled=True,
    )
    total = jnp.sum(held.astype(F32), axis=0)
    theirs = jnp.zeros_like(total)
    step = 1
    while step < wave_total:
        total = total + theirs if step > 1 else total
        theirs = lax.ppermute(total, "wave", [(i, i ^ step) for i in range(wave_total)])
        step *= 2
    out_shape = (ray_rows, line_table.shape[1])
    return pl.pallas_call(
        line_kernel,
        out_shape=jax.ShapeDtypeStruct(out_shape, F32),
        in_specs=[smem] + [vmem] * 4,
        out_specs=hbm,
        scratch_shapes=[pltpu.VMEM(out_shape, F32), pltpu.SemaphoreType.DMA((LINE_CHUNKS,))],
        compiler_params=params,
    )(core, total, theirs, even_line, odd_line)


def solution(mesh):
    in_specs = (
        P(("bin", "wave"), None),
        P(("bin", "wave")),
        P(("bin", "wave"), None),
        P(("bin", "wave")),
        P("bin", None, None),
        P(None, "wave"),
    )
    return jax.shard_map(
        per_device, mesh=mesh, in_specs=in_specs, out_specs=P("bin", "wave"), check_vma=False
    )
```

```python
import functools

import jax
import jax.numpy as jnp
from jax import lax
from jax.experimental import pallas as pl
from jax.experimental.pallas import tpu as pltpu
from jax.sharding import PartitionSpec as P

RAY_DEV = 16
META_ROWS = 8
RAY_BASE = 32
LANES = 128
LINE_CHUNKS = 4
OVERLAP_FLOPS = 10**10
VMEM_LIMIT = 32 * 1024 * 1024
F32 = jnp.float32
BF16 = jnp.bfloat16
I32 = jnp.int32


def nt_dot(a, b):
    return lax.dot_general(a, b, (((1,), (1,)), ((), ())), preferred_element_type=F32)


def iota(shape, dim):
    return lax.broadcasted_iota(I32, shape, dim)


def pack_kernel(plan, me_ref, src_hbm, den_hbm, bin_hbm, ray_hbm, line_hbm, *rest):
    targets, block = plan.targets, plan.block
    out, line_out, src_ref, den_ref, bin_ref, ray_ref, sems = rest
    copies = [
        pltpu.make_async_copy(a, b, sems.at[i])
        for i, (a, b) in enumerate(
            (
                (bin_hbm, bin_ref),
                (ray_hbm, ray_ref),
                (den_hbm, den_ref),
                (src_hbm, src_ref),
            )
        )
    ]
    for copy in copies:
        copy.start()
    line_copy = pltpu.make_async_copy(line_hbm, line_out, sems.at[len(copies)])
    even = me_ref[0] % 2 == 0

    @pl.when(jnp.logical_not(even))
    def _():
        line_copy.start()

    cells, levels = src_ref.shape
    lanes = min(cells, LANES)
    earlier = (iota((lanes, lanes), 0) < iota((lanes, lanes), 1)).astype(F32).astype(BF16)
    my_half = me_ref[0] // (targets * plan.wave)
    for copy in copies[:3]:
        copy.wait()

    @pl.when(even)
    def _():
        line_copy.start()

    bins = bin_ref[...]
    hot = (iota((plan.bins, cells), 0) == bins).astype(F32)
    parts = [hot[:, i : i + lanes] for i in range(0, cells, lanes)]
    ranks = jnp.dot(
        jnp.concatenate(parts, axis=0).astype(BF16), earlier, preferred_element_type=F32
    )
    sofar = jnp.zeros((plan.bins, 1), F32)
    places = []
    for i, part in enumerate(parts):
        rank = ranks[i * plan.bins : (i + 1) * plan.bins] + sofar
        places.append(jnp.sum(part * rank, axis=0, keepdims=True))
        sofar = sofar + jnp.sum(part, axis=1, keepdims=True)
    position = jnp.concatenate(places, axis=1).astype(I32)
    half = bins // targets
    target = bins - half * targets
    within = (half ^ my_half) * plan.capacity + position
    rays = ray_ref[...]
    ray_high = rays // RAY_BASE
    ray_low = rays - ray_high * RAY_BASE
    den = den_ref[...].astype(F32)
    den_row = jnp.concatenate([den[i : i + 1] for i in range(den.shape[0])], axis=1)
    meta = jnp.concatenate(
        [den_row, ray_high.astype(F32), ray_low.astype(F32), jnp.zeros((META_ROWS - 3, cells), F32)],
        axis=0,
    ).astype(BF16)
    base = (iota((block, cells), 0) == within).astype(F32).astype(BF16)
    masks = [(target == t).astype(F32).astype(BF16) for t in range(targets)]
    place = jnp.concatenate([base * mask for mask in masks], axis=0)
    moved = nt_dot(jnp.concatenate([meta * mask for mask in masks], axis=0), base).astype(BF16)
    copies[3].wait()
    rows = jnp.dot(place, src_ref[...], preferred_element_type=F32).astype(BF16)
    out[:, :block, :] = rows.reshape(targets, block, levels)
    out[:, block:, :] = jnp.zeros((targets, META_ROWS, levels), BF16)
    for t in range(targets):
        out[t, block:, :block] = moved[t * META_ROWS : (t + 1) * META_ROWS]
    line_copy.wait()


def window_kernel(arrived_ref, table_hbm, powers_ref, sem):
    levels = arrived_ref.shape[0]
    copy = pltpu.make_async_copy(table_hbm, powers_ref.at[0, :, pl.ds(0, levels)], sem)
    copy.start()
    powers_ref[1, :, :levels] = arrived_ref[...]
    copy.wait()
    for part in range(2):
        table = powers_ref[part, :, :levels]
        square = jnp.dot(table, table, preferred_element_type=F32)
        powers_ref[part, :, levels:] = square.astype(BF16)


def level_kernel(plan, rays, got_ref, powers_ref, out_ref):
    targets, block = plan.targets, plan.block
    meta = [got_ref[s, block:, :block].astype(F32) for s in range(targets)]
    columns = [jnp.transpose(m[:8]) for m in meta]
    total = jnp.zeros(out_ref.shape, F32)
    levels = got_ref.shape[2]
    for part in range(2):
        low, high = part * plan.capacity, (part + 1) * plan.capacity
        src = got_ref[:, low:high, :].reshape(targets * plan.capacity, got_ref.shape[2])
        den = jnp.concatenate([c[low:high, 0:1] for c in columns], axis=0)
        ray = jnp.concatenate(
            [m[1:2, low:high] * RAY_BASE + m[2:3, low:high] for m in meta], axis=1
        ).astype(I32)
        wide = src.astype(F32)
        steps = jnp.dot(src, powers_ref[part], preferred_element_type=F32)
        pops = (wide + den * (steps[:, :levels] + den * steps[:, levels:])).astype(BF16)
        pick = (iota((rays, src.shape[0]), 0) == ray).astype(F32).astype(BF16)
        total = total + jnp.dot(pick, pops, preferred_element_type=F32)
    out_ref[...] = total.astype(BF16)


def line_kernel(mine_ref, theirs_ref, line_ref, out_hbm, out_ref, sems):
    sums = mine_ref[...] + theirs_ref[...]
    rows = sums.shape[0]
    high = sums.astype(BF16)
    low = (sums - high.astype(F32)).astype(BF16)
    both = jnp.concatenate([high, low], axis=0)
    chunks = sems.shape[0]
    width = out_ref.shape[1] // chunks
    copies = []
    for i in range(chunks):
        part = pl.ds(i * width, width)
        got = jnp.dot(both, line_ref[:, part], preferred_element_type=F32)
        out_ref[:, part] = got[:rows] + got[rows:]
        copies.append(pltpu.make_async_copy(out_ref.at[:, part], out_hbm.at[:, part], sems.at[i]))
        copies[-1].start()
    for copy in copies:
        copy.wait()


class Plan:
    def __init__(self, bin_total, wave_total, cells):
        self.bins = bin_total
        self.wave = wave_total
        self.targets = bin_total // 2
        self.capacity = max(2, 2 * cells // bin_total)
        self.block = 2 * self.capacity

    def table_moves(self):
        return [(i, (i + self.targets) % self.bins) for i in range(self.bins)]

    def halves(self):
        return [list(range(self.targets)), list(range(self.targets, self.bins))]


def per_device(sources, density, temp_bins, ray_index, rate_tables, line_table):
    cells, levels = sources.shape
    bin_total = lax.axis_size("bin")
    wave_total = lax.axis_size("wave")
    plan = Plan(bin_total, wave_total, cells)
    rows = plan.block + META_ROWS
    params = pltpu.CompilerParams(vmem_limit_bytes=VMEM_LIMIT)
    vmem = pl.BlockSpec(memory_space=pltpu.VMEM)
    smem = pl.BlockSpec(memory_space=pltpu.SMEM)
    hbm = pl.BlockSpec(memory_space=pltpu.HBM)

    def in_hbm(x):
        return pltpu.with_memory_space_constraint(x, pltpu.HBM)

    arrived = lax.ppermute(rate_tables[0], "bin", plan.table_moves())
    me = lax.axis_index(("bin", "wave")).astype(I32).reshape(1)
    den_rows = cells // min(cells, LANES)
    outgoing, held_line = pl.pallas_call(
        functools.partial(pack_kernel, plan),
        out_shape=[
            jax.ShapeDtypeStruct(a, BF16) for a in ((plan.targets, rows, levels), line_table.shape)
        ],
        in_specs=[smem] + [hbm] * 5,
        out_specs=[vmem] * 2,
        scratch_shapes=[
            pltpu.VMEM((cells, levels), BF16),
            pltpu.VMEM((den_rows, cells // den_rows), BF16),
            pltpu.VMEM((1, cells), I32),
            pltpu.VMEM((1, cells), I32),
            pltpu.SemaphoreType.DMA((5,)),
        ],
        compiler_params=params,
    )(
        me,
        in_hbm(sources),
        in_hbm(density.reshape(den_rows, cells // den_rows)),
        in_hbm(temp_bins.reshape(1, cells)),
        in_hbm(ray_index.reshape(1, cells)),
        in_hbm(line_table),
    )
    got = lax.all_to_all(
        outgoing, "bin", split_axis=0, concat_axis=0, tiled=True, axis_index_groups=plan.halves()
    )
    powers = pl.pallas_call(
        window_kernel,
        out_shape=jax.ShapeDtypeStruct((2, levels, 2 * levels), BF16),
        in_specs=[vmem, hbm],
        out_specs=vmem,
        scratch_shapes=[pltpu.SemaphoreType.DMA],
        compiler_params=params,
        cost_estimate=pl.CostEstimate(
            flops=OVERLAP_FLOPS, bytes_accessed=4 * arrived.size, transcendentals=0
        ),
    )(arrived, in_hbm(rate_tables[0]))
    ray_rows = RAY_DEV
    rays = ray_rows * bin_total
    partial_sums = pl.pallas_call(
        functools.partial(level_kernel, plan, rays),
        out_shape=jax.ShapeDtypeStruct((rays, levels), BF16),
        in_specs=[vmem] * 2,
        out_specs=vmem,
        compiler_params=params,
    )(got, powers)
    held = lax.all_to_all(
        partial_sums.reshape(bin_total, ray_rows, levels),
        "bin",
        split_axis=0,
        concat_axis=0,
        tiled=True,
    )
    total = jnp.sum(held.astype(F32), axis=0)
    theirs = jnp.zeros_like(total)
    step = 1
    while step < wave_total:
        total = total + theirs if step > 1 else total
        theirs = lax.ppermute(total, "wave", [(i, i ^ step) for i in range(wave_total)])
        step *= 2
    out_shape = (ray_rows, line_table.shape[1])
    return pl.pallas_call(
        line_kernel,
        out_shape=jax.ShapeDtypeStruct(out_shape, F32),
        in_specs=[vmem, vmem, vmem],
        out_specs=hbm,
        scratch_shapes=[pltpu.VMEM(out_shape, F32), pltpu.SemaphoreType.DMA((LINE_CHUNKS,))],
        compiler_params=params,
    )(total, theirs, held_line)


def solution(mesh):
    in_specs = (
        P(("bin", "wave"), None),
        P(("bin", "wave")),
        P(("bin", "wave"), None),
        P(("bin", "wave")),
        P("bin", None, None),
        P(None, "wave"),
    )
    return jax.shard_map(
        per_device, mesh=mesh, in_specs=in_specs, out_specs=P("bin", "wave"), check_vma=False
    )
```

```python
import functools

import jax
import jax.numpy as jnp
from jax import lax
from jax.experimental import pallas as pl
from jax.experimental.pallas import tpu as pltpu
from jax.sharding import PartitionSpec as P

RAY_DEV = 16
META_ROWS = 8
RAY_BASE = 32
LANES = 128
LINE_CHUNKS = 4
OVERLAP_FLOPS = 10**10
VMEM_LIMIT = 32 * 1024 * 1024
F32 = jnp.float32
BF16 = jnp.bfloat16
I32 = jnp.int32


def nt_dot(a, b):
    return lax.dot_general(a, b, (((1,), (1,)), ((), ())), preferred_element_type=F32)


def iota(shape, dim):
    return lax.broadcasted_iota(I32, shape, dim)


def pack_kernel(plan, me_ref, src_hbm, den_hbm, bin_hbm, ray_hbm, *rest):
    targets, block = plan.targets, plan.block
    out, src_ref, den_ref, bin_ref, ray_ref, sems = rest
    copies = [
        pltpu.make_async_copy(a, b, sems.at[i])
        for i, (a, b) in enumerate(
            (
                (bin_hbm, bin_ref),
                (ray_hbm, ray_ref),
                (den_hbm, den_ref),
                (src_hbm, src_ref),
            )
        )
    ]
    for copy in copies:
        copy.start()
    cells, levels = src_ref.shape
    lanes = min(cells, LANES)
    earlier = (iota((lanes, lanes), 0) < iota((lanes, lanes), 1)).astype(F32).astype(BF16)
    my_half = me_ref[0] // targets
    for copy in copies[:3]:
        copy.wait()
    bins = bin_ref[...]
    hot = (iota((plan.bins, cells), 0) == bins).astype(F32)
    parts = [hot[:, i : i + lanes] for i in range(0, cells, lanes)]
    ranks = jnp.dot(
        jnp.concatenate(parts, axis=0).astype(BF16), earlier, preferred_element_type=F32
    )
    sofar = jnp.zeros((plan.bins, 1), F32)
    places = []
    for i, part in enumerate(parts):
        rank = ranks[i * plan.bins : (i + 1) * plan.bins] + sofar
        places.append(jnp.sum(part * rank, axis=0, keepdims=True))
        sofar = sofar + jnp.sum(part, axis=1, keepdims=True)
    position = jnp.concatenate(places, axis=1).astype(I32)
    half = bins // targets
    target = bins - half * targets
    within = (half ^ my_half) * plan.capacity + position
    rays = ray_ref[...]
    ray_high = rays // RAY_BASE
    ray_low = rays - ray_high * RAY_BASE
    den = den_ref[...].astype(F32)
    den_row = jnp.concatenate([den[i : i + 1] for i in range(den.shape[0])], axis=1)
    meta = jnp.concatenate(
        [den_row, ray_high.astype(F32), ray_low.astype(F32), jnp.zeros((META_ROWS - 3, cells), F32)],
        axis=0,
    ).astype(BF16)
    base = (iota((block, cells), 0) == within).astype(F32).astype(BF16)
    masks = [(target == t).astype(F32).astype(BF16) for t in range(targets)]
    place = jnp.concatenate([base * mask for mask in masks], axis=0)
    moved = nt_dot(jnp.concatenate([meta * mask for mask in masks], axis=0), base).astype(BF16)
    copies[3].wait()
    rows = jnp.dot(place, src_ref[...], preferred_element_type=F32).astype(BF16)
    out[:, :block, :] = rows.reshape(targets, block, levels)
    out[:, block:, :] = jnp.zeros((targets, META_ROWS, levels), BF16)
    for t in range(targets):
        out[t, block:, :block] = moved[t * META_ROWS : (t + 1) * META_ROWS]


def window_kernel(arrived_ref, table_hbm, line_hbm, own_ref, other_ref, line_ref, sems):
    levels = arrived_ref.shape[0]
    copies = [
        pltpu.make_async_copy(table_hbm, own_ref.at[:, pl.ds(0, levels)], sems.at[0]),
        pltpu.make_async_copy(line_hbm, line_ref, sems.at[1]),
    ]
    for copy in copies:
        copy.start()
    other_ref[:, :levels] = arrived_ref[...]
    copies[0].wait()
    for ref in (own_ref, other_ref):
        table = ref[:, :levels]
        square = jnp.dot(table, table, preferred_element_type=F32)
        ref[:, levels:] = square.astype(BF16)
    copies[1].wait()


def level_kernel(plan, rays, core_ref, got_ref, own_ref, other_ref, passed_ref, out_ref):
    other = jnp.where(core_ref[0] % 2 == 1, passed_ref[...], other_ref[...])
    targets, block = plan.targets, plan.block
    meta = [got_ref[s, block:, :block].astype(F32) for s in range(targets)]
    columns = [jnp.transpose(m[:8]) for m in meta]
    total = jnp.zeros(out_ref.shape, F32)
    levels = got_ref.shape[2]
    for part, powers in enumerate((own_ref[...], other)):
        low, high = part * plan.capacity, (part + 1) * plan.capacity
        src = got_ref[:, low:high, :].reshape(targets * plan.capacity, got_ref.shape[2])
        den = jnp.concatenate([c[low:high, 0:1] for c in columns], axis=0)
        ray = jnp.concatenate(
            [m[1:2, low:high] * RAY_BASE + m[2:3, low:high] for m in meta], axis=1
        ).astype(I32)
        wide = src.astype(F32)
        steps = jnp.dot(src, powers, preferred_element_type=F32)
        pops = (wide + den * (steps[:, :levels] + den * steps[:, levels:])).astype(BF16)
        pick = (iota((rays, src.shape[0]), 0) == ray).astype(F32).astype(BF16)
        total = total + jnp.dot(pick, pops, preferred_element_type=F32)
    out_ref[...] = total.astype(BF16)


def line_kernel(mine_ref, theirs_ref, line_ref, out_hbm, out_ref, sems):
    sums = mine_ref[...] + theirs_ref[...]
    rows = sums.shape[0]
    high = sums.astype(BF16)
    low = (sums - high.astype(F32)).astype(BF16)
    both = jnp.concatenate([high, low], axis=0)
    chunks = sems.shape[0]
    width = out_ref.shape[1] // chunks
    copies = []
    for i in range(chunks):
        part = pl.ds(i * width, width)
        got = jnp.dot(both, line_ref[:, part], preferred_element_type=F32)
        out_ref[:, part] = got[:rows] + got[rows:]
        copies.append(pltpu.make_async_copy(out_ref.at[:, part], out_hbm.at[:, part], sems.at[i]))
        copies[-1].start()
    for copy in copies:
        copy.wait()


class Plan:
    def __init__(self, bin_total, cells):
        self.bins = bin_total
        self.targets = bin_total // 2
        self.capacity = max(2, 2 * cells // bin_total)
        self.block = 2 * self.capacity

    def table_moves(self, wave_total):
        moves = []
        for b in range(self.bins):
            for w in range(wave_total):
                to = b ^ 1 if w % 2 else (b + self.targets) % self.bins
                moves.append((b * wave_total + w, to * wave_total + w))
        return moves

    def halves(self):
        return [list(range(self.targets)), list(range(self.targets, self.bins))]


def per_device(sources, density, temp_bins, ray_index, rate_tables, line_table):
    cells, levels = sources.shape
    bin_total = lax.axis_size("bin")
    wave_total = lax.axis_size("wave")
    plan = Plan(bin_total, cells)
    rows = plan.block + META_ROWS
    params = pltpu.CompilerParams(vmem_limit_bytes=VMEM_LIMIT)
    vmem = pl.BlockSpec(memory_space=pltpu.VMEM)
    smem = pl.BlockSpec(memory_space=pltpu.SMEM)
    hbm = pl.BlockSpec(memory_space=pltpu.HBM)

    def in_hbm(x):
        return pltpu.with_memory_space_constraint(x, pltpu.HBM)

    arrived = lax.ppermute(rate_tables[0], ("bin", "wave"), plan.table_moves(wave_total))
    core = lax.axis_index("wave").astype(I32).reshape(1)
    me = lax.axis_index("bin").astype(I32).reshape(1)
    den_rows = cells // min(cells, LANES)
    outgoing = pl.pallas_call(
        functools.partial(pack_kernel, plan),
        out_shape=jax.ShapeDtypeStruct((plan.targets, rows, levels), BF16),
        in_specs=[smem] + [hbm] * 4,
        out_specs=vmem,
        scratch_shapes=[
            pltpu.VMEM((cells, levels), BF16),
            pltpu.VMEM((den_rows, cells // den_rows), BF16),
            pltpu.VMEM((1, cells), I32),
            pltpu.VMEM((1, cells), I32),
            pltpu.SemaphoreType.DMA((4,)),
        ],
        compiler_params=params,
    )(
        me,
        in_hbm(sources),
        in_hbm(density.reshape(den_rows, cells // den_rows)),
        in_hbm(temp_bins.reshape(1, cells)),
        in_hbm(ray_index.reshape(1, cells)),
    )
    got = lax.all_to_all(
        outgoing, "bin", split_axis=0, concat_axis=0, tiled=True, axis_index_groups=plan.halves()
    )
    own, other, held_line = pl.pallas_call(
        window_kernel,
        out_shape=[
            jax.ShapeDtypeStruct(a, BF16)
            for a in ((levels, 2 * levels), (levels, 2 * levels), line_table.shape)
        ],
        in_specs=[vmem, hbm, hbm],
        out_specs=[vmem] * 3,
        scratch_shapes=[pltpu.SemaphoreType.DMA((2,))],
        compiler_params=params,
        cost_estimate=pl.CostEstimate(
            flops=OVERLAP_FLOPS, bytes_accessed=4 * arrived.size, transcendentals=0
        ),
    )(arrived, in_hbm(rate_tables[0]), in_hbm(line_table))
    passed = lax.ppermute(other, "wave", [(i, i ^ 1) for i in range(wave_total)])
    ray_rows = RAY_DEV
    rays = ray_rows * bin_total
    partial_sums = pl.pallas_call(
        functools.partial(level_kernel, plan, rays),
        out_shape=jax.ShapeDtypeStruct((rays, levels), BF16),
        in_specs=[smem] + [vmem] * 4,
        out_specs=vmem,
        compiler_params=params,
    )(core, got, own, other, passed)
    held = lax.all_to_all(
        partial_sums.reshape(bin_total, ray_rows, levels),
        "bin",
        split_axis=0,
        concat_axis=0,
        tiled=True,
    )
    total = jnp.sum(held.astype(F32), axis=0)
    theirs = jnp.zeros_like(total)
    step = 1
    while step < wave_total:
        total = total + theirs if step > 1 else total
        theirs = lax.ppermute(total, "wave", [(i, i ^ step) for i in range(wave_total)])
        step *= 2
    out_shape = (ray_rows, line_table.shape[1])
    return pl.pallas_call(
        line_kernel,
        out_shape=jax.ShapeDtypeStruct(out_shape, F32),
        in_specs=[vmem, vmem, vmem],
        out_specs=hbm,
        scratch_shapes=[pltpu.VMEM(out_shape, F32), pltpu.SemaphoreType.DMA((LINE_CHUNKS,))],
        compiler_params=params,
    )(total, theirs, held_line)


def solution(mesh):
    in_specs = (
        P(("bin", "wave"), None),
        P(("bin", "wave")),
        P(("bin", "wave"), None),
        P(("bin", "wave")),
        P("bin", None, None),
        P(None, "wave"),
    )
    return jax.shard_map(
        per_device, mesh=mesh, in_specs=in_specs, out_specs=P("bin", "wave"), check_vma=False
    )
```

```python
import functools

import jax
import jax.numpy as jnp
from jax import lax
from jax.experimental import pallas as pl
from jax.experimental.pallas import tpu as pltpu
from jax.sharding import PartitionSpec as P

RAY_DEV = 16
META_ROWS = 8
RAY_BASE = 32
LANES = 128
LINE_CHUNKS = 4
OVERLAP_FLOPS = 10**10
VMEM_LIMIT = 32 * 1024 * 1024
F32 = jnp.float32
BF16 = jnp.bfloat16
I32 = jnp.int32


def nt_dot(a, b):
    return lax.dot_general(a, b, (((1,), (1,)), ((), ())), preferred_element_type=F32)


def iota(shape, dim):
    return lax.broadcasted_iota(I32, shape, dim)


def pack_kernel(plan, me_ref, src_hbm, den_hbm, bin_hbm, ray_hbm, *rest):
    targets, block = plan.targets, plan.block
    out, src_ref, den_ref, bin_ref, ray_ref, sems = rest
    copies = [
        pltpu.make_async_copy(a, b, sems.at[i])
        for i, (a, b) in enumerate(
            (
                (bin_hbm, bin_ref),
                (ray_hbm, ray_ref),
                (den_hbm, den_ref),
                (src_hbm, src_ref),
            )
        )
    ]
    for copy in copies:
        copy.start()
    cells, levels = src_ref.shape
    lanes = min(cells, LANES)
    earlier = (iota((lanes, lanes), 0) < iota((lanes, lanes), 1)).astype(F32).astype(BF16)
    my_half = me_ref[0] // targets
    for copy in copies[:3]:
        copy.wait()
    bins = bin_ref[...]
    hot = (iota((plan.bins, cells), 0) == bins).astype(F32)
    parts = [hot[:, i : i + lanes] for i in range(0, cells, lanes)]
    ranks = jnp.dot(
        jnp.concatenate(parts, axis=0).astype(BF16), earlier, preferred_element_type=F32
    )
    sofar = jnp.zeros((plan.bins, 1), F32)
    places = []
    for i, part in enumerate(parts):
        rank = ranks[i * plan.bins : (i + 1) * plan.bins] + sofar
        places.append(jnp.sum(part * rank, axis=0, keepdims=True))
        sofar = sofar + jnp.sum(part, axis=1, keepdims=True)
    position = jnp.concatenate(places, axis=1).astype(I32)
    half = bins // targets
    target = bins - half * targets
    within = (half ^ my_half) * plan.capacity + position
    rays = ray_ref[...]
    ray_high = rays // RAY_BASE
    ray_low = rays - ray_high * RAY_BASE
    den = den_ref[...].astype(F32)
    den_row = jnp.concatenate([den[i : i + 1] for i in range(den.shape[0])], axis=1)
    meta = jnp.concatenate(
        [den_row, ray_high.astype(F32), ray_low.astype(F32), jnp.zeros((META_ROWS - 3, cells), F32)],
        axis=0,
    ).astype(BF16)
    base = (iota((block, cells), 0) == within).astype(F32).astype(BF16)
    masks = [(target == t).astype(F32).astype(BF16) for t in range(targets)]
    place = jnp.concatenate([base * mask for mask in masks], axis=0)
    moved = nt_dot(jnp.concatenate([meta * mask for mask in masks], axis=0), base).astype(BF16)
    copies[3].wait()
    rows = jnp.dot(place, src_ref[...], preferred_element_type=F32).astype(BF16)
    out[:, :block, :] = rows.reshape(targets, block, levels)
    out[:, block:, :] = jnp.zeros((targets, META_ROWS, levels), BF16)
    for t in range(targets):
        out[t, block:, :block] = moved[t * META_ROWS : (t + 1) * META_ROWS]


def window_kernel(arrived_ref, table_hbm, line_hbm, own_ref, other_ref, line_ref, sems):
    levels = arrived_ref.shape[0]
    copies = [
        pltpu.make_async_copy(table_hbm, own_ref.at[:, pl.ds(0, levels)], sems.at[0]),
        pltpu.make_async_copy(line_hbm, line_ref, sems.at[1]),
    ]
    for copy in copies:
        copy.start()
    other_ref[:, :levels] = arrived_ref[...]
    copies[0].wait()
    for ref in (own_ref, other_ref):
        table = ref[:, :levels]
        square = jnp.dot(table, table, preferred_element_type=F32)
        ref[:, levels:] = square.astype(BF16)
    copies[1].wait()


def level_kernel(plan, rays, core_ref, got_ref, own_ref, other_ref, passed_ref, out_ref):
    other = jnp.where(core_ref[0] % 2 == 1, passed_ref[...], other_ref[...])
    targets, block = plan.targets, plan.block
    meta = [got_ref[s, block:, :block].astype(F32) for s in range(targets)]
    columns = [jnp.transpose(m[:8]) for m in meta]
    total = jnp.zeros(out_ref.shape, F32)
    levels = got_ref.shape[2]
    for part, powers in enumerate((own_ref[...], other)):
        low, high = part * plan.capacity, (part + 1) * plan.capacity
        src = got_ref[:, low:high, :].reshape(targets * plan.capacity, got_ref.shape[2])
        den = jnp.concatenate([c[low:high, 0:1] for c in columns], axis=0)
        ray = jnp.concatenate(
            [m[1:2, low:high] * RAY_BASE + m[2:3, low:high] for m in meta], axis=1
        ).astype(I32)
        wide = src.astype(F32)
        steps = jnp.dot(src, powers, preferred_element_type=F32)
        pops = (wide + den * (steps[:, :levels] + den * steps[:, levels:])).astype(BF16)
        pick = (iota((rays, src.shape[0]), 0) == ray).astype(F32).astype(BF16)
        total = total + jnp.dot(pick, pops, preferred_element_type=F32)
    out_ref[...] = total.astype(BF16)


def line_kernel(mine_ref, theirs_ref, line_ref, out_hbm, out_ref, sems):
    sums = mine_ref[...] + theirs_ref[...]
    rows = sums.shape[0]
    high = sums.astype(BF16)
    low = (sums - high.astype(F32)).astype(BF16)
    both = jnp.concatenate([high, low], axis=0)
    chunks = sems.shape[0]
    width = out_ref.shape[1] // chunks
    copies = []
    for i in range(chunks):
        part = pl.ds(i * width, width)
        got = jnp.dot(both, line_ref[:, part], preferred_element_type=F32)
        out_ref[:, part] = got[:rows] + got[rows:]
        copies.append(pltpu.make_async_copy(out_ref.at[:, part], out_hbm.at[:, part], sems.at[i]))
        copies[-1].start()
    for copy in copies:
        copy.wait()


class Plan:
    def __init__(self, bin_total, cells):
        self.bins = bin_total
        self.targets = bin_total // 2
        self.capacity = max(2, 2 * cells // bin_total)
        self.block = 2 * self.capacity

    def table_moves(self, wave_total):
        moves = []
        for b in range(self.bins):
            for w in range(wave_total):
                to = b ^ 2 if w % 2 else (b + self.targets) % self.bins
                moves.append((b * wave_total + w, to * wave_total + w))
        return moves

    def halves(self):
        return [list(range(self.targets)), list(range(self.targets, self.bins))]


def per_device(sources, density, temp_bins, ray_index, rate_tables, line_table):
    cells, levels = sources.shape
    bin_total = lax.axis_size("bin")
    wave_total = lax.axis_size("wave")
    plan = Plan(bin_total, cells)
    rows = plan.block + META_ROWS
    params = pltpu.CompilerParams(vmem_limit_bytes=VMEM_LIMIT)
    vmem = pl.BlockSpec(memory_space=pltpu.VMEM)
    smem = pl.BlockSpec(memory_space=pltpu.SMEM)
    hbm = pl.BlockSpec(memory_space=pltpu.HBM)

    def in_hbm(x):
        return pltpu.with_memory_space_constraint(x, pltpu.HBM)

    arrived = lax.ppermute(rate_tables[0], ("bin", "wave"), plan.table_moves(wave_total))
    core = lax.axis_index("wave").astype(I32).reshape(1)
    me = lax.axis_index("bin").astype(I32).reshape(1)
    den_rows = cells // min(cells, LANES)
    outgoing = pl.pallas_call(
        functools.partial(pack_kernel, plan),
        out_shape=jax.ShapeDtypeStruct((plan.targets, rows, levels), BF16),
        in_specs=[smem] + [hbm] * 4,
        out_specs=vmem,
        scratch_shapes=[
            pltpu.VMEM((cells, levels), BF16),
            pltpu.VMEM((den_rows, cells // den_rows), BF16),
            pltpu.VMEM((1, cells), I32),
            pltpu.VMEM((1, cells), I32),
            pltpu.SemaphoreType.DMA((4,)),
        ],
        compiler_params=params,
    )(
        me,
        in_hbm(sources),
        in_hbm(density.reshape(den_rows, cells // den_rows)),
        in_hbm(temp_bins.reshape(1, cells)),
        in_hbm(ray_index.reshape(1, cells)),
    )
    got = lax.all_to_all(
        outgoing, "bin", split_axis=0, concat_axis=0, tiled=True, axis_index_groups=plan.halves()
    )
    own, other, held_line = pl.pallas_call(
        window_kernel,
        out_shape=[
            jax.ShapeDtypeStruct(a, BF16)
            for a in ((levels, 2 * levels), (levels, 2 * levels), line_table.shape)
        ],
        in_specs=[vmem, hbm, hbm],
        out_specs=[vmem] * 3,
        scratch_shapes=[pltpu.SemaphoreType.DMA((2,))],
        compiler_params=params,
        cost_estimate=pl.CostEstimate(
            flops=OVERLAP_FLOPS, bytes_accessed=4 * arrived.size, transcendentals=0
        ),
    )(arrived, in_hbm(rate_tables[0]), in_hbm(line_table))
    passed = lax.ppermute(other, "wave", [(i, i ^ 1) for i in range(wave_total)])
    ray_rows = RAY_DEV
    rays = ray_rows * bin_total
    partial_sums = pl.pallas_call(
        functools.partial(level_kernel, plan, rays),
        out_shape=jax.ShapeDtypeStruct((rays, levels), BF16),
        in_specs=[smem] + [vmem] * 4,
        out_specs=vmem,
        compiler_params=params,
    )(core, got, own, other, passed)
    held = lax.all_to_all(
        partial_sums.reshape(bin_total, ray_rows, levels),
        "bin",
        split_axis=0,
        concat_axis=0,
        tiled=True,
    )
    total = jnp.sum(held.astype(F32), axis=0)
    theirs = jnp.zeros_like(total)
    step = 1
    while step < wave_total:
        total = total + theirs if step > 1 else total
        theirs = lax.ppermute(total, "wave", [(i, i ^ step) for i in range(wave_total)])
        step *= 2
    out_shape = (ray_rows, line_table.shape[1])
    return pl.pallas_call(
        line_kernel,
        out_shape=jax.ShapeDtypeStruct(out_shape, F32),
        in_specs=[vmem, vmem, vmem],
        out_specs=hbm,
        scratch_shapes=[pltpu.VMEM(out_shape, F32), pltpu.SemaphoreType.DMA((LINE_CHUNKS,))],
        compiler_params=params,
    )(total, theirs, held_line)


def solution(mesh):
    in_specs = (
        P(("bin", "wave"), None),
        P(("bin", "wave")),
        P(("bin", "wave"), None),
        P(("bin", "wave")),
        P("bin", None, None),
        P(None, "wave"),
    )
    return jax.shard_map(
        per_device, mesh=mesh, in_specs=in_specs, out_specs=P("bin", "wave"), check_vma=False
    )
```

```python
import functools

import jax
import jax.numpy as jnp
from jax import lax
from jax.experimental import pallas as pl
from jax.experimental.pallas import tpu as pltpu
from jax.sharding import PartitionSpec as P

RAY_DEV = 16
META_ROWS = 8
RAY_BASE = 32
LANES = 128
LINE_CHUNKS = 8
OVERLAP_FLOPS = 10**10
VMEM_LIMIT = 32 * 1024 * 1024
F32 = jnp.float32
BF16 = jnp.bfloat16
I32 = jnp.int32


def nt_dot(a, b):
    return lax.dot_general(a, b, (((1,), (1,)), ((), ())), preferred_element_type=F32)


def iota(shape, dim):
    return lax.broadcasted_iota(I32, shape, dim)


def pack_kernel(plan, me_ref, src_hbm, den_hbm, bin_hbm, ray_hbm, *rest):
    targets, block = plan.targets, plan.block
    out, src_ref, den_ref, bin_ref, ray_ref, sems = rest
    copies = [
        pltpu.make_async_copy(a, b, sems.at[i])
        for i, (a, b) in enumerate(
            (
                (bin_hbm, bin_ref),
                (ray_hbm, ray_ref),
                (den_hbm, den_ref),
                (src_hbm, src_ref),
            )
        )
    ]
    for copy in copies:
        copy.start()
    cells, levels = src_ref.shape
    lanes = min(cells, LANES)
    earlier = (iota((lanes, lanes), 0) < iota((lanes, lanes), 1)).astype(F32).astype(BF16)
    my_half = me_ref[0] // targets
    for copy in copies[:3]:
        copy.wait()
    bins = bin_ref[...]
    hot = (iota((plan.bins, cells), 0) == bins).astype(F32)
    parts = [hot[:, i : i + lanes] for i in range(0, cells, lanes)]
    ranks = jnp.dot(
        jnp.concatenate(parts, axis=0).astype(BF16), earlier, preferred_element_type=F32
    )
    sofar = jnp.zeros((plan.bins, 1), F32)
    places = []
    for i, part in enumerate(parts):
        rank = ranks[i * plan.bins : (i + 1) * plan.bins] + sofar
        places.append(jnp.sum(part * rank, axis=0, keepdims=True))
        sofar = sofar + jnp.sum(part, axis=1, keepdims=True)
    position = jnp.concatenate(places, axis=1).astype(I32)
    half = bins // targets
    target = bins - half * targets
    within = (half ^ my_half) * plan.capacity + position
    rays = ray_ref[...]
    ray_high = rays // RAY_BASE
    ray_low = rays - ray_high * RAY_BASE
    den = den_ref[...].astype(F32)
    den_row = jnp.concatenate([den[i : i + 1] for i in range(den.shape[0])], axis=1)
    meta = jnp.concatenate(
        [den_row, ray_high.astype(F32), ray_low.astype(F32), jnp.zeros((META_ROWS - 3, cells), F32)],
        axis=0,
    ).astype(BF16)
    base = (iota((block, cells), 0) == within).astype(F32).astype(BF16)
    masks = [(target == t).astype(F32).astype(BF16) for t in range(targets)]
    place = jnp.concatenate([base * mask for mask in masks], axis=0)
    moved = nt_dot(jnp.concatenate([meta * mask for mask in masks], axis=0), base).astype(BF16)
    copies[3].wait()
    rows = jnp.dot(place, src_ref[...], preferred_element_type=F32).astype(BF16)
    out[:, :block, :] = rows.reshape(targets, block, levels)
    out[:, block:, :] = jnp.zeros((targets, META_ROWS, levels), BF16)
    for t in range(targets):
        out[t, block:, :block] = moved[t * META_ROWS : (t + 1) * META_ROWS]


def window_kernel(arrived_ref, table_hbm, line_hbm, own_ref, other_ref, line_ref, sems):
    levels = arrived_ref.shape[0]
    copies = [
        pltpu.make_async_copy(table_hbm, own_ref.at[:, pl.ds(0, levels)], sems.at[0]),
        pltpu.make_async_copy(line_hbm, line_ref, sems.at[1]),
    ]
    for copy in copies:
        copy.start()
    other_ref[:, :levels] = arrived_ref[...]
    copies[0].wait()
    for ref in (own_ref, other_ref):
        table = ref[:, :levels]
        square = jnp.dot(table, table, preferred_element_type=F32)
        ref[:, levels:] = square.astype(BF16)
    copies[1].wait()


def level_kernel(plan, rays, core_ref, got_ref, own_ref, other_ref, passed_ref, out_ref):
    other = jnp.where(core_ref[0] % 2 == 1, passed_ref[...], other_ref[...])
    targets, block = plan.targets, plan.block
    meta = [got_ref[s, block:, :block].astype(F32) for s in range(targets)]
    columns = [jnp.transpose(m[:8]) for m in meta]
    total = jnp.zeros(out_ref.shape, F32)
    levels = got_ref.shape[2]
    for part, powers in enumerate((own_ref[...], other)):
        low, high = part * plan.capacity, (part + 1) * plan.capacity
        src = got_ref[:, low:high, :].reshape(targets * plan.capacity, got_ref.shape[2])
        den = jnp.concatenate([c[low:high, 0:1] for c in columns], axis=0)
        ray = jnp.concatenate(
            [m[1:2, low:high] * RAY_BASE + m[2:3, low:high] for m in meta], axis=1
        ).astype(I32)
        wide = src.astype(F32)
        steps = jnp.dot(src, powers, preferred_element_type=F32)
        pops = (wide + den * (steps[:, :levels] + den * steps[:, levels:])).astype(BF16)
        pick = (iota((rays, src.shape[0]), 0) == ray).astype(F32).astype(BF16)
        total = total + jnp.dot(pick, pops, preferred_element_type=F32)
    out_ref[...] = total.astype(BF16)


def line_kernel(mine_ref, theirs_ref, line_ref, out_hbm, out_ref, sems):
    sums = mine_ref[...] + theirs_ref[...]
    rows = sums.shape[0]
    high = sums.astype(BF16)
    low = (sums - high.astype(F32)).astype(BF16)
    both = jnp.concatenate([high, low], axis=0)
    chunks = sems.shape[0]
    width = out_ref.shape[1] // chunks
    copies = []
    for i in range(chunks):
        part = pl.ds(i * width, width)
        got = jnp.dot(both, line_ref[:, part], preferred_element_type=F32)
        out_ref[:, part] = got[:rows] + got[rows:]
        copies.append(pltpu.make_async_copy(out_ref.at[:, part], out_hbm.at[:, part], sems.at[i]))
        copies[-1].start()
    for copy in copies:
        copy.wait()


class Plan:
    def __init__(self, bin_total, cells):
        self.bins = bin_total
        self.targets = bin_total // 2
        self.capacity = max(2, 2 * cells // bin_total)
        self.block = 2 * self.capacity

    def table_moves(self, wave_total):
        moves = []
        for b in range(self.bins):
            for w in range(wave_total):
                to = b ^ 2 if w % 2 else (b + self.targets) % self.bins
                moves.append((b * wave_total + w, to * wave_total + w))
        return moves

    def halves(self):
        return [list(range(self.targets)), list(range(self.targets, self.bins))]


def per_device(sources, density, temp_bins, ray_index, rate_tables, line_table):
    cells, levels = sources.shape
    bin_total = lax.axis_size("bin")
    wave_total = lax.axis_size("wave")
    plan = Plan(bin_total, cells)
    rows = plan.block + META_ROWS
    params = pltpu.CompilerParams(vmem_limit_bytes=VMEM_LIMIT)
    vmem = pl.BlockSpec(memory_space=pltpu.VMEM)
    smem = pl.BlockSpec(memory_space=pltpu.SMEM)
    hbm = pl.BlockSpec(memory_space=pltpu.HBM)

    def in_hbm(x):
        return pltpu.with_memory_space_constraint(x, pltpu.HBM)

    arrived = lax.ppermute(rate_tables[0], ("bin", "wave"), plan.table_moves(wave_total))
    core = lax.axis_index("wave").astype(I32).reshape(1)
    me = lax.axis_index("bin").astype(I32).reshape(1)
    den_rows = cells // min(cells, LANES)
    outgoing = pl.pallas_call(
        functools.partial(pack_kernel, plan),
        out_shape=jax.ShapeDtypeStruct((plan.targets, rows, levels), BF16),
        in_specs=[smem] + [hbm] * 4,
        out_specs=vmem,
        scratch_shapes=[
            pltpu.VMEM((cells, levels), BF16),
            pltpu.VMEM((den_rows, cells // den_rows), BF16),
            pltpu.VMEM((1, cells), I32),
            pltpu.VMEM((1, cells), I32),
            pltpu.SemaphoreType.DMA((4,)),
        ],
        compiler_params=params,
    )(
        me,
        in_hbm(sources),
        in_hbm(density.reshape(den_rows, cells // den_rows)),
        in_hbm(temp_bins.reshape(1, cells)),
        in_hbm(ray_index.reshape(1, cells)),
    )
    got = lax.all_to_all(
        outgoing, "bin", split_axis=0, concat_axis=0, tiled=True, axis_index_groups=plan.halves()
    )
    own, other, held_line = pl.pallas_call(
        window_kernel,
        out_shape=[
            jax.ShapeDtypeStruct(a, BF16)
            for a in ((levels, 2 * levels), (levels, 2 * levels), line_table.shape)
        ],
        in_specs=[vmem, hbm, hbm],
        out_specs=[vmem] * 3,
        scratch_shapes=[pltpu.SemaphoreType.DMA((2,))],
        compiler_params=params,
        cost_estimate=pl.CostEstimate(
            flops=OVERLAP_FLOPS, bytes_accessed=4 * arrived.size, transcendentals=0
        ),
    )(arrived, in_hbm(rate_tables[0]), in_hbm(line_table))
    passed = lax.ppermute(other, "wave", [(i, i ^ 1) for i in range(wave_total)])
    ray_rows = RAY_DEV
    rays = ray_rows * bin_total
    partial_sums = pl.pallas_call(
        functools.partial(level_kernel, plan, rays),
        out_shape=jax.ShapeDtypeStruct((rays, levels), BF16),
        in_specs=[smem] + [vmem] * 4,
        out_specs=vmem,
        compiler_params=params,
    )(core, got, own, other, passed)
    held = lax.all_to_all(
        partial_sums.reshape(bin_total, ray_rows, levels),
        "bin",
        split_axis=0,
        concat_axis=0,
        tiled=True,
    )
    total = jnp.sum(held.astype(F32), axis=0)
    theirs = jnp.zeros_like(total)
    step = 1
    while step < wave_total:
        total = total + theirs if step > 1 else total
        theirs = lax.ppermute(total, "wave", [(i, i ^ step) for i in range(wave_total)])
        step *= 2
    out_shape = (ray_rows, line_table.shape[1])
    return pl.pallas_call(
        line_kernel,
        out_shape=jax.ShapeDtypeStruct(out_shape, F32),
        in_specs=[vmem, vmem, vmem],
        out_specs=hbm,
        scratch_shapes=[pltpu.VMEM(out_shape, F32), pltpu.SemaphoreType.DMA((LINE_CHUNKS,))],
        compiler_params=params,
    )(total, theirs, held_line)


def solution(mesh):
    in_specs = (
        P(("bin", "wave"), None),
        P(("bin", "wave")),
        P(("bin", "wave"), None),
        P(("bin", "wave")),
        P("bin", None, None),
        P(None, "wave"),
    )
    return jax.shard_map(
        per_device, mesh=mesh, in_specs=in_specs, out_specs=P("bin", "wave"), check_vma=False
    )
```

```python
import functools

import jax
import jax.numpy as jnp
from jax import lax
from jax.experimental import pallas as pl
from jax.experimental.pallas import tpu as pltpu
from jax.sharding import PartitionSpec as P

RAY_DEV = 16
META_ROWS = 8
RAY_BASE = 32
LANES = 128
LINE_CHUNKS = 4
OVERLAP_FLOPS = 10**10
VMEM_LIMIT = 32 * 1024 * 1024
F32 = jnp.float32
BF16 = jnp.bfloat16
I32 = jnp.int32


def nt_dot(a, b):
    return lax.dot_general(a, b, (((1,), (1,)), ((), ())), preferred_element_type=F32)


def iota(shape, dim):
    return lax.broadcasted_iota(I32, shape, dim)


def pack_kernel(plan, me_ref, src_hbm, den_hbm, bin_hbm, ray_hbm, *rest):
    targets, block = plan.targets, plan.block
    out, src_ref, den_ref, bin_ref, ray_ref, sems = rest
    copies = [
        pltpu.make_async_copy(a, b, sems.at[i])
        for i, (a, b) in enumerate(
            (
                (bin_hbm, bin_ref),
                (ray_hbm, ray_ref),
                (den_hbm, den_ref),
                (src_hbm, src_ref),
            )
        )
    ]
    for copy in copies:
        copy.start()
    cells, levels = src_ref.shape
    lanes = min(cells, LANES)
    earlier = (iota((lanes, lanes), 0) < iota((lanes, lanes), 1)).astype(F32).astype(BF16)
    my_half = me_ref[0] // targets
    for copy in copies[:3]:
        copy.wait()
    bins = bin_ref[...]
    hot = (iota((plan.bins, cells), 0) == bins).astype(F32)
    parts = [hot[:, i : i + lanes] for i in range(0, cells, lanes)]
    ranks = jnp.dot(
        jnp.concatenate(parts, axis=0).astype(BF16), earlier, preferred_element_type=F32
    )
    sofar = jnp.zeros((plan.bins, 1), F32)
    places = []
    for i, part in enumerate(parts):
        rank = ranks[i * plan.bins : (i + 1) * plan.bins] + sofar
        places.append(jnp.sum(part * rank, axis=0, keepdims=True))
        sofar = sofar + jnp.sum(part, axis=1, keepdims=True)
    position = jnp.concatenate(places, axis=1).astype(I32)
    half = bins // targets
    target = bins - half * targets
    within = (half ^ my_half) * plan.capacity + position
    rays = ray_ref[...]
    ray_high = rays // RAY_BASE
    ray_low = rays - ray_high * RAY_BASE
    den = den_ref[...].astype(F32)
    den_row = jnp.concatenate([den[i : i + 1] for i in range(den.shape[0])], axis=1)
    meta = jnp.concatenate(
        [den_row, ray_high.astype(F32), ray_low.astype(F32), jnp.zeros((META_ROWS - 3, cells), F32)],
        axis=0,
    ).astype(BF16)
    base = (iota((block, cells), 0) == within).astype(F32).astype(BF16)
    masks = [(target == t).astype(F32).astype(BF16) for t in range(targets)]
    place = jnp.concatenate([base * mask for mask in masks], axis=0)
    moved = nt_dot(jnp.concatenate([meta * mask for mask in masks], axis=0), base).astype(BF16)
    copies[3].wait()
    rows = jnp.dot(place, src_ref[...], preferred_element_type=F32).astype(BF16)
    out[:, :block, :] = rows.reshape(targets, block, levels)
    out[:, block:, :] = jnp.zeros((targets, META_ROWS, levels), BF16)
    for t in range(targets):
        out[t, block:, :block] = moved[t * META_ROWS : (t + 1) * META_ROWS]


def window_kernel(arrived_ref, table_hbm, line_hbm, own_ref, other_ref, line_ref, sems):
    levels = arrived_ref.shape[0]
    copies = [
        pltpu.make_async_copy(table_hbm, own_ref.at[:, pl.ds(0, levels)], sems.at[0]),
        pltpu.make_async_copy(line_hbm, line_ref, sems.at[1]),
    ]
    for copy in copies:
        copy.start()
    other_ref[:, :levels] = arrived_ref[...]
    copies[0].wait()
    for ref in (own_ref, other_ref):
        table = ref[:, :levels]
        square = jnp.dot(table, table, preferred_element_type=F32)
        ref[:, levels:] = square.astype(BF16)
    copies[1].wait()


def level_kernel(plan, rays, core_ref, got_ref, own_ref, other_ref, passed_ref, out_ref):
    other = jnp.where(core_ref[0] % 2 == 1, passed_ref[...], other_ref[...])
    targets, block = plan.targets, plan.block
    meta = [got_ref[s, block:, :block].astype(F32) for s in range(targets)]
    columns = [jnp.transpose(m[:8]) for m in meta]
    total = jnp.zeros(out_ref.shape, F32)
    levels = got_ref.shape[2]
    for part, powers in enumerate((own_ref[...], other)):
        low, high = part * plan.capacity, (part + 1) * plan.capacity
        src = got_ref[:, low:high, :].reshape(targets * plan.capacity, got_ref.shape[2])
        den = jnp.concatenate([c[low:high, 0:1] for c in columns], axis=0)
        ray = jnp.concatenate(
            [m[1:2, low:high] * RAY_BASE + m[2:3, low:high] for m in meta], axis=1
        ).astype(I32)
        wide = src.astype(F32)
        steps = jnp.dot(src, powers, preferred_element_type=F32)
        pops = (wide + den * (steps[:, :levels] + den * steps[:, levels:])).astype(BF16)
        pick = (iota((rays, src.shape[0]), 0) == ray).astype(F32).astype(BF16)
        total = total + jnp.dot(pick, pops, preferred_element_type=F32)
    out_ref[...] = total.astype(BF16)


def line_kernel(mine_ref, theirs_ref, line_ref, out_hbm, out_ref, sems):
    sums = mine_ref[...] + theirs_ref[...].astype(F32)
    rows = sums.shape[0]
    high = sums.astype(BF16)
    low = (sums - high.astype(F32)).astype(BF16)
    both = jnp.concatenate([high, low], axis=0)
    chunks = sems.shape[0]
    width = out_ref.shape[1] // chunks
    copies = []
    for i in range(chunks):
        part = pl.ds(i * width, width)
        got = jnp.dot(both, line_ref[:, part], preferred_element_type=F32)
        out_ref[:, part] = got[:rows] + got[rows:]
        copies.append(pltpu.make_async_copy(out_ref.at[:, part], out_hbm.at[:, part], sems.at[i]))
        copies[-1].start()
    for copy in copies:
        copy.wait()


class Plan:
    def __init__(self, bin_total, cells):
        self.bins = bin_total
        self.targets = bin_total // 2
        self.capacity = max(2, 2 * cells // bin_total)
        self.block = 2 * self.capacity

    def table_moves(self, wave_total):
        moves = []
        for b in range(self.bins):
            for w in range(wave_total):
                to = b ^ 2 if w % 2 else (b + self.targets) % self.bins
                moves.append((b * wave_total + w, to * wave_total + w))
        return moves

    def halves(self):
        return [list(range(self.targets)), list(range(self.targets, self.bins))]


def per_device(sources, density, temp_bins, ray_index, rate_tables, line_table):
    cells, levels = sources.shape
    bin_total = lax.axis_size("bin")
    wave_total = lax.axis_size("wave")
    plan = Plan(bin_total, cells)
    rows = plan.block + META_ROWS
    params = pltpu.CompilerParams(vmem_limit_bytes=VMEM_LIMIT)
    vmem = pl.BlockSpec(memory_space=pltpu.VMEM)
    smem = pl.BlockSpec(memory_space=pltpu.SMEM)
    hbm = pl.BlockSpec(memory_space=pltpu.HBM)

    def in_hbm(x):
        return pltpu.with_memory_space_constraint(x, pltpu.HBM)

    arrived = lax.ppermute(rate_tables[0], ("bin", "wave"), plan.table_moves(wave_total))
    core = lax.axis_index("wave").astype(I32).reshape(1)
    me = lax.axis_index("bin").astype(I32).reshape(1)
    den_rows = cells // min(cells, LANES)
    outgoing = pl.pallas_call(
        functools.partial(pack_kernel, plan),
        out_shape=jax.ShapeDtypeStruct((plan.targets, rows, levels), BF16),
        in_specs=[smem] + [hbm] * 4,
        out_specs=vmem,
        scratch_shapes=[
            pltpu.VMEM((cells, levels), BF16),
            pltpu.VMEM((den_rows, cells // den_rows), BF16),
            pltpu.VMEM((1, cells), I32),
            pltpu.VMEM((1, cells), I32),
            pltpu.SemaphoreType.DMA((4,)),
        ],
        compiler_params=params,
    )(
        me,
        in_hbm(sources),
        in_hbm(density.reshape(den_rows, cells // den_rows)),
        in_hbm(temp_bins.reshape(1, cells)),
        in_hbm(ray_index.reshape(1, cells)),
    )
    got = lax.all_to_all(
        outgoing, "bin", split_axis=0, concat_axis=0, tiled=True, axis_index_groups=plan.halves()
    )
    own, other, held_line = pl.pallas_call(
        window_kernel,
        out_shape=[
            jax.ShapeDtypeStruct(a, BF16)
            for a in ((levels, 2 * levels), (levels, 2 * levels), line_table.shape)
        ],
        in_specs=[vmem, hbm, hbm],
        out_specs=[vmem] * 3,
        scratch_shapes=[pltpu.SemaphoreType.DMA((2,))],
        compiler_params=params,
        cost_estimate=pl.CostEstimate(
            flops=OVERLAP_FLOPS, bytes_accessed=4 * arrived.size, transcendentals=0
        ),
    )(arrived, in_hbm(rate_tables[0]), in_hbm(line_table))
    passed = lax.ppermute(other, "wave", [(i, i ^ 1) for i in range(wave_total)])
    ray_rows = RAY_DEV
    rays = ray_rows * bin_total
    partial_sums = pl.pallas_call(
        functools.partial(level_kernel, plan, rays),
        out_shape=jax.ShapeDtypeStruct((rays, levels), BF16),
        in_specs=[smem] + [vmem] * 4,
        out_specs=vmem,
        compiler_params=params,
    )(core, got, own, other, passed)
    held = lax.all_to_all(
        partial_sums.reshape(bin_total, ray_rows, levels),
        "bin",
        split_axis=0,
        concat_axis=0,
        tiled=True,
    )
    total = jnp.sum(held.astype(F32), axis=0)
    theirs = jnp.zeros_like(total)
    step = 1
    while step < wave_total:
        total = total + theirs if step > 1 else total
        theirs = lax.ppermute(total.astype(BF16), "wave", [(i, i ^ step) for i in range(wave_total)])
        step *= 2
    out_shape = (ray_rows, line_table.shape[1])
    return pl.pallas_call(
        line_kernel,
        out_shape=jax.ShapeDtypeStruct(out_shape, F32),
        in_specs=[vmem, vmem, vmem],
        out_specs=hbm,
        scratch_shapes=[pltpu.VMEM(out_shape, F32), pltpu.SemaphoreType.DMA((LINE_CHUNKS,))],
        compiler_params=params,
    )(total, theirs, held_line)


def solution(mesh):
    in_specs = (
        P(("bin", "wave"), None),
        P(("bin", "wave")),
        P(("bin", "wave"), None),
        P(("bin", "wave")),
        P("bin", None, None),
        P(None, "wave"),
    )
    return jax.shard_map(
        per_device, mesh=mesh, in_specs=in_specs, out_specs=P("bin", "wave"), check_vma=False
    )
```
